32 devices in a mesh: dp: 8 (over z, y), seq: 4 (over x, core).
Axes of the slice: x: 2, y: 2, z: 4, core: 2. Of those that a mesh axis runs over, the one named last changes fastest.
Arguments:
- tokens: bfloat16 [32, 576, 768], P('dp', 'seq'), may hold values from -6 to 6
- cotangent: bfloat16 [32, 576, 768], P('dp', 'seq'), may hold values from -6 to 6
- pad_mask: int32 [32, 576], P('dp', 'seq'), may hold values from 0 to 1, as said below
- expert_ids: int32 [32, 576, 2], P('dp', 'seq'), may hold values from 0 to 7, all different within a row
- priority: int32 [32, 576], P('dp', 'seq'), may hold values from 0 to 575, as said below
- ln1_gain: bfloat16 [768], P(('dp', 'seq')), may hold values from 0.5 to 1.5
- ln1_shift: bfloat16 [768], P(('dp', 'seq')), may hold values from -1.25 to 1.25
- w_qkv: bfloat16 [768, 2304], P(('dp', 'seq')), may hold values from -0.3125 to 0.3125
- w_out: bfloat16 [768, 768], P(('dp', 'seq')), may hold values from -0.875 to 0.875
- out_bias: bfloat16 [768], P(('dp', 'seq')), may hold values from -0.625 to 0.625
- ln2_gain: bfloat16 [768], P(('dp', 'seq')), may hold values from 0.5 to 1.5
- ln2_shift: bfloat16 [768], P(('dp', 'seq')), may hold values from -1.25 to 1.25
- w_router: bfloat16 [768, 8], P(('dp', 'seq')), may hold values from -0.15625 to 0.15625
- w_in: bfloat16 [8, 768, 3072], P('dp', None, 'seq'), may hold values from -0.21875 to 0.21875
- in_bias: bfloat16 [8, 3072], P('dp', 'seq'), may hold values from -1.75 to 1.75
- w_exp_out: bfloat16 [8, 3072, 768], P('dp', 'seq'), may hold values from -0.625 to 0.625
- exp_out_bias: bfloat16 [8, 768], P('dp', 'seq'), may hold values from -2.5 to 2.5
Outputs:
- block_output: bfloat16 [32, 576, 768], P('dp', 'seq')
- tokens_grad: bfloat16 [32, 576, 768], P('dp', 'seq')
- ln1_gain_grad: float32 [768], P(('dp', 'seq'))
- ln1_shift_grad: float32 [768], P(('dp', 'seq'))
- w_qkv_grad: float32 [768, 2304], P(('dp', 'seq'))
- w_out_grad: float32 [768, 768], P(('dp', 'seq'))
- out_bias_grad: float32 [768], P(('dp', 'seq'))
- ln2_gain_grad: float32 [768], P(('dp', 'seq'))
- ln2_shift_grad: float32 [768], P(('dp', 'seq'))
- w_router_grad: float32 [768, 8], P(('dp', 'seq'))
- w_in_grad: float32 [8, 768, 3072], P('dp', None, 'seq')
- in_bias_grad: float32 [8, 3072], P('dp', 'seq')
- w_exp_out_grad: float32 [8, 3072, 768], P('dp', 'seq')
- exp_out_bias_grad: float32 [8, 768], P('dp', 'seq')
The draws below stay inside these ranges and needn't reach their ends.
Inputs may be any that keep to these rules, and one draw needn't show every extreme that they name: `pad_mask`: each row is 1 on its first positions and 0 after them; in each aligned group of 4 rows one row is all ones. `priority`: each device's block of 4 rows and 144 positions, read row by row, lists every index r * 144 + p of the block's patches exactly once (r and p the row and position within the block). `expert_ids`: the two ids of a patch differ.
All inputs are finite; a program needn't handle non-finite values.
Results may differ from the reference program's by a relative error of at most 0.017.
Values may be sent and summed in bfloat16 or wider, within the bound.
A program may use at most 192 MiB of HBM per device.

```python
import jax
import jax.numpy as jnp
from jax import lax

D = 768
HEADS = 12
HEAD = 64
FF = 3072
LEN = 576
ROWS_DEV = 4
ROWS = 32
POS_DEV = 144
TOK_DEV = 576
EXPERTS = 8
CAP = 152
N_DP = 8
N_SEQ = 4


def draw_pad_mask(key, part):
    key = jax.random.fold_in(key, 11)
    length_key, pick_key = jax.random.split(key)
    lengths = jax.random.randint(length_key, (ROWS,), LEN - LEN // 3, LEN + 1)
    groups = ROWS // ROWS_DEV
    chosen_rows = jnp.arange(groups) * ROWS_DEV + jax.random.randint(pick_key, (groups,), 0, ROWS_DEV)
    lengths = lengths.at[chosen_rows].set(LEN)
    return (jnp.arange(LEN)[None, :] < lengths[:, None]).astype(jnp.int32)


def draw_priority(key, part):
    key = jax.random.fold_in(key, 23)
    blocks_rows = ROWS // ROWS_DEV
    blocks_seq = LEN // POS_DEV
    block_keys = jax.random.split(key, blocks_rows * blocks_seq)
    orders = jax.vmap(lambda sub_key: jax.random.permutation(sub_key, TOK_DEV))(block_keys)
    orders = orders.reshape(blocks_rows, blocks_seq, ROWS_DEV, POS_DEV)
    return jnp.transpose(orders, (0, 2, 1, 3)).reshape(ROWS, LEN).astype(jnp.int32)


def with_spikes(entries, own_key, source, target, parts, factor):
    owner, partner = [(jnp.arange(entries.shape[axis_at]) // (entries.shape[axis_at] // parts)).reshape([-1 if axis == axis_at else 1 for axis in range(entries.ndim)]) for axis_at in (source, target)]
    chosen = jax.random.permutation(own_key, parts)[partner]
    strong = (owner == chosen) | (owner == (partner + parts // 2) % parts)
    return jnp.where(strong, factor * entries, entries)


def block_scale(rng, shape, cuts, least, largest):
    factor_of, own = 1.0, jax.random.fold_in(rng, 6)
    for axis_at, parts in cuts:
        steps = jnp.exp(jax.random.uniform(jax.random.fold_in(own, axis_at), (parts,), jnp.float32, least / len(cuts), largest / len(cuts)))
        factor_of = factor_of * jnp.repeat(steps, shape[axis_at] // parts).reshape([-1 if axis == axis_at else 1 for axis in range(len(shape))])
    return factor_of


def picks_of(own_key, rows, amount, top, lift):
    ranking = jax.random.permutation(jax.random.fold_in(own_key, 1), amount)
    pull = ranking
    for power in range(3):
        pull = pull * pull // amount
    pull = pull * lift // amount
    chance = jax.random.randint(jax.random.fold_in(own_key, 2), (rows, amount), 0, 4096) + pull
    fixed_rows = jax.random.permutation(jax.random.fold_in(own_key, 3), rows)[jnp.arange(amount) % rows]
    chance = jnp.where(jnp.arange(rows)[:, None] == fixed_rows[None, :], 1 << 14, chance)
    score = chance * amount + jnp.arange(amount)
    return lax.top_k(score.astype(jnp.int32), top)[1].astype(jnp.int32)


def noise(rng, shape, width, limit, shards=(), held_as=jnp.bfloat16):
    drawn = width * jax.random.normal(rng, shape, jnp.float32)
    if shards:
        drawn = drawn * block_scale(rng, shape, shards, -0.22, 0.18)
    return jnp.clip(drawn, -limit, limit).astype(held_as)


def gaussian_with(key, extent, width, bound, cuts, heavy, held_as=jnp.bfloat16):
    entries = width * jax.random.normal(key, extent, jnp.float32)
    if cuts:
        entries = entries * block_scale(key, extent, cuts, -0.22, 0.18)
    return jnp.clip(with_spikes(entries, jax.random.fold_in(key, 3), *heavy), -bound, bound).astype(held_as)


def setup_inputs(seed: int = 0) -> dict:
    seeds = jax.random.split(jax.random.key(seed), 18)
    return {
        "tokens": noise(seeds[0], (ROWS, LEN, D), 1.0, 6.0, ((0, 8), (1, 4))),
        "cotangent": gaussian_with(seeds[1], (ROWS, LEN, D), 1.0, 6.0, ((0, 8), (1, 4)), (0, 2, 8, 2.0)),
        "pad_mask": draw_pad_mask(jax.random.fold_in(seeds[17], 71), 0),
        "expert_ids": picks_of(seeds[3], ROWS * LEN, EXPERTS, 2, 4096).reshape((ROWS, LEN, 2)),
        "priority": draw_priority(jax.random.fold_in(seeds[17], 71), 0),
        "ln1_gain": jnp.clip(1.0 + 0.1 * jax.random.normal(seeds[5], (D,), jnp.float32), 0.5, 1.5).astype(jnp.bfloat16),
        "ln1_shift": noise(seeds[6], (D,), 0.2, 1.25, ((0, 32),)),
        "w_qkv": noise(seeds[7], (D, 3 * D), (D // 2) ** -0.5, 0.3125, ((0, 32),)),
        "w_out": noise(seeds[8], (D, D), (D // 16) ** -0.5, 0.875, ((0, 32),)),
        "out_bias": noise(seeds[9], (D,), 0.1, 0.625, ((0, 32),)),
        "ln2_gain": jnp.clip(1.0 + 0.1 * jax.random.normal(seeds[10], (D,), jnp.float32), 0.5, 1.5).astype(jnp.bfloat16),
        "ln2_shift": noise(seeds[11], (D,), 0.2, 1.25, ((0, 32),)),
        "w_router": noise(seeds[12], (D, EXPERTS), 0.025, 0.15625, ((0, 32),)),
        "w_in": noise(seeds[13], (EXPERTS, D, FF), D ** -0.5, 0.21875, ((0, 8), (2, 4))),
        "in_bias": noise(seeds[14], (EXPERTS, FF), 0.3, 1.75, ((0, 8), (1, 4))),
        "w_exp_out": noise(seeds[15], (EXPERTS, FF, D), (max(1, 2 * FF // (EXPERTS * EXPERTS))) ** -0.5, 0.625, ((0, 8), (1, 4))),
        "exp_out_bias": noise(seeds[16], (EXPERTS, D), (0.05 * EXPERTS), 2.5, ((0, 8), (1, 4))),
    }


@jax.custom_vjp
def low(v):
    return lax.optimization_barrier(v.astype(jnp.bfloat16)).astype(jnp.float32)

@jax.custom_vjp
def low_back(v):
    return v

def low_keep(v):
    return (low(v), None)

def low_pass(kept, grad):
    return (grad,)

def back_keep(v):
    return (v, None)

def back_low(kept, grad):
    return (low(grad),)
low.defvjp(low_keep, low_pass)
low_back.defvjp(back_keep, back_low)
best_precision = lax.Precision.HIGHEST

def layer_norm(values, norm_gain, norm_shift):
    average = lax.optimization_barrier(jnp.mean(values, axis=-1, keepdims=True))
    centred = values - average
    variance = lax.optimization_barrier(jnp.mean(centred * centred, axis=-1, keepdims=True))
    return centred * lax.rsqrt(variance + 1e-06) * norm_gain + norm_shift

def to_blocks(array):
    tail_shape = array.shape[2:]
    blocked = array.reshape((N_DP, ROWS_DEV, N_SEQ, POS_DEV) + tail_shape)
    blocked = jnp.swapaxes(blocked, 1, 2)
    return blocked.reshape((N_DP * N_SEQ * TOK_DEV,) + tail_shape)

def from_blocks(array):
    tail_shape = array.shape[1:]
    blocked = array.reshape((N_DP, N_SEQ, ROWS_DEV, POS_DEV) + tail_shape)
    blocked = jnp.swapaxes(blocked, 1, 2)
    return blocked.reshape((ROWS, LEN) + tail_shape)

def pair_slots(order, expert_picks, valid_flags):
    pair_half = order.shape[0]
    token_pairs = jnp.concatenate([order, order]).astype(jnp.int32)
    which_pick = jnp.concatenate([jnp.zeros((pair_half,), jnp.int32), jnp.ones((pair_half,), jnp.int32)])
    expert_pairs = expert_picks[token_pairs, which_pick]
    valid_pairs = valid_flags[token_pairs]
    matches = (expert_pairs[:, None] == jnp.arange(EXPERTS, dtype=jnp.int32)[None, :]).astype(jnp.int32)
    counted = matches * valid_pairs[:, None]
    earlier = jnp.cumsum(counted, axis=0) - counted
    slot_index = lax.optimization_barrier(jnp.sum(earlier * matches, axis=1))
    kept_flags = valid_pairs * (slot_index < CAP).astype(jnp.int32)
    return (token_pairs, expert_pairs, slot_index, kept_flags)

def attend_row(inputs):
    query_row, key_row, value_row, open_row = inputs
    scores = low_back(jnp.einsum('qhd,khd->hqk', query_row, key_row, precision=best_precision) * HEAD ** (-0.5))
    scores = jnp.where(open_row[None, None, :] > 0, scores, -1e+30)
    weights = low(jax.nn.softmax(scores, axis=-1))
    return jnp.einsum('hqk,khd->qhd', weights, value_row, precision=best_precision).reshape(LEN, D)

def expert_apply(inputs):
    rows_in, weight_in, bias_in, weight_out, bias_out = inputs
    pre_act = low_back(jnp.dot(rows_in, weight_in, precision=best_precision) + bias_in)
    activated = low(jax.nn.gelu(pre_act, approximate=False))
    return low(low_back(jnp.dot(activated, weight_out, precision=best_precision) + bias_out))

def reference(tokens, cotangent, pad_mask, expert_ids, priority, ln1_gain, ln1_shift, w_qkv, w_out, out_bias, ln2_gain, ln2_shift, w_router, w_in, in_bias, w_exp_out, exp_out_bias):
    block_count = N_DP * N_SEQ
    order_blocks = to_blocks(priority).reshape(block_count, TOK_DEV)
    pick_blocks = to_blocks(expert_ids).reshape(block_count, TOK_DEV, 2)
    open_blocks = to_blocks(pad_mask).reshape(block_count, TOK_DEV)
    token_pairs, expert_pairs, slot_index, kept_flags = jax.vmap(pair_slots)(order_blocks, pick_blocks, open_blocks)
    block_ids = jnp.arange(block_count, dtype=jnp.int32)[:, None]
    global_tokens = (token_pairs + block_ids * TOK_DEV).reshape(-1)
    rows_per_expert = block_count * CAP
    destination = jnp.where(kept_flags > 0, expert_pairs * rows_per_expert + block_ids * CAP + slot_index, EXPERTS * rows_per_expert).reshape(-1)
    expert_flat = expert_pairs.reshape(-1)
    kept_float = kept_flags.reshape(-1).astype(jnp.float32)
    open_mask = pad_mask.astype(jnp.float32)

    def forward(x_in, gain_one, shift_one, qkv_weight, out_weight, out_shift, gain_two, shift_two, router_weight, first_weight, first_bias, second_weight, second_bias):
        h_one = low(layer_norm(x_in, gain_one, shift_one))
        qkv = low(low_back(jnp.einsum('rld,de->rle', h_one, qkv_weight, precision=best_precision)))
        queries = qkv[:, :, :D].reshape(ROWS, LEN, HEADS, HEAD)
        keys_all = qkv[:, :, D:2 * D].reshape(ROWS, LEN, HEADS, HEAD)
        values_all = qkv[:, :, 2 * D:].reshape(ROWS, LEN, HEADS, HEAD)
        attended = lax.map(jax.checkpoint(attend_row), (queries, keys_all, values_all, open_mask))
        attended = low(low_back(attended))
        branch = low_back(jnp.einsum('rld,de->rle', attended, out_weight, precision=best_precision) + out_shift)
        resid = x_in + branch
        h_two = low(layer_norm(resid, gain_two, shift_two))
        logits = low_back(jnp.einsum('rld,de->rle', h_two, router_weight, precision=best_precision))
        router_probs = to_blocks(jax.nn.softmax(logits, axis=-1))
        h_flat = to_blocks(h_two)
        gates = router_probs[global_tokens, expert_flat] * kept_float
        buffer_rows = jnp.zeros((EXPERTS * rows_per_expert + 1, D), jnp.float32).at[destination].add(h_flat[global_tokens])
        expert_rows = low_back(buffer_rows[:-1].reshape(EXPERTS, rows_per_expert, D))
        expert_outs = lax.map(jax.checkpoint(expert_apply), (expert_rows, first_weight, first_bias, second_weight, second_bias))
        returned = jnp.concatenate([expert_outs.reshape(-1, D), jnp.zeros((1, D), jnp.float32)], axis=0)[destination]
        mixture = jnp.zeros((block_count * TOK_DEV, D), jnp.float32).at[global_tokens].add(gates[:, None] * returned)
        return resid + from_blocks(mixture)
    float_args = tuple((array.astype(jnp.float32) for array in (tokens, ln1_gain, ln1_shift, w_qkv, w_out, out_bias, ln2_gain, ln2_shift, w_router, w_in, in_bias, w_exp_out, exp_out_bias)))
    block_output, pullback = jax.vjp(forward, *float_args)
    grads = pullback(cotangent.astype(jnp.float32))
    return (block_output.astype(jnp.bfloat16), grads[0].astype(jnp.bfloat16), grads[1], grads[2], grads[3], grads[4], grads[5], grads[6], grads[7], grads[8], grads[9], grads[10], grads[11], grads[12])
```

```python
import jax
import jax.numpy as jnp
from jax import lax
from jax.sharding import PartitionSpec as P

D = 768
HEADS = 12
HEAD = 64


norm_eps = 1e-06


def norm_forward(values, norm_gain, norm_shift):
    average = jnp.mean(values, axis=-1, keepdims=True)
    centred = values - average
    inv_scale = lax.rsqrt(jnp.mean(centred * centred, axis=-1, keepdims=True) + norm_eps)
    normed = centred * inv_scale
    return (
        normed * norm_gain.astype(jnp.float32) + norm_shift.astype(jnp.float32),
        normed,
        inv_scale,
    )


def norm_backward(grad_output, normed, inv_scale, norm_gain):
    scaled = grad_output * norm_gain.astype(jnp.float32)
    grad_input = inv_scale * (
        scaled
        - jnp.mean(scaled, axis=-1, keepdims=True)
        - normed * jnp.mean(scaled * normed, axis=-1, keepdims=True)
    )
    return (
        grad_input,
        jnp.sum(grad_output * normed, axis=(0, 1)),
        jnp.sum(grad_output, axis=(0, 1)),
    )


def gelu_slope(values):
    return (
        0.5 * (1.0 + lax.erf(values * 0.7071067811865476))
        + values * jnp.exp(-0.5 * values * values) * 0.3989422804014327
    )


def slot_ranks(order, picks, valid, experts, capacity):
    count = order.shape[0]
    index = jnp.arange(count, dtype=jnp.int32)
    rank = jnp.sum(jnp.where(order[:, None] == index[None, :], index[:, None], 0), axis=0)
    earlier = (rank[None, :] < rank[:, None]).astype(jnp.bfloat16)
    chosen = picks[:, :, None] == jnp.arange(experts, dtype=jnp.int32)
    counted = chosen.astype(jnp.float32) * valid.astype(jnp.float32)[:, None, None]
    before = jnp.dot(
        earlier,
        counted.reshape(count, 2 * experts).astype(jnp.bfloat16),
        preferred_element_type=jnp.float32,
    ).reshape(count, 2, experts)
    firsts = jnp.sum(counted[:, 0], axis=0)
    before = before + jnp.stack([jnp.zeros_like(firsts), firsts])[None]
    slot = jnp.sum(jnp.where(chosen, before, 0.0), axis=2).astype(jnp.int32)
    kept = (valid[:, None] > 0) & (slot < capacity)
    return kept, slot


def pair_slots(order, expert_picks, valid_flags, expert_count, capacity):
    kept, slot = slot_ranks(order, expert_picks, valid_flags, expert_count, capacity)
    tokens = jnp.arange(order.shape[0], dtype=jnp.int32)
    return (
        jnp.concatenate([tokens, tokens]),
        expert_picks.T.reshape(-1),
        slot.T.reshape(-1),
        kept.T.reshape(-1).astype(jnp.int32),
    )


def shards_general(
    tokens,
    cotangent,
    pad_mask,
    expert_ids,
    priority,
    ln1_gain,
    ln1_shift,
    w_qkv,
    w_out,
    out_bias,
    ln2_gain,
    ln2_shift,
    w_router,
    w_in,
    in_bias,
    w_exp_out,
    exp_out_bias,
):
    rows_dev, pos_dev = pad_mask.shape
    tok_count = rows_dev * pos_dev
    expert_count = w_router.shape[1]
    local_experts = w_in.shape[0]
    capacity = (21 * tok_count + 10 * expert_count - 1) // (10 * expert_count)
    scale_factor = HEAD ** (-0.5)
    gain_one, shift_one, qkv_weight, out_weight, out_shift, gain_two, shift_two, router_weight = (
        lax.all_gather(ln1_gain, ("dp", "seq"), axis=0, tiled=True),
        lax.all_gather(ln1_shift, ("dp", "seq"), axis=0, tiled=True),
        lax.all_gather(w_qkv, ("dp", "seq"), axis=0, tiled=True),
        lax.all_gather(w_out, ("dp", "seq"), axis=0, tiled=True),
        lax.all_gather(out_bias, ("dp", "seq"), axis=0, tiled=True),
        lax.all_gather(ln2_gain, ("dp", "seq"), axis=0, tiled=True),
        lax.all_gather(ln2_shift, ("dp", "seq"), axis=0, tiled=True),
        lax.all_gather(w_router, ("dp", "seq"), axis=0, tiled=True),
    )
    x_float = tokens.astype(jnp.float32)
    h_one, normed_one, inv_one = norm_forward(x_float, gain_one, shift_one)
    h_one_low = h_one.astype(jnp.bfloat16)
    qkv_low = jnp.einsum(
        "rpd,de->rpe", h_one_low, qkv_weight, preferred_element_type=jnp.float32
    ).astype(jnp.bfloat16)
    queries = qkv_low[:, :, :D].reshape(rows_dev, pos_dev, HEADS, HEAD)
    kv_all, mask_all = (
        lax.all_gather(qkv_low[:, :, D:], "seq", axis=1, tiled=True),
        lax.all_gather(pad_mask.astype(jnp.bfloat16), "seq", axis=1, tiled=True),
    )
    full_len = kv_all.shape[1]
    keys_all = kv_all[:, :, :D].reshape(rows_dev, full_len, HEADS, HEAD)
    values_all = kv_all[:, :, D:].reshape(rows_dev, full_len, HEADS, HEAD)
    key_open = (mask_all > 0)[:, None, None, :]

    def score_block():
        raw_scores = (
            jnp.einsum("rphd,rkhd->rhpk", queries, keys_all, preferred_element_type=jnp.float32)
            * scale_factor
        )
        return jnp.where(key_open, raw_scores, -1e30)

    scores = score_block()
    row_max = jnp.max(scores, axis=-1, keepdims=True)
    exp_scores = jnp.exp(scores - row_max)
    row_total = jnp.sum(exp_scores, axis=-1, keepdims=True)
    log_total = row_max + jnp.log(row_total)
    probs_low = (exp_scores / row_total).astype(jnp.bfloat16)
    attended = (
        jnp.einsum("rhpk,rkhd->rphd", probs_low, values_all, preferred_element_type=jnp.float32)
        .reshape(rows_dev, pos_dev, D)
        .astype(jnp.bfloat16)
    )
    branch = jnp.einsum(
        "rpd,de->rpe", attended, out_weight, preferred_element_type=jnp.float32
    ) + out_shift.astype(jnp.float32)
    resid = x_float + branch
    h_two, normed_two, inv_two = norm_forward(resid, gain_two, shift_two)
    flat_low = h_two.astype(jnp.bfloat16).reshape(tok_count, D)
    logits = jnp.dot(flat_low, router_weight, preferred_element_type=jnp.float32)
    router_probs = jax.nn.softmax(logits, axis=-1)
    token_pairs, expert_pairs, slot_index, kept_flags = pair_slots(
        priority.reshape(-1),
        expert_ids.reshape(tok_count, 2),
        pad_mask.reshape(-1),
        expert_count,
        capacity,
    )
    dummy_row = expert_count * capacity
    destination = jnp.where(kept_flags > 0, expert_pairs * capacity + slot_index, dummy_row)
    kept_float = kept_flags.astype(jnp.float32)
    gate_pairs = router_probs[token_pairs, expert_pairs] * kept_float
    send_rows = (
        jnp.zeros((dummy_row + 1, D), jnp.bfloat16)
        .at[destination]
        .set(flat_low[token_pairs])[:-1]
        .reshape(expert_count, capacity, D)
    )
    received = lax.all_to_all(send_rows, "dp", split_axis=0, concat_axis=1, tiled=True)
    seq_index = lax.axis_index("seq")
    bias_cols = exp_out_bias.shape[1]
    rows_all = lax.all_gather(received, "seq", axis=1, tiled=True)
    pre_act = (
        jnp.einsum("erd,edf->erf", rows_all, w_in, preferred_element_type=jnp.float32)
        + in_bias.astype(jnp.float32)[:, None, :]
    )
    act_low = jax.nn.gelu(pre_act, approximate=False).astype(jnp.bfloat16)
    partial_out = jnp.einsum("erf,efd->erd", act_low, w_exp_out, preferred_element_type=jnp.float32)
    bias_full = lax.dynamic_update_slice_in_dim(
        jnp.zeros((local_experts, D), jnp.float32),
        exp_out_bias.astype(jnp.float32),
        seq_index * bias_cols,
        1,
    )
    partial_out = partial_out + bias_full[:, None, :]
    expert_out = lax.psum_scatter(
        partial_out.astype(jnp.bfloat16), "seq", scatter_dimension=1, tiled=True
    )
    returned_buf = lax.all_to_all(expert_out, "dp", split_axis=1, concat_axis=0, tiled=True)
    returned = jnp.concatenate(
        [returned_buf.reshape(-1, D), jnp.zeros((1, D), jnp.bfloat16)], axis=0
    )[destination].astype(jnp.float32)
    mixture = (
        jnp.zeros((tok_count, D), jnp.float32).at[token_pairs].add(gate_pairs[:, None] * returned)
    )
    block_output = (resid + mixture.reshape(rows_dev, pos_dev, D)).astype(jnp.bfloat16)
    grad_y = cotangent.astype(jnp.float32)
    grad_pairs = grad_y.reshape(tok_count, D)[token_pairs]
    grad_gates = jnp.sum(grad_pairs * returned, axis=-1) * kept_float
    grad_ret = (gate_pairs[:, None] * grad_pairs).astype(jnp.bfloat16)
    grad_send = (
        jnp.zeros((dummy_row + 1, D), jnp.bfloat16)
        .at[destination]
        .set(grad_ret)[:-1]
        .reshape(expert_count, capacity, D)
    )
    grad_recv = lax.all_to_all(grad_send, "dp", split_axis=0, concat_axis=1, tiled=True)
    grad_all = lax.all_gather(grad_recv, "seq", axis=1, tiled=True)
    pre_again = (
        jnp.einsum("erd,edf->erf", rows_all, w_in, preferred_element_type=jnp.float32)
        + in_bias.astype(jnp.float32)[:, None, :]
    )
    act_again = jax.nn.gelu(pre_again, approximate=False).astype(jnp.bfloat16)
    grad_act = jnp.einsum("erd,efd->erf", grad_all, w_exp_out, preferred_element_type=jnp.float32)
    grad_pre = (grad_act * gelu_slope(pre_again)).astype(jnp.bfloat16)
    w_exp_out_grad = jnp.einsum(
        "erf,erd->efd", act_again, grad_all, preferred_element_type=jnp.float32
    )
    bias_sums = jnp.sum(grad_all, axis=1, dtype=jnp.float32)
    exp_out_bias_grad = lax.dynamic_slice_in_dim(bias_sums, seq_index * bias_cols, bias_cols, 1)
    w_in_grad = jnp.einsum("erd,erf->edf", rows_all, grad_pre, preferred_element_type=jnp.float32)
    in_bias_grad = jnp.sum(grad_pre, axis=1, dtype=jnp.float32)
    grad_rows_part = jnp.einsum("erf,edf->erd", grad_pre, w_in, preferred_element_type=jnp.float32)
    grad_back = lax.psum_scatter(
        grad_rows_part.astype(jnp.bfloat16), "seq", scatter_dimension=1, tiled=True
    )
    grad_buf = lax.all_to_all(grad_back, "dp", split_axis=1, concat_axis=0, tiled=True)
    grad_rows_back = jnp.concatenate(
        [grad_buf.reshape(-1, D), jnp.zeros((1, D), jnp.bfloat16)], axis=0
    )[destination].astype(jnp.float32)
    grad_h2_experts = jnp.zeros((tok_count, D), jnp.float32).at[token_pairs].add(grad_rows_back)
    grad_probs = (
        jnp.zeros((tok_count, expert_count), jnp.float32)
        .at[token_pairs, expert_pairs]
        .add(grad_gates)
    )
    grad_logits = (
        router_probs * (grad_probs - jnp.sum(router_probs * grad_probs, axis=-1, keepdims=True))
    ).astype(jnp.bfloat16)
    router_grad = jnp.einsum("td,te->de", flat_low, grad_logits, preferred_element_type=jnp.float32)
    grad_h2 = grad_h2_experts + jnp.einsum(
        "te,de->td", grad_logits, router_weight, preferred_element_type=jnp.float32
    )
    grad_resid_norm, gain_two_grad, shift_two_grad = norm_backward(
        grad_h2.reshape(rows_dev, pos_dev, D), normed_two, inv_two, gain_two
    )
    grad_resid = grad_y + grad_resid_norm
    grad_branch = grad_resid.astype(jnp.bfloat16)
    out_weight_grad = jnp.einsum(
        "rpd,rpe->de", attended, grad_branch, preferred_element_type=jnp.float32
    )
    out_shift_grad = jnp.sum(grad_branch, axis=(0, 1), dtype=jnp.float32)
    grad_attended = jnp.einsum(
        "rpe,de->rpd", grad_branch, out_weight, preferred_element_type=jnp.float32
    ).astype(jnp.bfloat16)
    grad_att_heads = grad_attended.reshape(rows_dev, pos_dev, HEADS, HEAD)
    scores_again = score_block()
    probs_again = jnp.exp(scores_again - log_total)
    probs_again_low = probs_again.astype(jnp.bfloat16)
    grad_probs_att = jnp.einsum(
        "rphd,rkhd->rhpk", grad_att_heads, values_all, preferred_element_type=jnp.float32
    )
    row_delta = jnp.sum(probs_again * grad_probs_att, axis=-1, keepdims=True)
    grad_scores = (probs_again * (grad_probs_att - row_delta)).astype(jnp.bfloat16)
    grad_queries = (
        jnp.einsum("rhpk,rkhd->rphd", grad_scores, keys_all, preferred_element_type=jnp.float32)
        * scale_factor
    ).reshape(rows_dev, pos_dev, D)
    grad_keys = (
        jnp.einsum("rhpk,rphd->rkhd", grad_scores, queries, preferred_element_type=jnp.float32)
        * scale_factor
    ).reshape(rows_dev, full_len, D)
    grad_values = jnp.einsum(
        "rhpk,rphd->rkhd", probs_again_low, grad_att_heads, preferred_element_type=jnp.float32
    ).reshape(rows_dev, full_len, D)
    grad_kv = lax.psum_scatter(
        jnp.concatenate([grad_keys, grad_values], axis=-1).astype(jnp.bfloat16),
        "seq",
        scatter_dimension=1,
        tiled=True,
    )
    grad_qkv = jnp.concatenate([grad_queries.astype(jnp.bfloat16), grad_kv], axis=-1)
    qkv_weight_grad = jnp.einsum(
        "rpd,rpe->de", h_one_low, grad_qkv, preferred_element_type=jnp.float32
    )
    grad_h1 = jnp.einsum("rpe,de->rpd", grad_qkv, qkv_weight, preferred_element_type=jnp.float32)
    grad_x_norm, gain_one_grad, shift_one_grad = norm_backward(
        grad_h1, normed_one, inv_one, gain_one
    )
    tokens_grad = (grad_resid + grad_x_norm).astype(jnp.bfloat16)
    dense_parts = (
        lax.psum_scatter(gain_one_grad, ("dp", "seq"), scatter_dimension=0, tiled=True),
        lax.psum_scatter(shift_one_grad, ("dp", "seq"), scatter_dimension=0, tiled=True),
        lax.psum_scatter(qkv_weight_grad, ("dp", "seq"), scatter_dimension=0, tiled=True),
        lax.psum_scatter(out_weight_grad, ("dp", "seq"), scatter_dimension=0, tiled=True),
        lax.psum_scatter(out_shift_grad, ("dp", "seq"), scatter_dimension=0, tiled=True),
        lax.psum_scatter(gain_two_grad, ("dp", "seq"), scatter_dimension=0, tiled=True),
        lax.psum_scatter(shift_two_grad, ("dp", "seq"), scatter_dimension=0, tiled=True),
        lax.psum_scatter(router_grad, ("dp", "seq"), scatter_dimension=0, tiled=True),
    )
    return (
        block_output,
        tokens_grad,
        dense_parts[0],
        dense_parts[1],
        dense_parts[2],
        dense_parts[3],
        dense_parts[4],
        dense_parts[5],
        dense_parts[6],
        dense_parts[7],
        w_in_grad,
        in_bias_grad,
        w_exp_out_grad,
        exp_out_bias_grad,
    )


def mm(a, b, contract, low=False):
    out = lax.dot_general(a, b, (contract, ((), ())), preferred_element_type=jnp.float32)
    return out.astype(jnp.bfloat16) if low else out


def norm_stats(values):
    average = jnp.mean(values, axis=-1, keepdims=True)
    centred = values - average
    inv = lax.rsqrt(jnp.mean(centred * centred, axis=-1, keepdims=True) + norm_eps)
    return centred * inv, inv


def norm_grad(grad_output, normed, inv, gain):
    scaled = grad_output * gain
    return inv * (
        scaled
        - jnp.mean(scaled, axis=-1, keepdims=True)
        - normed * jnp.mean(scaled * normed, axis=-1, keepdims=True)
    )


def to_row(block):
    return lax.all_to_all(block, "seq", split_axis=0, concat_axis=1, tiled=True)[0]


def to_block(row, rows_dev):
    split = row.reshape(rows_dev, row.shape[0] // rows_dev, row.shape[1])
    return lax.all_to_all(split, "seq", split_axis=0, concat_axis=0, tiled=True)


def shards_rows(
    tokens,
    cotangent,
    pad_mask,
    expert_ids,
    priority,
    ln1_gain,
    ln1_shift,
    w_qkv,
    w_out,
    out_bias,
    ln2_gain,
    ln2_shift,
    w_router,
    w_in,
    in_bias,
    w_exp_out,
    exp_out_bias,
):
    both = ("dp", "seq")
    rows_dev, pos_dev = pad_mask.shape
    tok = rows_dev * pos_dev
    experts = w_router.shape[1]
    cap = (21 * tok + 10 * experts - 1) // (10 * experts)
    n_seq = lax.axis_size("seq")
    bf, f32 = jnp.bfloat16, jnp.float32
    vectors = jnp.stack([ln1_gain, ln1_shift, out_bias, ln2_gain, ln2_shift], axis=1)
    pad = jnp.zeros((vectors.shape[0], 128 - 5 - experts), bf)
    packed = lax.all_gather(
        jnp.concatenate([w_qkv, w_out, vectors, w_router, pad], axis=1), both, axis=0, tiled=True
    )
    qkv_weight, out_weight = packed[:, : 3 * D], packed[:, 3 * D : 4 * D]
    vectors = packed[:, 4 * D : 4 * D + 5].T.astype(f32)
    gain_one, shift_one, out_shift, gain_two, shift_two = (v[None] for v in vectors)
    router = packed[:, 4 * D + 5 : 4 * D + 5 + experts]
    bias_cols = exp_out_bias.shape[1]
    extra = jnp.zeros((16, D), bf).at[0].set(in_bias[0]).at[1, :bias_cols].set(exp_out_bias[0])
    expert_pack = lax.all_gather(
        jnp.concatenate([w_in[0], w_exp_out[0], extra], axis=0), "seq", axis=0
    )
    first, second = expert_pack[:, :D], expert_pack[:, D : 2 * D]
    first_bias = expert_pack[:, 2 * D].astype(f32)
    second_bias = expert_pack[:, 2 * D + 1, :bias_cols].reshape(1, D).astype(f32)
    picks = expert_ids.reshape(tok, 2)
    kept, slot = slot_ranks(priority.reshape(-1), picks, pad_mask.reshape(-1), experts, cap)
    place = jnp.where(kept, picks * cap + slot, experts * cap)
    where = jnp.arange(experts * cap, dtype=jnp.int32)[None]
    spread = ((place[:, :1] == where) | (place[:, 1:] == where)).astype(bf)
    dy_block = cotangent.reshape(tok, D)
    dy_slots = mm(spread, dy_block, ((0,), (0,)), True).reshape(experts, cap, D)
    dy_slots = lax.all_to_all(dy_slots, "dp", split_axis=0, concat_axis=0, tiled=True)
    dy_slots = dy_slots.reshape(-1, D)
    x = to_row(tokens).astype(f32)
    dy = to_row(cotangent).astype(f32)
    open_row = lax.all_to_all(
        jnp.broadcast_to(pad_mask[:, None], (rows_dev, 8, pos_dev)), "seq", 0, 2, tiled=True
    )[0, :1]
    normed_one, inv_one = norm_stats(x)
    h_one = (normed_one * gain_one + shift_one).astype(bf)
    qkv = mm(h_one, qkv_weight, ((1,), (0,)), True)
    q, k, v = (qkv[:, i * D : (i + 1) * D].reshape(-1, HEADS, HEAD) for i in range(3))
    scale = HEAD ** (-0.5)
    scores = jnp.einsum("qhd,khd->hqk", q, k, preferred_element_type=f32) * scale
    scores = jnp.where((open_row > 0)[:, None], scores, -1e30)
    weights = jnp.exp(scores - jnp.max(scores, axis=-1, keepdims=True))
    probs = weights / jnp.sum(weights, axis=-1, keepdims=True)
    probs_low = probs.astype(bf)
    attended = jnp.einsum("hqk,khd->qhd", probs_low, v, preferred_element_type=f32)
    attended = attended.astype(bf).reshape(-1, D)
    branch = mm(attended, out_weight, ((1,), (0,))) + out_shift
    normed_two, inv_two = norm_stats(x + branch)
    h_two = (normed_two * gain_two + shift_two).astype(bf)
    h_block = to_block(h_two, rows_dev).reshape(tok, D)
    branch_block = to_block(branch.astype(bf), rows_dev).reshape(tok, D)
    rows = mm(spread, h_block, ((0,), (0,)), True).reshape(experts, cap, D)
    rows = lax.all_to_all(rows, "dp", split_axis=0, concat_axis=0, tiled=True).reshape(-1, D)
    mine = lax.axis_index("dp")
    probs_rt = jax.nn.softmax(mm(rows, router, ((1,), (0,))), axis=-1)
    is_mine = (jnp.arange(experts) == mine).astype(f32)[None]
    gate = jnp.sum(probs_rt * is_mine, axis=-1, keepdims=True)
    pre = jnp.einsum("rd,qdf->qrf", rows, first, preferred_element_type=f32) + first_bias[:, None]
    act = jax.nn.gelu(pre, approximate=False).astype(bf)
    made = jnp.einsum("qrf,qfd->rd", act, second, preferred_element_type=f32) + second_bias
    made = made.astype(bf).astype(f32)
    dy_f32 = dy_slots.astype(f32)
    grad_out = (gate * dy_f32).astype(bf)
    grad_act = jnp.einsum("rd,qfd->qrf", grad_out, second, preferred_element_type=f32)
    grad_pre = (grad_act * gelu_slope(pre)).astype(bf)
    grad_gate = jnp.sum(dy_f32 * made, axis=-1, keepdims=True)
    grad_logits = (grad_gate * gate * (is_mine - probs_rt)).astype(bf)
    grad_rows = jnp.einsum("qrf,qdf->rd", grad_pre, first, preferred_element_type=f32)
    grad_rows = (grad_rows + mm(grad_logits, router, ((1,), (1,)))).astype(bf)
    grad_rows = lax.all_to_all(
        grad_rows.reshape(experts, cap, D), "dp", split_axis=0, concat_axis=0, tiled=True
    ).reshape(-1, D)
    made = lax.all_to_all(
        (gate * made).astype(bf).reshape(experts, cap, D),
        "dp",
        split_axis=0,
        concat_axis=0,
        tiled=True,
    ).reshape(-1, D)
    second_grad = jnp.einsum("qrf,rd->qfd", act, grad_out, preferred_element_type=f32)
    first_grad = jnp.einsum("rd,qrf->qdf", rows, grad_pre, preferred_element_type=f32)
    router_grad = mm(rows, grad_logits, ((0,), (0,)))
    extra = jnp.zeros((n_seq, 16, D), f32)
    extra = extra.at[:, 0].set(jnp.sum(grad_pre, axis=1, dtype=f32))
    extra = extra.at[:, 1, :bias_cols].set(
        jnp.sum(grad_out, axis=0, dtype=f32).reshape(n_seq, bias_cols)
    )
    expert_grads = lax.psum_scatter(
        jnp.concatenate([first_grad, second_grad, extra], axis=1).astype(bf),
        "seq",
        scatter_dimension=0,
    ).astype(f32)
    block_output = (
        tokens.reshape(tok, D).astype(f32)
        + branch_block.astype(f32)
        + mm(spread, made, ((1,), (0,)))
    ).astype(bf)
    grad_h2 = mm(spread, grad_rows, ((1,), (0,)), True).reshape(rows_dev, pos_dev, D)
    grad_h2 = to_row(grad_h2).astype(f32)
    gain_two_grad = jnp.sum(grad_h2 * normed_two, axis=0)
    shift_two_grad = jnp.sum(grad_h2, axis=0)
    grad_resid = dy + norm_grad(grad_h2, normed_two, inv_two, gain_two)
    grad_branch = grad_resid.astype(bf)
    out_weight_grad = mm(attended, grad_branch, ((0,), (0,)))
    out_shift_grad = jnp.sum(grad_branch, axis=0, dtype=f32)
    grad_att = mm(grad_branch, out_weight, ((1,), (1,)), True).reshape(-1, HEADS, HEAD)
    grad_probs = jnp.einsum("qhd,khd->hqk", grad_att, v, preferred_element_type=f32)
    delta = jnp.sum(probs * grad_probs, axis=-1, keepdims=True)
    grad_scores = (probs * (grad_probs - delta)).astype(bf)
    grad_q = jnp.einsum("hqk,khd->qhd", grad_scores, k, preferred_element_type=f32) * scale
    grad_k = jnp.einsum("hqk,qhd->khd", grad_scores, q, preferred_element_type=f32) * scale
    grad_v = jnp.einsum("hqk,qhd->khd", probs_low, grad_att, preferred_element_type=f32)
    grad_qkv = jnp.concatenate(
        [g.astype(bf).reshape(-1, D) for g in (grad_q, grad_k, grad_v)], axis=1
    )
    qkv_weight_grad = mm(h_one, grad_qkv, ((0,), (0,)))
    grad_h1 = mm(grad_qkv, qkv_weight, ((1,), (1,)))
    gain_one_grad = jnp.sum(grad_h1 * normed_one, axis=0)
    shift_one_grad = jnp.sum(grad_h1, axis=0)
    grad_x = (grad_resid + norm_grad(grad_h1, normed_one, inv_one, gain_one)).astype(bf)
    tokens_grad = to_block(grad_x, rows_dev)
    vectors = jnp.stack(
        [gain_one_grad, shift_one_grad, out_shift_grad, gain_two_grad, shift_two_grad], axis=1
    )
    pad = jnp.zeros((D, 128 - 5 - experts), f32)
    dense = lax.psum_scatter(
        jnp.concatenate([qkv_weight_grad, out_weight_grad, vectors, router_grad, pad], axis=1),
        both,
        scatter_dimension=0,
        tiled=True,
    )
    vectors = dense[:, 4 * D : 4 * D + 5].T
    return (
        block_output.reshape(rows_dev, pos_dev, D),
        tokens_grad,
        vectors[0],
        vectors[1],
        dense[:, : 3 * D],
        dense[:, 3 * D : 4 * D],
        vectors[2],
        vectors[3],
        vectors[4],
        dense[:, 4 * D + 5 : 4 * D + 5 + experts],
        expert_grads[None, :D],
        expert_grads[None, 2 * D],
        expert_grads[None, D : 2 * D],
        expert_grads[None, 2 * D + 1, :bias_cols],
    )


def shards(*args):
    if args[2].shape[0] == lax.axis_size("seq") and args[13].shape[0] == 1:
        return shards_rows(*args)
    return shards_general(*args)


def solution(mesh):
    return jax.shard_map(
        shards,
        mesh=mesh,
        in_specs=(
            P("dp", "seq", None),
            P("dp", "seq", None),
            P("dp", "seq"),
            P("dp", "seq", None),
            P("dp", "seq"),
            P(("dp", "seq")),
            P(("dp", "seq")),
            P(("dp", "seq"), None),
            P(("dp", "seq"), None),
            P(("dp", "seq")),
            P(("dp", "seq")),
            P(("dp", "seq")),
            P(("dp", "seq"), None),
            P("dp", None, "seq"),
            P("dp", "seq"),
            P("dp", "seq", None),
            P("dp", "seq"),
        ),
        out_specs=(
            P("dp", "seq", None),
            P("dp", "seq", None),
            P(("dp", "seq")),
            P(("dp", "seq")),
            P(("dp", "seq"), None),
            P(("dp", "seq"), None),
            P(("dp", "seq")),
            P(("dp", "seq")),
            P(("dp", "seq")),
            P(("dp", "seq"), None),
            P("dp", None, "seq"),
            P("dp", "seq"),
            P("dp", "seq", None),
            P("dp", "seq"),
        ),
        check_vma=False,
    )
```

```python
import functools

import jax
import jax.numpy as jnp
from jax import lax
from jax.experimental import pallas as pl
from jax.experimental.pallas import tpu as pltpu
from jax.sharding import PartitionSpec as P

D = 768
HEADS = 12
HEAD = 64


norm_eps = 1e-06


def norm_forward(values, norm_gain, norm_shift):
    average = jnp.mean(values, axis=-1, keepdims=True)
    centred = values - average
    inv_scale = lax.rsqrt(jnp.mean(centred * centred, axis=-1, keepdims=True) + norm_eps)
    normed = centred * inv_scale
    return (
        normed * norm_gain.astype(jnp.float32) + norm_shift.astype(jnp.float32),
        normed,
        inv_scale,
    )


def norm_backward(grad_output, normed, inv_scale, norm_gain):
    scaled = grad_output * norm_gain.astype(jnp.float32)
    grad_input = inv_scale * (
        scaled
        - jnp.mean(scaled, axis=-1, keepdims=True)
        - normed * jnp.mean(scaled * normed, axis=-1, keepdims=True)
    )
    return (
        grad_input,
        jnp.sum(grad_output * normed, axis=(0, 1)),
        jnp.sum(grad_output, axis=(0, 1)),
    )


def gelu_slope(values):
    return (
        0.5 * (1.0 + lax.erf(values * 0.7071067811865476))
        + values * jnp.exp(-0.5 * values * values) * 0.3989422804014327
    )


def slot_ranks(order, picks, valid, experts, capacity):
    count = order.shape[0]
    index = jnp.arange(count, dtype=jnp.int32)
    rank = jnp.sum(jnp.where(order[:, None] == index[None, :], index[:, None], 0), axis=0)
    earlier = (rank[None, :] < rank[:, None]).astype(jnp.bfloat16)
    chosen = picks[:, :, None] == jnp.arange(experts, dtype=jnp.int32)
    counted = chosen.astype(jnp.float32) * valid.astype(jnp.float32)[:, None, None]
    before = jnp.dot(
        earlier,
        counted.reshape(count, 2 * experts).astype(jnp.bfloat16),
        preferred_element_type=jnp.float32,
    ).reshape(count, 2, experts)
    firsts = jnp.sum(counted[:, 0], axis=0)
    before = before + jnp.stack([jnp.zeros_like(firsts), firsts])[None]
    slot = jnp.sum(jnp.where(chosen, before, 0.0), axis=2).astype(jnp.int32)
    kept = (valid[:, None] > 0) & (slot < capacity)
    return kept, slot


def pair_slots(order, expert_picks, valid_flags, expert_count, capacity):
    kept, slot = slot_ranks(order, expert_picks, valid_flags, expert_count, capacity)
    tokens = jnp.arange(order.shape[0], dtype=jnp.int32)
    return (
        jnp.concatenate([tokens, tokens]),
        expert_picks.T.reshape(-1),
        slot.T.reshape(-1),
        kept.T.reshape(-1).astype(jnp.int32),
    )


def shards_general(
    tokens,
    cotangent,
    pad_mask,
    expert_ids,
    priority,
    ln1_gain,
    ln1_shift,
    w_qkv,
    w_out,
    out_bias,
    ln2_gain,
    ln2_shift,
    w_router,
    w_in,
    in_bias,
    w_exp_out,
    exp_out_bias,
):
    rows_dev, pos_dev = pad_mask.shape
    tok_count = rows_dev * pos_dev
    expert_count = w_router.shape[1]
    local_experts = w_in.shape[0]
    capacity = (21 * tok_count + 10 * expert_count - 1) // (10 * expert_count)
    scale_factor = HEAD ** (-0.5)
    gain_one, shift_one, qkv_weight, out_weight, out_shift, gain_two, shift_two, router_weight = (
        lax.all_gather(ln1_gain, ("dp", "seq"), axis=0, tiled=True),
        lax.all_gather(ln1_shift, ("dp", "seq"), axis=0, tiled=True),
        lax.all_gather(w_qkv, ("dp", "seq"), axis=0, tiled=True),
        lax.all_gather(w_out, ("dp", "seq"), axis=0, tiled=True),
        lax.all_gather(out_bias, ("dp", "seq"), axis=0, tiled=True),
        lax.all_gather(ln2_gain, ("dp", "seq"), axis=0, tiled=True),
        lax.all_gather(ln2_shift, ("dp", "seq"), axis=0, tiled=True),
        lax.all_gather(w_router, ("dp", "seq"), axis=0, tiled=True),
    )
    x_float = tokens.astype(jnp.float32)
    h_one, normed_one, inv_one = norm_forward(x_float, gain_one, shift_one)
    h_one_low = h_one.astype(jnp.bfloat16)
    qkv_low = jnp.einsum(
        "rpd,de->rpe", h_one_low, qkv_weight, preferred_element_type=jnp.float32
    ).astype(jnp.bfloat16)
    queries = qkv_low[:, :, :D].reshape(rows_dev, pos_dev, HEADS, HEAD)
    kv_all, mask_all = (
        lax.all_gather(qkv_low[:, :, D:], "seq", axis=1, tiled=True),
        lax.all_gather(pad_mask.astype(jnp.bfloat16), "seq", axis=1, tiled=True),
    )
    full_len = kv_all.shape[1]
    keys_all = kv_all[:, :, :D].reshape(rows_dev, full_len, HEADS, HEAD)
    values_all = kv_all[:, :, D:].reshape(rows_dev, full_len, HEADS, HEAD)
    key_open = (mask_all > 0)[:, None, None, :]

    def score_block():
        raw_scores = (
            jnp.einsum("rphd,rkhd->rhpk", queries, keys_all, preferred_element_type=jnp.float32)
            * scale_factor
        )
        return jnp.where(key_open, raw_scores, -1e30)

    scores = score_block()
    row_max = jnp.max(scores, axis=-1, keepdims=True)
    exp_scores = jnp.exp(scores - row_max)
    row_total = jnp.sum(exp_scores, axis=-1, keepdims=True)
    log_total = row_max + jnp.log(row_total)
    probs_low = (exp_scores / row_total).astype(jnp.bfloat16)
    attended = (
        jnp.einsum("rhpk,rkhd->rphd", probs_low, values_all, preferred_element_type=jnp.float32)
        .reshape(rows_dev, pos_dev, D)
        .astype(jnp.bfloat16)
    )
    branch = jnp.einsum(
        "rpd,de->rpe", attended, out_weight, preferred_element_type=jnp.float32
    ) + out_shift.astype(jnp.float32)
    resid = x_float + branch
    h_two, normed_two, inv_two = norm_forward(resid, gain_two, shift_two)
    flat_low = h_two.astype(jnp.bfloat16).reshape(tok_count, D)
    logits = jnp.dot(flat_low, router_weight, preferred_element_type=jnp.float32)
    router_probs = jax.nn.softmax(logits, axis=-1)
    token_pairs, expert_pairs, slot_index, kept_flags = pair_slots(
        priority.reshape(-1),
        expert_ids.reshape(tok_count, 2),
        pad_mask.reshape(-1),
        expert_count,
        capacity,
    )
    dummy_row = expert_count * capacity
    destination = jnp.where(kept_flags > 0, expert_pairs * capacity + slot_index, dummy_row)
    kept_float = kept_flags.astype(jnp.float32)
    gate_pairs = router_probs[token_pairs, expert_pairs] * kept_float
    send_rows = (
        jnp.zeros((dummy_row + 1, D), jnp.bfloat16)
        .at[destination]
        .set(flat_low[token_pairs])[:-1]
        .reshape(expert_count, capacity, D)
    )
    received = lax.all_to_all(send_rows, "dp", split_axis=0, concat_axis=1, tiled=True)
    seq_index = lax.axis_index("seq")
    bias_cols = exp_out_bias.shape[1]
    rows_all = lax.all_gather(received, "seq", axis=1, tiled=True)
    pre_act = (
        jnp.einsum("erd,edf->erf", rows_all, w_in, preferred_element_type=jnp.float32)
        + in_bias.astype(jnp.float32)[:, None, :]
    )
    act_low = jax.nn.gelu(pre_act, approximate=False).astype(jnp.bfloat16)
    partial_out = jnp.einsum("erf,efd->erd", act_low, w_exp_out, preferred_element_type=jnp.float32)
    bias_full = lax.dynamic_update_slice_in_dim(
        jnp.zeros((local_experts, D), jnp.float32),
        exp_out_bias.astype(jnp.float32),
        seq_index * bias_cols,
        1,
    )
    partial_out = partial_out + bias_full[:, None, :]
    expert_out = lax.psum_scatter(
        partial_out.astype(jnp.bfloat16), "seq", scatter_dimension=1, tiled=True
    )
    returned_buf = lax.all_to_all(expert_out, "dp", split_axis=1, concat_axis=0, tiled=True)
    returned = jnp.concatenate(
        [returned_buf.reshape(-1, D), jnp.zeros((1, D), jnp.bfloat16)], axis=0
    )[destination].astype(jnp.float32)
    mixture = (
        jnp.zeros((tok_count, D), jnp.float32).at[token_pairs].add(gate_pairs[:, None] * returned)
    )
    block_output = (resid + mixture.reshape(rows_dev, pos_dev, D)).astype(jnp.bfloat16)
    grad_y = cotangent.astype(jnp.float32)
    grad_pairs = grad_y.reshape(tok_count, D)[token_pairs]
    grad_gates = jnp.sum(grad_pairs * returned, axis=-1) * kept_float
    grad_ret = (gate_pairs[:, None] * grad_pairs).astype(jnp.bfloat16)
    grad_send = (
        jnp.zeros((dummy_row + 1, D), jnp.bfloat16)
        .at[destination]
        .set(grad_ret)[:-1]
        .reshape(expert_count, capacity, D)
    )
    grad_recv = lax.all_to_all(grad_send, "dp", split_axis=0, concat_axis=1, tiled=True)
    grad_all = lax.all_gather(grad_recv, "seq", axis=1, tiled=True)
    pre_again = (
        jnp.einsum("erd,edf->erf", rows_all, w_in, preferred_element_type=jnp.float32)
        + in_bias.astype(jnp.float32)[:, None, :]
    )
    act_again = jax.nn.gelu(pre_again, approximate=False).astype(jnp.bfloat16)
    grad_act = jnp.einsum("erd,efd->erf", grad_all, w_exp_out, preferred_element_type=jnp.float32)
    grad_pre = (grad_act * gelu_slope(pre_again)).astype(jnp.bfloat16)
    w_exp_out_grad = jnp.einsum(
        "erf,erd->efd", act_again, grad_all, preferred_element_type=jnp.float32
    )
    bias_sums = jnp.sum(grad_all, axis=1, dtype=jnp.float32)
    exp_out_bias_grad = lax.dynamic_slice_in_dim(bias_sums, seq_index * bias_cols, bias_cols, 1)
    w_in_grad = jnp.einsum("erd,erf->edf", rows_all, grad_pre, preferred_element_type=jnp.float32)
    in_bias_grad = jnp.sum(grad_pre, axis=1, dtype=jnp.float32)
    grad_rows_part = jnp.einsum("erf,edf->erd", grad_pre, w_in, preferred_element_type=jnp.float32)
    grad_back = lax.psum_scatter(
        grad_rows_part.astype(jnp.bfloat16), "seq", scatter_dimension=1, tiled=True
    )
    grad_buf = lax.all_to_all(grad_back, "dp", split_axis=1, concat_axis=0, tiled=True)
    grad_rows_back = jnp.concatenate(
        [grad_buf.reshape(-1, D), jnp.zeros((1, D), jnp.bfloat16)], axis=0
    )[destination].astype(jnp.float32)
    grad_h2_experts = jnp.zeros((tok_count, D), jnp.float32).at[token_pairs].add(grad_rows_back)
    grad_probs = (
        jnp.zeros((tok_count, expert_count), jnp.float32)
        .at[token_pairs, expert_pairs]
        .add(grad_gates)
    )
    grad_logits = (
        router_probs * (grad_probs - jnp.sum(router_probs * grad_probs, axis=-1, keepdims=True))
    ).astype(jnp.bfloat16)
    router_grad = jnp.einsum("td,te->de", flat_low, grad_logits, preferred_element_type=jnp.float32)
    grad_h2 = grad_h2_experts + jnp.einsum(
        "te,de->td", grad_logits, router_weight, preferred_element_type=jnp.float32
    )
    grad_resid_norm, gain_two_grad, shift_two_grad = norm_backward(
        grad_h2.reshape(rows_dev, pos_dev, D), normed_two, inv_two, gain_two
    )
    grad_resid = grad_y + grad_resid_norm
    grad_branch = grad_resid.astype(jnp.bfloat16)
    out_weight_grad = jnp.einsum(
        "rpd,rpe->de", attended, grad_branch, preferred_element_type=jnp.float32
    )
    out_shift_grad = jnp.sum(grad_branch, axis=(0, 1), dtype=jnp.float32)
    grad_attended = jnp.einsum(
        "rpe,de->rpd", grad_branch, out_weight, preferred_element_type=jnp.float32
    ).astype(jnp.bfloat16)
    grad_att_heads = grad_attended.reshape(rows_dev, pos_dev, HEADS, HEAD)
    scores_again = score_block()
    probs_again = jnp.exp(scores_again - log_total)
    probs_again_low = probs_again.astype(jnp.bfloat16)
    grad_probs_att = jnp.einsum(
        "rphd,rkhd->rhpk", grad_att_heads, values_all, preferred_element_type=jnp.float32
    )
    row_delta = jnp.sum(probs_again * grad_probs_att, axis=-1, keepdims=True)
    grad_scores = (probs_again * (grad_probs_att - row_delta)).astype(jnp.bfloat16)
    grad_queries = (
        jnp.einsum("rhpk,rkhd->rphd", grad_scores, keys_all, preferred_element_type=jnp.float32)
        * scale_factor
    ).reshape(rows_dev, pos_dev, D)
    grad_keys = (
        jnp.einsum("rhpk,rphd->rkhd", grad_scores, queries, preferred_element_type=jnp.float32)
        * scale_factor
    ).reshape(rows_dev, full_len, D)
    grad_values = jnp.einsum(
        "rhpk,rphd->rkhd", probs_again_low, grad_att_heads, preferred_element_type=jnp.float32
    ).reshape(rows_dev, full_len, D)
    grad_kv = lax.psum_scatter(
        jnp.concatenate([grad_keys, grad_values], axis=-1).astype(jnp.bfloat16),
        "seq",
        scatter_dimension=1,
        tiled=True,
    )
    grad_qkv = jnp.concatenate([grad_queries.astype(jnp.bfloat16), grad_kv], axis=-1)
    qkv_weight_grad = jnp.einsum(
        "rpd,rpe->de", h_one_low, grad_qkv, preferred_element_type=jnp.float32
    )
    grad_h1 = jnp.einsum("rpe,de->rpd", grad_qkv, qkv_weight, preferred_element_type=jnp.float32)
    grad_x_norm, gain_one_grad, shift_one_grad = norm_backward(
        grad_h1, normed_one, inv_one, gain_one
    )
    tokens_grad = (grad_resid + grad_x_norm).astype(jnp.bfloat16)
    dense_parts = (
        lax.psum_scatter(gain_one_grad, ("dp", "seq"), scatter_dimension=0, tiled=True),
        lax.psum_scatter(shift_one_grad, ("dp", "seq"), scatter_dimension=0, tiled=True),
        lax.psum_scatter(qkv_weight_grad, ("dp", "seq"), scatter_dimension=0, tiled=True),
        lax.psum_scatter(out_weight_grad, ("dp", "seq"), scatter_dimension=0, tiled=True),
        lax.psum_scatter(out_shift_grad, ("dp", "seq"), scatter_dimension=0, tiled=True),
        lax.psum_scatter(gain_two_grad, ("dp", "seq"), scatter_dimension=0, tiled=True),
        lax.psum_scatter(shift_two_grad, ("dp", "seq"), scatter_dimension=0, tiled=True),
        lax.psum_scatter(router_grad, ("dp", "seq"), scatter_dimension=0, tiled=True),
    )
    return (
        block_output,
        tokens_grad,
        dense_parts[0],
        dense_parts[1],
        dense_parts[2],
        dense_parts[3],
        dense_parts[4],
        dense_parts[5],
        dense_parts[6],
        dense_parts[7],
        w_in_grad,
        in_bias_grad,
        w_exp_out_grad,
        exp_out_bias_grad,
    )


MESH = pl.DeviceIdType.MESH
VMEM = pl.BlockSpec(memory_space=pltpu.VMEM)
ANY = pl.BlockSpec(memory_space=pl.ANY)
ERF = (0.1274147955, -0.142248368, 0.7107068705, -0.7265760135, 0.5307027145)


def nn(a, b):
    return lax.dot_general(a, b, (((1,), (0,)), ((), ())), preferred_element_type=jnp.float32)


def nt(a, b):
    return lax.dot_general(a, b, (((1,), (1,)), ((), ())), preferred_element_type=jnp.float32)


def tn(a, b):
    return lax.dot_general(a, b, (((0,), (0,)), ((), ())), preferred_element_type=jnp.float32)


def gelu_parts(v):
    bell = jnp.exp(v * v * -0.5)
    t = 1.0 / (jnp.abs(v) * (0.3275911 * 0.7071067811865476) + 1.0)
    a, b, c, d, e = ERF
    tail = ((((e * t + d) * t + c) * t + b) * t + a) * t * bell
    cdf = jnp.where(v < 0.0, tail, 1.0 - tail)
    return v * cdf, cdf + v * (bell * 0.3989422804014327)


def other(me, step):
    bit = lambda k: lax.rem(me // k + step // k, 2) * k
    return bit(4) + bit(2) + bit(1)


def moe_kernel(
    experts,
    h_ref,
    into_ref,
    from_ref,
    dy_ref,
    first_any,
    second_any,
    bias1_ref,
    bias2_ref,
    router_ref,
    grad_ref,
    outs_ref,
    first_grad_ref,
    second_grad_ref,
    router_grad_ref,
    bias1_grad_ref,
    bias2_grad_ref,
    sent,
    rows,
    rows_t,
    go,
    act,
    gp,
    back_sent,
    back,
    logit_grad,
    first,
    second,
    w_sem,
    send_sem,
    recv_sem,
    send_sem2,
    recv_sem2,
):
    n = experts
    cap = dy_ref.shape[0] // n
    bf, f32 = jnp.bfloat16, jnp.float32
    blocks = first.shape[0]
    me, seq = lax.axis_index("dp"), lax.axis_index("seq")
    barrier = pltpu.get_barrier_semaphore()
    for step in range(1, n):
        pl.semaphore_signal(barrier, inc=1, device_id=(other(me, step), seq), device_id_type=MESH)
    load1 = pltpu.make_async_copy(first_any, first, w_sem.at[0])
    load2 = pltpu.make_async_copy(second_any, second, w_sem.at[1])
    load1.start()
    load2.start()
    at = lambda i: pl.ds(pl.multiple_of(i * cap, cap), cap)
    pl.semaphore_wait(barrier, n - 1)

    def dispatch(step, source, target, sems):
        to = other(me, step)
        return pltpu.make_async_remote_copy(
            source.at[at(to)],
            target.at[at(me)],
            sems[0].at[step],
            sems[1].at[step],
            device_id=(to, seq),
            device_id_type=MESH,
        )

    out_sems, back_sems = (send_sem, recv_sem), (send_sem2, recv_sem2)

    @pl.loop(0, n - 1)
    def _(i):
        step = n - 1 - i
        to = other(me, step)
        sent[at(to), :] = nn(into_ref[at(to), :], h_ref[...]).astype(bf)
        dispatch(step, sent, rows, out_sems).start()

    rows[at(me), :] = nn(into_ref[at(me), :], h_ref[...]).astype(bf)
    load1.wait()
    load2.wait()
    lane = lax.broadcasted_iota(jnp.int32, (cap, 128), 1)

    @pl.loop(0, n)
    def _(step):
        peer = other(me, step)

        @pl.when(step > 0)
        def _():
            dispatch(step, sent, rows, out_sems).wait_recv()

        x = rows[at(peer), :]
        dy = dy_ref[at(peer), :].astype(f32)
        logits = jnp.where(lane < n, nn(x, router_ref[...]), -1e30)
        probs = jnp.exp(logits - jnp.max(logits, axis=-1, keepdims=True))
        probs = probs / jnp.sum(probs, axis=-1, keepdims=True)
        mine = (lane == me).astype(f32)
        gate = jnp.sum(probs * mine, axis=-1, keepdims=True)
        grad_out = (gate * dy).astype(bf)
        go[at(peer), :] = grad_out

        def block(q, sums):
            out, grad_row = sums
            value, slope = gelu_parts(nn(x, first[q]) + bias1_ref[q])
            value = value.astype(bf)
            act[q, at(peer), :] = value
            grad_pre = (nt(grad_out, second[q]) * slope).astype(bf)
            gp[q, at(peer), :] = grad_pre
            return out + nn(value, second[q]), grad_row + nt(grad_pre, first[q])

        zero = jnp.zeros((cap, x.shape[1]), f32)
        out, grad_row = lax.fori_loop(0, blocks, block, (zero, zero))
        made = (out + bias2_ref[...]).astype(bf).astype(f32)
        grad_gate = jnp.sum(dy * made, axis=-1, keepdims=True)
        grad_logits = (grad_gate * gate * (mine - probs)).astype(bf)
        logit_grad[at(peer), :] = grad_logits
        grad_row = (grad_row + nt(grad_logits, router_ref[...])).astype(bf)
        outs_ref[at(peer), :] = (gate * made).astype(bf)

        @pl.when(step > 0)
        def _():
            back_sent[at(peer), :] = grad_row
            dispatch(step, back_sent, back, back_sems).start()

        @pl.when(step == 0)
        def _():
            back[at(peer), :] = grad_row

    rows_t[...] = rows[...].T
    ones = jnp.ones((8, rows.shape[0]), bf)

    @pl.loop(0, blocks)
    def _(q):
        first_grad_ref[q] = nn(rows_t[...], gp[q]).astype(bf)
        second_grad_ref[q] = tn(act[q], go[...]).astype(bf)
        bias1_grad_ref[q] = nn(ones, gp[q])

    bias2_grad_ref[...] = nn(ones, go[...])
    router_grad_ref[...] = nn(rows_t[...], logit_grad[...])

    @pl.loop(1, n)
    def _(step):
        dispatch(step, back_sent, back, back_sems).wait()
        dispatch(step, sent, rows, out_sems).wait_send()

    grad_ref[...] = nn(from_ref[...], back[...]).astype(bf)


def moe(h_block, into, outof, dy_slots, first, second, bias1, bias2, router, experts):
    bf, f32 = jnp.bfloat16, jnp.float32
    tok, width = h_block.shape
    slots = into.shape[0]
    blocks, hidden = first.shape[0], first.shape[2]
    sds = jax.ShapeDtypeStruct
    dma = pltpu.SemaphoreType.DMA
    big = (slots, width)
    return pl.pallas_call(
        functools.partial(moe_kernel, experts),
        out_shape=(
            sds((tok, width), bf),
            sds(big, bf),
            sds(first.shape, bf),
            sds(second.shape, bf),
            sds((width, 128), f32),
            sds((blocks, 8, hidden), f32),
            sds((8, width), f32),
        ),
        in_specs=[VMEM] * 4 + [ANY] * 2 + [VMEM] * 3,
        out_specs=(VMEM,) * 7,
        scratch_shapes=[
            pltpu.VMEM(big, bf),
            pltpu.VMEM(big, bf),
            pltpu.VMEM((width, slots), bf),
            pltpu.VMEM(big, bf),
            pltpu.VMEM((blocks, slots, hidden), bf),
            pltpu.VMEM((blocks, slots, hidden), bf),
            pltpu.VMEM(big, bf),
            pltpu.VMEM(big, bf),
            pltpu.VMEM((slots, 128), bf),
            pltpu.VMEM(first.shape, bf),
            pltpu.VMEM(second.shape, bf),
            dma((2,)),
            dma((experts,)),
            dma((experts,)),
            dma((experts,)),
            dma((experts,)),
        ],
        compiler_params=pltpu.CompilerParams(
            collective_id=1, has_side_effects=True, vmem_limit_bytes=61 * 2**20
        ),
        cost_estimate=pl.CostEstimate(
            flops=12 * slots * width * hidden * blocks, bytes_accessed=4 * 10**7, transcendentals=slots * hidden * blocks
        ),
        name="moe",
    )(h_block, into, outof, dy_slots, first, second, bias1, bias2, router)


def mm(a, b, contract, low=False):
    out = lax.dot_general(a, b, (contract, ((), ())), preferred_element_type=jnp.float32)
    return out.astype(jnp.bfloat16) if low else out


def norm_stats(values):
    average = jnp.mean(values, axis=-1, keepdims=True)
    centred = values - average
    inv = lax.rsqrt(jnp.mean(centred * centred, axis=-1, keepdims=True) + norm_eps)
    return centred * inv, inv


def norm_grad(grad_output, normed, inv, gain):
    scaled = grad_output * gain
    return inv * (
        scaled
        - jnp.mean(scaled, axis=-1, keepdims=True)
        - normed * jnp.mean(scaled * normed, axis=-1, keepdims=True)
    )


def to_row(block):
    return lax.all_to_all(block, "seq", split_axis=0, concat_axis=1, tiled=True)[0]


def to_block(row, rows_dev):
    split = row.reshape(rows_dev, row.shape[0] // rows_dev, row.shape[1])
    return lax.all_to_all(split, "seq", split_axis=0, concat_axis=0, tiled=True)


def shards_rows(
    tokens,
    cotangent,
    pad_mask,
    expert_ids,
    priority,
    ln1_gain,
    ln1_shift,
    w_qkv,
    w_out,
    out_bias,
    ln2_gain,
    ln2_shift,
    w_router,
    w_in,
    in_bias,
    w_exp_out,
    exp_out_bias,
):
    both = ("dp", "seq")
    rows_dev, pos_dev = pad_mask.shape
    tok = rows_dev * pos_dev
    experts = w_router.shape[1]
    cap = (21 * tok + 10 * experts - 1) // (10 * experts)
    n_seq = lax.axis_size("seq")
    bf, f32 = jnp.bfloat16, jnp.float32
    vectors = jnp.stack([ln1_gain, ln1_shift, out_bias, ln2_gain, ln2_shift], axis=1)
    pad = jnp.zeros((vectors.shape[0], 128 - 5 - experts), bf)
    packed = lax.all_gather(
        jnp.concatenate([w_qkv, w_out, vectors, w_router, pad], axis=1), both, axis=0, tiled=True
    )
    qkv_weight, out_weight = packed[:, : 3 * D], packed[:, 3 * D : 4 * D]
    vectors = packed[:, 4 * D : 4 * D + 5].T.astype(f32)
    gain_one, shift_one, out_shift, gain_two, shift_two = (v[None] for v in vectors)
    router = packed[:, 4 * D + 5 : 4 * D + 5 + experts]
    bias_cols = exp_out_bias.shape[1]
    extra = jnp.zeros((16, D), bf).at[0].set(in_bias[0]).at[1, :bias_cols].set(exp_out_bias[0])
    expert_pack = lax.all_gather(
        jnp.concatenate([w_in[0], w_exp_out[0], extra], axis=0), "seq", axis=0
    )
    first, second = expert_pack[:, :D], expert_pack[:, D : 2 * D]
    first_bias = expert_pack[:, 2 * D].astype(f32)
    second_bias = expert_pack[:, 2 * D + 1, :bias_cols].reshape(1, D).astype(f32)
    held = -(-cap // 16) * 16
    picks = expert_ids.reshape(tok, 2)
    kept, slot = slot_ranks(priority.reshape(-1), picks, pad_mask.reshape(-1), experts, cap)
    place = jnp.where(kept, picks * held + slot, experts * held)
    where = jnp.arange(experts * held, dtype=jnp.int32)
    outof = ((place[:, :1] == where[None]) | (place[:, 1:] == where[None])).astype(bf)
    place = place.T
    into = ((place[:1] == where[:, None]) | (place[1:] == where[:, None])).astype(bf)
    dy_slots = mm(into, cotangent.reshape(tok, D), ((1,), (0,)), True).reshape(experts, held, D)
    dy_slots = lax.all_to_all(dy_slots, "dp", split_axis=0, concat_axis=0, tiled=True)
    dy_slots = dy_slots.reshape(-1, D)
    x = to_row(tokens).astype(f32)
    dy = to_row(cotangent).astype(f32)
    open_row = lax.all_to_all(
        jnp.broadcast_to(pad_mask[:, None], (rows_dev, 8, pos_dev)), "seq", 0, 2, tiled=True
    )[0, :1]
    normed_one, inv_one = norm_stats(x)
    h_one = (normed_one * gain_one + shift_one).astype(bf)
    qkv = mm(h_one, qkv_weight, ((1,), (0,)), True)
    q, k, v = (qkv[:, i * D : (i + 1) * D].reshape(-1, HEADS, HEAD) for i in range(3))
    scale = HEAD ** (-0.5)
    scores = jnp.einsum("qhd,khd->hqk", q, k, preferred_element_type=f32) * scale
    scores = jnp.where((open_row > 0)[:, None], scores, -1e30)
    weights = jnp.exp(scores - jnp.max(scores, axis=-1, keepdims=True))
    probs = weights / jnp.sum(weights, axis=-1, keepdims=True)
    probs_low = probs.astype(bf)
    attended = jnp.einsum("hqk,khd->qhd", probs_low, v, preferred_element_type=f32)
    attended = attended.astype(bf).reshape(-1, D)
    branch = mm(attended, out_weight, ((1,), (0,))) + out_shift
    normed_two, inv_two = norm_stats(x + branch)
    h_two = (normed_two * gain_two + shift_two).astype(bf)
    h_block = to_block(h_two, rows_dev).reshape(tok, D)
    branch_block = to_block(branch.astype(bf), rows_dev).reshape(tok, D)
    wide_router = jnp.pad(router, ((0, 0), (0, 128 - experts)))
    grad_h2, made, first_grad, second_grad, router_grad, bias1_grad, bias2_grad = moe(
        h_block, into, outof, dy_slots, first, second, first_bias[:, None], second_bias, wide_router, experts
    )
    made = lax.all_to_all(
        made.reshape(experts, held, D),
        "dp",
        split_axis=0,
        concat_axis=0,
        tiled=True,
    ).reshape(-1, D)
    extra = jnp.zeros((n_seq, 16, D), f32).at[:, 0].set(bias1_grad[:, 0])
    extra = extra.at[:, 1, :bias_cols].set(bias2_grad[0].reshape(n_seq, bias_cols))
    extra = extra.astype(bf)
    router_grad = router_grad[:, :experts]
    expert_grads = lax.psum_scatter(
        jnp.concatenate([first_grad, second_grad, extra], axis=1),
        "seq",
        scatter_dimension=0,
    ).astype(f32)
    block_output = (
        tokens.reshape(tok, D).astype(f32)
        + branch_block.astype(f32)
        + mm(outof, made, ((1,), (0,)))
    ).astype(bf)
    grad_h2 = to_row(grad_h2.reshape(rows_dev, pos_dev, D)).astype(f32)
    gain_two_grad = jnp.sum(grad_h2 * normed_two, axis=0)
    shift_two_grad = jnp.sum(grad_h2, axis=0)
    grad_resid = dy + norm_grad(grad_h2, normed_two, inv_two, gain_two)
    grad_branch = grad_resid.astype(bf)
    out_weight_grad = mm(attended, grad_branch, ((0,), (0,)))
    out_shift_grad = jnp.sum(grad_branch, axis=0, dtype=f32)
    grad_att = mm(grad_branch, out_weight, ((1,), (1,)), True).reshape(-1, HEADS, HEAD)
    grad_probs = jnp.einsum("qhd,khd->hqk", grad_att, v, preferred_element_type=f32)
    delta = jnp.sum(probs * grad_probs, axis=-1, keepdims=True)
    grad_scores = (probs * (grad_probs - delta)).astype(bf)
    grad_q = jnp.einsum("hqk,khd->qhd", grad_scores, k, preferred_element_type=f32) * scale
    grad_k = jnp.einsum("hqk,qhd->khd", grad_scores, q, preferred_element_type=f32) * scale
    grad_v = jnp.einsum("hqk,qhd->khd", probs_low, grad_att, preferred_element_type=f32)
    grad_qkv = jnp.concatenate(
        [g.astype(bf).reshape(-1, D) for g in (grad_q, grad_k, grad_v)], axis=1
    )
    qkv_weight_grad = mm(h_one, grad_qkv, ((0,), (0,)))
    grad_h1 = mm(grad_qkv, qkv_weight, ((1,), (1,)))
    gain_one_grad = jnp.sum(grad_h1 * normed_one, axis=0)
    shift_one_grad = jnp.sum(grad_h1, axis=0)
    grad_x = (grad_resid + norm_grad(grad_h1, normed_one, inv_one, gain_one)).astype(bf)
    tokens_grad = to_block(grad_x, rows_dev)
    vectors = jnp.stack(
        [gain_one_grad, shift_one_grad, out_shift_grad, gain_two_grad, shift_two_grad], axis=1
    )
    pad = jnp.zeros((D, 128 - 5 - experts), f32)
    dense = lax.psum_scatter(
        jnp.concatenate([qkv_weight_grad, out_weight_grad, vectors, router_grad, pad], axis=1),
        both,
        scatter_dimension=0,
        tiled=True,
    )
    vectors = dense[:, 4 * D : 4 * D + 5].T
    return (
        block_output.reshape(rows_dev, pos_dev, D),
        tokens_grad,
        vectors[0],
        vectors[1],
        dense[:, : 3 * D],
        dense[:, 3 * D : 4 * D],
        vectors[2],
        vectors[3],
        vectors[4],
        dense[:, 4 * D + 5 : 4 * D + 5 + experts],
        expert_grads[None, :D],
        expert_grads[None, 2 * D],
        expert_grads[None, D : 2 * D],
        expert_grads[None, 2 * D + 1, :bias_cols],
    )


def shards(*args):
    block_rows, local_experts, n_dp = args[2].shape[0], args[13].shape[0], lax.axis_size("dp")
    if block_rows == lax.axis_size("seq") and local_experts == 1 and n_dp == 8:
        return shards_rows(*args)
    return shards_general(*args)


def solution(mesh):
    return jax.shard_map(
        shards,
        mesh=mesh,
        in_specs=(
            P("dp", "seq", None),
            P("dp", "seq", None),
            P("dp", "seq"),
            P("dp", "seq", None),
            P("dp", "seq"),
            P(("dp", "seq")),
            P(("dp", "seq")),
            P(("dp", "seq"), None),
            P(("dp", "seq"), None),
            P(("dp", "seq")),
            P(("dp", "seq")),
            P(("dp", "seq")),
            P(("dp", "seq"), None),
            P("dp", None, "seq"),
            P("dp", "seq"),
            P("dp", "seq", None),
            P("dp", "seq"),
        ),
        out_specs=(
            P("dp", "seq", None),
            P("dp", "seq", None),
            P(("dp", "seq")),
            P(("dp", "seq")),
            P(("dp", "seq"), None),
            P(("dp", "seq"), None),
            P(("dp", "seq")),
            P(("dp", "seq")),
            P(("dp", "seq")),
            P(("dp", "seq"), None),
            P("dp", None, "seq"),
            P("dp", "seq"),
            P("dp", "seq", None),
            P("dp", "seq"),
        ),
        check_vma=False,
    )
```

```python
import functools

import jax
import jax.numpy as jnp
from jax import lax
from jax.experimental import pallas as pl
from jax.experimental.pallas import tpu as pltpu
from jax.sharding import PartitionSpec as P

D = 768
HEADS = 12
HEAD = 64


norm_eps = 1e-06


def norm_forward(values, norm_gain, norm_shift):
    average = jnp.mean(values, axis=-1, keepdims=True)
    centred = values - average
    inv_scale = lax.rsqrt(jnp.mean(centred * centred, axis=-1, keepdims=True) + norm_eps)
    normed = centred * inv_scale
    return (
        normed * norm_gain.astype(jnp.float32) + norm_shift.astype(jnp.float32),
        normed,
        inv_scale,
    )


def norm_backward(grad_output, normed, inv_scale, norm_gain):
    scaled = grad_output * norm_gain.astype(jnp.float32)
    grad_input = inv_scale * (
        scaled
        - jnp.mean(scaled, axis=-1, keepdims=True)
        - normed * jnp.mean(scaled * normed, axis=-1, keepdims=True)
    )
    return (
        grad_input,
        jnp.sum(grad_output * normed, axis=(0, 1)),
        jnp.sum(grad_output, axis=(0, 1)),
    )


def gelu_slope(values):
    return (
        0.5 * (1.0 + lax.erf(values * 0.7071067811865476))
        + values * jnp.exp(-0.5 * values * values) * 0.3989422804014327
    )


def slot_ranks(order, picks, valid, experts, capacity):
    count = order.shape[0]
    index = jnp.arange(count, dtype=jnp.int32)
    rank = jnp.sum(jnp.where(order[:, None] == index[None, :], index[:, None], 0), axis=0)
    earlier = (rank[None, :] < rank[:, None]).astype(jnp.bfloat16)
    chosen = picks[:, :, None] == jnp.arange(experts, dtype=jnp.int32)
    counted = chosen.astype(jnp.float32) * valid.astype(jnp.float32)[:, None, None]
    before = jnp.dot(
        earlier,
        counted.reshape(count, 2 * experts).astype(jnp.bfloat16),
        preferred_element_type=jnp.float32,
    ).reshape(count, 2, experts)
    firsts = jnp.sum(counted[:, 0], axis=0)
    before = before + jnp.stack([jnp.zeros_like(firsts), firsts])[None]
    slot = jnp.sum(jnp.where(chosen, before, 0.0), axis=2).astype(jnp.int32)
    kept = (valid[:, None] > 0) & (slot < capacity)
    return kept, slot


def pair_slots(order, expert_picks, valid_flags, expert_count, capacity):
    kept, slot = slot_ranks(order, expert_picks, valid_flags, expert_count, capacity)
    tokens = jnp.arange(order.shape[0], dtype=jnp.int32)
    return (
        jnp.concatenate([tokens, tokens]),
        expert_picks.T.reshape(-1),
        slot.T.reshape(-1),
        kept.T.reshape(-1).astype(jnp.int32),
    )


def shards_general(
    tokens,
    cotangent,
    pad_mask,
    expert_ids,
    priority,
    ln1_gain,
    ln1_shift,
    w_qkv,
    w_out,
    out_bias,
    ln2_gain,
    ln2_shift,
    w_router,
    w_in,
    in_bias,
    w_exp_out,
    exp_out_bias,
):
    rows_dev, pos_dev = pad_mask.shape
    tok_count = rows_dev * pos_dev
    expert_count = w_router.shape[1]
    local_experts = w_in.shape[0]
    capacity = (21 * tok_count + 10 * expert_count - 1) // (10 * expert_count)
    scale_factor = HEAD ** (-0.5)
    gain_one, shift_one, qkv_weight, out_weight, out_shift, gain_two, shift_two, router_weight = (
        lax.all_gather(ln1_gain, ("dp", "seq"), axis=0, tiled=True),
        lax.all_gather(ln1_shift, ("dp", "seq"), axis=0, tiled=True),
        lax.all_gather(w_qkv, ("dp", "seq"), axis=0, tiled=True),
        lax.all_gather(w_out, ("dp", "seq"), axis=0, tiled=True),
        lax.all_gather(out_bias, ("dp", "seq"), axis=0, tiled=True),
        lax.all_gather(ln2_gain, ("dp", "seq"), axis=0, tiled=True),
        lax.all_gather(ln2_shift, ("dp", "seq"), axis=0, tiled=True),
        lax.all_gather(w_router, ("dp", "seq"), axis=0, tiled=True),
    )
    x_float = tokens.astype(jnp.float32)
    h_one, normed_one, inv_one = norm_forward(x_float, gain_one, shift_one)
    h_one_low = h_one.astype(jnp.bfloat16)
    qkv_low = jnp.einsum(
        "rpd,de->rpe", h_one_low, qkv_weight, preferred_element_type=jnp.float32
    ).astype(jnp.bfloat16)
    queries = qkv_low[:, :, :D].reshape(rows_dev, pos_dev, HEADS, HEAD)
    kv_all, mask_all = (
        lax.all_gather(qkv_low[:, :, D:], "seq", axis=1, tiled=True),
        lax.all_gather(pad_mask.astype(jnp.bfloat16), "seq", axis=1, tiled=True),
    )
    full_len = kv_all.shape[1]
    keys_all = kv_all[:, :, :D].reshape(rows_dev, full_len, HEADS, HEAD)
    values_all = kv_all[:, :, D:].reshape(rows_dev, full_len, HEADS, HEAD)
    key_open = (mask_all > 0)[:, None, None, :]

    def score_block():
        raw_scores = (
            jnp.einsum("rphd,rkhd->rhpk", queries, keys_all, preferred_element_type=jnp.float32)
            * scale_factor
        )
        return jnp.where(key_open, raw_scores, -1e30)

    scores = score_block()
    row_max = jnp.max(scores, axis=-1, keepdims=True)
    exp_scores = jnp.exp(scores - row_max)
    row_total = jnp.sum(exp_scores, axis=-1, keepdims=True)
    log_total = row_max + jnp.log(row_total)
    probs_low = (exp_scores / row_total).astype(jnp.bfloat16)
    attended = (
        jnp.einsum("rhpk,rkhd->rphd", probs_low, values_all, preferred_element_type=jnp.float32)
        .reshape(rows_dev, pos_dev, D)
        .astype(jnp.bfloat16)
    )
    branch = jnp.einsum(
        "rpd,de->rpe", attended, out_weight, preferred_element_type=jnp.float32
    ) + out_shift.astype(jnp.float32)
    resid = x_float + branch
    h_two, normed_two, inv_two = norm_forward(resid, gain_two, shift_two)
    flat_low = h_two.astype(jnp.bfloat16).reshape(tok_count, D)
    logits = jnp.dot(flat_low, router_weight, preferred_element_type=jnp.float32)
    router_probs = jax.nn.softmax(logits, axis=-1)
    token_pairs, expert_pairs, slot_index, kept_flags = pair_slots(
        priority.reshape(-1),
        expert_ids.reshape(tok_count, 2),
        pad_mask.reshape(-1),
        expert_count,
        capacity,
    )
    dummy_row = expert_count * capacity
    destination = jnp.where(kept_flags > 0, expert_pairs * capacity + slot_index, dummy_row)
    kept_float = kept_flags.astype(jnp.float32)
    gate_pairs = router_probs[token_pairs, expert_pairs] * kept_float
    send_rows = (
        jnp.zeros((dummy_row + 1, D), jnp.bfloat16)
        .at[destination]
        .set(flat_low[token_pairs])[:-1]
        .reshape(expert_count, capacity, D)
    )
    received = lax.all_to_all(send_rows, "dp", split_axis=0, concat_axis=1, tiled=True)
    seq_index = lax.axis_index("seq")
    bias_cols = exp_out_bias.shape[1]
    rows_all = lax.all_gather(received, "seq", axis=1, tiled=True)
    pre_act = (
        jnp.einsum("erd,edf->erf", rows_all, w_in, preferred_element_type=jnp.float32)
        + in_bias.astype(jnp.float32)[:, None, :]
    )
    act_low = jax.nn.gelu(pre_act, approximate=False).astype(jnp.bfloat16)
    partial_out = jnp.einsum("erf,efd->erd", act_low, w_exp_out, preferred_element_type=jnp.float32)
    bias_full = lax.dynamic_update_slice_in_dim(
        jnp.zeros((local_experts, D), jnp.float32),
        exp_out_bias.astype(jnp.float32),
        seq_index * bias_cols,
        1,
    )
    partial_out = partial_out + bias_full[:, None, :]
    expert_out = lax.psum_scatter(
        partial_out.astype(jnp.bfloat16), "seq", scatter_dimension=1, tiled=True
    )
    returned_buf = lax.all_to_all(expert_out, "dp", split_axis=1, concat_axis=0, tiled=True)
    returned = jnp.concatenate(
        [returned_buf.reshape(-1, D), jnp.zeros((1, D), jnp.bfloat16)], axis=0
    )[destination].astype(jnp.float32)
    mixture = (
        jnp.zeros((tok_count, D), jnp.float32).at[token_pairs].add(gate_pairs[:, None] * returned)
    )
    block_output = (resid + mixture.reshape(rows_dev, pos_dev, D)).astype(jnp.bfloat16)
    grad_y = cotangent.astype(jnp.float32)
    grad_pairs = grad_y.reshape(tok_count, D)[token_pairs]
    grad_gates = jnp.sum(grad_pairs * returned, axis=-1) * kept_float
    grad_ret = (gate_pairs[:, None] * grad_pairs).astype(jnp.bfloat16)
    grad_send = (
        jnp.zeros((dummy_row + 1, D), jnp.bfloat16)
        .at[destination]
        .set(grad_ret)[:-1]
        .reshape(expert_count, capacity, D)
    )
    grad_recv = lax.all_to_all(grad_send, "dp", split_axis=0, concat_axis=1, tiled=True)
    grad_all = lax.all_gather(grad_recv, "seq", axis=1, tiled=True)
    pre_again = (
        jnp.einsum("erd,edf->erf", rows_all, w_in, preferred_element_type=jnp.float32)
        + in_bias.astype(jnp.float32)[:, None, :]
    )
    act_again = jax.nn.gelu(pre_again, approximate=False).astype(jnp.bfloat16)
    grad_act = jnp.einsum("erd,efd->erf", grad_all, w_exp_out, preferred_element_type=jnp.float32)
    grad_pre = (grad_act * gelu_slope(pre_again)).astype(jnp.bfloat16)
    w_exp_out_grad = jnp.einsum(
        "erf,erd->efd", act_again, grad_all, preferred_element_type=jnp.float32
    )
    bias_sums = jnp.sum(grad_all, axis=1, dtype=jnp.float32)
    exp_out_bias_grad = lax.dynamic_slice_in_dim(bias_sums, seq_index * bias_cols, bias_cols, 1)
    w_in_grad = jnp.einsum("erd,erf->edf", rows_all, grad_pre, preferred_element_type=jnp.float32)
    in_bias_grad = jnp.sum(grad_pre, axis=1, dtype=jnp.float32)
    grad_rows_part = jnp.einsum("erf,edf->erd", grad_pre, w_in, preferred_element_type=jnp.float32)
    grad_back = lax.psum_scatter(
        grad_rows_part.astype(jnp.bfloat16), "seq", scatter_dimension=1, tiled=True
    )
    grad_buf = lax.all_to_all(grad_back, "dp", split_axis=1, concat_axis=0, tiled=True)
    grad_rows_back = jnp.concatenate(
        [grad_buf.reshape(-1, D), jnp.zeros((1, D), jnp.bfloat16)], axis=0
    )[destination].astype(jnp.float32)
    grad_h2_experts = jnp.zeros((tok_count, D), jnp.float32).at[token_pairs].add(grad_rows_back)
    grad_probs = (
        jnp.zeros((tok_count, expert_count), jnp.float32)
        .at[token_pairs, expert_pairs]
        .add(grad_gates)
    )
    grad_logits = (
        router_probs * (grad_probs - jnp.sum(router_probs * grad_probs, axis=-1, keepdims=True))
    ).astype(jnp.bfloat16)
    router_grad = jnp.einsum("td,te->de", flat_low, grad_logits, preferred_element_type=jnp.float32)
    grad_h2 = grad_h2_experts + jnp.einsum(
        "te,de->td", grad_logits, router_weight, preferred_element_type=jnp.float32
    )
    grad_resid_norm, gain_two_grad, shift_two_grad = norm_backward(
        grad_h2.reshape(rows_dev, pos_dev, D), normed_two, inv_two, gain_two
    )
    grad_resid = grad_y + grad_resid_norm
    grad_branch = grad_resid.astype(jnp.bfloat16)
    out_weight_grad = jnp.einsum(
        "rpd,rpe->de", attended, grad_branch, preferred_element_type=jnp.float32
    )
    out_shift_grad = jnp.sum(grad_branch, axis=(0, 1), dtype=jnp.float32)
    grad_attended = jnp.einsum(
        "rpe,de->rpd", grad_branch, out_weight, preferred_element_type=jnp.float32
    ).astype(jnp.bfloat16)
    grad_att_heads = grad_attended.reshape(rows_dev, pos_dev, HEADS, HEAD)
    scores_again = score_block()
    probs_again = jnp.exp(scores_again - log_total)
    probs_again_low = probs_again.astype(jnp.bfloat16)
    grad_probs_att = jnp.einsum(
        "rphd,rkhd->rhpk", grad_att_heads, values_all, preferred_element_type=jnp.float32
    )
    row_delta = jnp.sum(probs_again * grad_probs_att, axis=-1, keepdims=True)
    grad_scores = (probs_again * (grad_probs_att - row_delta)).astype(jnp.bfloat16)
    grad_queries = (
        jnp.einsum("rhpk,rkhd->rphd", grad_scores, keys_all, preferred_element_type=jnp.float32)
        * scale_factor
    ).reshape(rows_dev, pos_dev, D)
    grad_keys = (
        jnp.einsum("rhpk,rphd->rkhd", grad_scores, queries, preferred_element_type=jnp.float32)
        * scale_factor
    ).reshape(rows_dev, full_len, D)
    grad_values = jnp.einsum(
        "rhpk,rphd->rkhd", probs_again_low, grad_att_heads, preferred_element_type=jnp.float32
    ).reshape(rows_dev, full_len, D)
    grad_kv = lax.psum_scatter(
        jnp.concatenate([grad_keys, grad_values], axis=-1).astype(jnp.bfloat16),
        "seq",
        scatter_dimension=1,
        tiled=True,
    )
    grad_qkv = jnp.concatenate([grad_queries.astype(jnp.bfloat16), grad_kv], axis=-1)
    qkv_weight_grad = jnp.einsum(
        "rpd,rpe->de", h_one_low, grad_qkv, preferred_element_type=jnp.float32
    )
    grad_h1 = jnp.einsum("rpe,de->rpd", grad_qkv, qkv_weight, preferred_element_type=jnp.float32)
    grad_x_norm, gain_one_grad, shift_one_grad = norm_backward(
        grad_h1, normed_one, inv_one, gain_one
    )
    tokens_grad = (grad_resid + grad_x_norm).astype(jnp.bfloat16)
    dense_parts = (
        lax.psum_scatter(gain_one_grad, ("dp", "seq"), scatter_dimension=0, tiled=True),
        lax.psum_scatter(shift_one_grad, ("dp", "seq"), scatter_dimension=0, tiled=True),
        lax.psum_scatter(qkv_weight_grad, ("dp", "seq"), scatter_dimension=0, tiled=True),
        lax.psum_scatter(out_weight_grad, ("dp", "seq"), scatter_dimension=0, tiled=True),
        lax.psum_scatter(out_shift_grad, ("dp", "seq"), scatter_dimension=0, tiled=True),
        lax.psum_scatter(gain_two_grad, ("dp", "seq"), scatter_dimension=0, tiled=True),
        lax.psum_scatter(shift_two_grad, ("dp", "seq"), scatter_dimension=0, tiled=True),
        lax.psum_scatter(router_grad, ("dp", "seq"), scatter_dimension=0, tiled=True),
    )
    return (
        block_output,
        tokens_grad,
        dense_parts[0],
        dense_parts[1],
        dense_parts[2],
        dense_parts[3],
        dense_parts[4],
        dense_parts[5],
        dense_parts[6],
        dense_parts[7],
        w_in_grad,
        in_bias_grad,
        w_exp_out_grad,
        exp_out_bias_grad,
    )


MESH = pl.DeviceIdType.MESH
VMEM = pl.BlockSpec(memory_space=pltpu.VMEM)
ANY = pl.BlockSpec(memory_space=pl.ANY)
ERF = (0.1274147955, -0.142248368, 0.7107068705, -0.7265760135, 0.5307027145)


def nn(a, b):
    return lax.dot_general(a, b, (((1,), (0,)), ((), ())), preferred_element_type=jnp.float32)


def nt(a, b):
    return lax.dot_general(a, b, (((1,), (1,)), ((), ())), preferred_element_type=jnp.float32)


def tn(a, b):
    return lax.dot_general(a, b, (((0,), (0,)), ((), ())), preferred_element_type=jnp.float32)


def gelu_parts(v):
    bell = jnp.exp(v * v * -0.5)
    t = 1.0 / (jnp.abs(v) * (0.3275911 * 0.7071067811865476) + 1.0)
    a, b, c, d, e = ERF
    tail = ((((e * t + d) * t + c) * t + b) * t + a) * t * bell
    cdf = jnp.where(v < 0.0, tail, 1.0 - tail)
    return v * cdf, cdf + v * (bell * 0.3989422804014327)


def other(me, step):
    bit = lambda k: lax.rem(me // k + step // k, 2) * k
    return bit(4) + bit(2) + bit(1)


def moe_kernel(
    experts,
    h_ref,
    into_ref,
    from_ref,
    dy_ref,
    first_any,
    second_any,
    bias1_ref,
    bias2_ref,
    router_ref,
    grad_ref,
    outs_ref,
    first_grad_ref,
    second_grad_ref,
    router_grad_ref,
    bias_grad_ref,
    sent,
    rows,
    rows_t,
    go,
    act,
    gp,
    back_sent,
    back,
    logit_grad,
    first,
    second,
    w_sem,
    send_sem,
    recv_sem,
    send_sem2,
    recv_sem2,
):
    n = experts
    cap = dy_ref.shape[0] // n
    bf, f32 = jnp.bfloat16, jnp.float32
    blocks = first.shape[0]
    me, seq = lax.axis_index("dp"), lax.axis_index("seq")
    barrier = pltpu.get_barrier_semaphore()
    for step in range(1, n):
        pl.semaphore_signal(barrier, inc=1, device_id=(other(me, step), seq), device_id_type=MESH)
    load1 = pltpu.make_async_copy(first_any, first, w_sem.at[0])
    load2 = pltpu.make_async_copy(second_any, second, w_sem.at[1])
    load1.start()
    load2.start()
    at = lambda i: pl.ds(pl.multiple_of(i * cap, cap), cap)
    pl.semaphore_wait(barrier, n - 1)

    def dispatch(step, source, target, sems):
        to = other(me, step)
        return pltpu.make_async_remote_copy(
            source.at[at(to)],
            target.at[at(me)],
            sems[0].at[step],
            sems[1].at[step],
            device_id=(to, seq),
            device_id_type=MESH,
        )

    out_sems, back_sems = (send_sem, recv_sem), (send_sem2, recv_sem2)

    @pl.loop(0, n - 1)
    def _(i):
        step = n - 1 - i
        to = other(me, step)
        sent[at(to), :] = nn(into_ref[at(to), :], h_ref[...]).astype(bf)
        dispatch(step, sent, rows, out_sems).start()

    rows[at(me), :] = nn(into_ref[at(me), :], h_ref[...]).astype(bf)
    load1.wait()
    load2.wait()
    lane = lax.broadcasted_iota(jnp.int32, (cap, 128), 1)

    @pl.loop(0, n)
    def _(step):
        peer = other(me, step)

        @pl.when(step > 0)
        def _():
            dispatch(step, sent, rows, out_sems).wait_recv()

        x = rows[at(peer), :]
        dy = dy_ref[at(peer), :].astype(f32)
        logits = jnp.where(lane < n, nn(x, router_ref[...]), -1e30)
        probs = jnp.exp(logits - jnp.max(logits, axis=-1, keepdims=True))
        probs = probs / jnp.sum(probs, axis=-1, keepdims=True)
        mine = (lane == me).astype(f32)
        gate = jnp.sum(probs * mine, axis=-1, keepdims=True)
        grad_out = (gate * dy).astype(bf)
        go[at(peer), :] = grad_out

        def block(q, sums):
            out, grad_row = sums
            value, slope = gelu_parts(nn(x, first[q]) + bias1_ref[q])
            value = value.astype(bf)
            act[q, at(peer), :] = value
            grad_pre = (nt(grad_out, second[q]) * slope).astype(bf)
            gp[q, at(peer), :] = grad_pre
            return out + nn(value, second[q]), grad_row + nt(grad_pre, first[q])

        zero = jnp.zeros((cap, x.shape[1]), f32)
        out, grad_row = lax.fori_loop(0, blocks, block, (zero, zero))
        made = (out + bias2_ref[...]).astype(bf).astype(f32)
        grad_gate = jnp.sum(dy * made, axis=-1, keepdims=True)
        grad_logits = (grad_gate * gate * (mine - probs)).astype(bf)
        logit_grad[at(peer), :] = grad_logits
        grad_row = (grad_row + nt(grad_logits, router_ref[...])).astype(bf)
        outs_ref[at(peer), :] = (gate * made).astype(bf)

        @pl.when(step > 0)
        def _():
            back_sent[at(peer), :] = grad_row
            dispatch(step, back_sent, back, back_sems).start()

        @pl.when(step == 0)
        def _():
            back[at(peer), :] = grad_row

    rows_t[...] = rows[...].T
    ones = jnp.ones((8, rows.shape[0]), bf)

    @pl.loop(0, blocks)
    def _(q):
        first_grad_ref[q] = nn(rows_t[...], gp[q]).astype(bf)
        second_grad_ref[q] = tn(act[q], go[...]).astype(bf)
        bias_grad_ref[q, :8] = nn(ones, gp[q])
        bias_grad_ref[q, 8:] = nn(ones, go[...])

    router_grad_ref[...] = tn(logit_grad[...], rows[...])[: router_grad_ref.shape[0]]

    @pl.loop(1, n)
    def _(step):
        dispatch(step, back_sent, back, back_sems).wait()
        dispatch(step, sent, rows, out_sems).wait_send()

    grad_ref[...] = nn(from_ref[...], back[...]).astype(bf)


def moe(h_block, into, outof, dy_slots, first, second, bias1, bias2, router, experts):
    bf, f32 = jnp.bfloat16, jnp.float32
    tok, width = h_block.shape
    slots = into.shape[0]
    blocks, hidden = first.shape[0], first.shape[2]
    sds = jax.ShapeDtypeStruct
    dma = pltpu.SemaphoreType.DMA
    big = (slots, width)
    return pl.pallas_call(
        functools.partial(moe_kernel, experts),
        out_shape=(
            sds((tok, width), bf),
            sds(big, bf),
            sds(first.shape, bf),
            sds(second.shape, bf),
            sds((8, width), f32),
            sds((blocks, 16, hidden), f32),
        ),
        in_specs=[VMEM] * 4 + [ANY] * 2 + [VMEM] * 3,
        out_specs=(VMEM,) * 6,
        scratch_shapes=[
            pltpu.VMEM(big, bf),
            pltpu.VMEM(big, bf),
            pltpu.VMEM((width, slots), bf),
            pltpu.VMEM(big, bf),
            pltpu.VMEM((blocks, slots, hidden), bf),
            pltpu.VMEM((blocks, slots, hidden), bf),
            pltpu.VMEM(big, bf),
            pltpu.VMEM(big, bf),
            pltpu.VMEM((slots, 128), bf),
            pltpu.VMEM(first.shape, bf),
            pltpu.VMEM(second.shape, bf),
            dma((2,)),
            dma((experts,)),
            dma((experts,)),
            dma((experts,)),
            dma((experts,)),
        ],
        compiler_params=pltpu.CompilerParams(
            collective_id=1, has_side_effects=True, vmem_limit_bytes=61 * 2**20
        ),
        cost_estimate=pl.CostEstimate(
            flops=12 * slots * width * hidden * blocks, bytes_accessed=4 * 10**7, transcendentals=slots * hidden * blocks
        ),
        name="moe",
    )(h_block, into, outof, dy_slots, first, second, bias1, bias2, router)


def mm(a, b, contract, low=False):
    out = lax.dot_general(a, b, (contract, ((), ())), preferred_element_type=jnp.float32)
    return out.astype(jnp.bfloat16) if low else out


def norm_stats(values):
    average = jnp.mean(values, axis=-1, keepdims=True)
    centred = values - average
    inv = lax.rsqrt(jnp.mean(centred * centred, axis=-1, keepdims=True) + norm_eps)
    return centred * inv, inv


def norm_grad(grad_output, normed, inv, gain):
    scaled = grad_output * gain
    return inv * (
        scaled
        - jnp.mean(scaled, axis=-1, keepdims=True)
        - normed * jnp.mean(scaled * normed, axis=-1, keepdims=True)
    )


def rows_of(i, size):
    return pl.ds(pl.multiple_of(i * size, size), size)


def split_axes():
    dp, seq = lax.axis_index("dp"), lax.axis_index("seq")
    return dp // 2, lax.rem(dp, 2), seq // 2, lax.rem(seq, 2)


def greet(n_dp, n_seq):
    dp, seq = lax.axis_index("dp"), lax.axis_index("seq")
    barrier = pltpu.get_barrier_semaphore()
    for step in range(1, n_dp):
        pl.semaphore_signal(
            barrier, inc=1, device_id=(other(dp, step), seq), device_id_type=MESH
        )
    for step in range(1, n_seq):
        pl.semaphore_signal(
            barrier, inc=1, device_id=(dp, lax.rem(seq + step, n_seq)), device_id_type=MESH
        )
    pl.semaphore_wait(barrier, n_dp - 1 + n_seq - 1)


def remote(source, target, send, recv, device):
    return pltpu.make_async_remote_copy(
        source, target, send, recv, device_id=device, device_id_type=MESH
    )


def back_kernel(
    n_dp,
    n_seq,
    grad_any,
    resid_any,
    x_any,
    dy_any,
    att_any,
    qkv_any,
    probs_any,
    packed_any,
    vectors_ref,
    outs_any,
    outof_any,
    tokens_any,
    branch_any,
    first_any,
    second_any,
    bias_ref,
    router_grad_ref,
    block_out_ref,
    tokens_grad_ref,
    dense_ref,
    small_ref,
    expert_ref,
    bias_out_ref,
    grad_rows,
    resid,
    x_row,
    dy_row,
    att,
    qkv,
    probs,
    w_qkv,
    w_out,
    outs,
    outof,
    tokens,
    branch,
    own_e,
    recv_e,
    recv_x,
    recv_b,
    grad_resid,
    grad_att,
    grad_qkv,
    h_one,
    grad_x,
    part,
    recv_c,
    recv_1,
    recv_2,
    recv_3,
    sums,
    recv_s,
    load_sem,
    probs_sem,
    own_sem,
    gs_sem,
    gr_sem,
    os_sem,
    or_sem,
    es_sem,
    er_sem,
    xs_sem,
    xr_sem,
    bs_sem,
    br_sem,
    ps_sem,
    pr_sem,
    ss_sem,
    sr_sem,
    ts_sem,
    tr_sem,
):
    bf, f32 = jnp.bfloat16, jnp.float32
    dp, seq = lax.axis_index("dp"), lax.axis_index("seq")
    z, y, x, c = split_axes()
    pos = grad_rows.shape[0] // n_seq
    cap = outs.shape[0] // n_dp
    core_peer, x_peer = (dp, x * 2 + 1 - c), (dp, (1 - x) * 2 + c)
    y_peer = (z * 2 + 1 - y, seq)
    z_peer = lambda step: (lax.rem(z + step, 4) * 2 + y, seq)
    loads = [
        pltpu.make_async_copy(a, b, load_sem.at[i])
        for i, (a, b) in enumerate(
            (
                (resid_any, resid),
                (dy_any, dy_row),
                (att_any, att),
                (packed_any.at[:, 3 * D : 4 * D], w_out),
                (qkv_any, qkv),
                (x_any, x_row),
                (packed_any.at[:, : 3 * D], w_qkv),
                (outof_any, outof),
                (tokens_any, tokens),
                (branch_any, branch),
            )
        )
    ]
    fetch = lambda head: pltpu.make_async_copy(
        probs_any.at[head], probs.at[head % 2], probs_sem.at[head % 2]
    )
    for load in loads[:4]:
        load.start()
    greet(n_dp, n_seq)
    to_rows = []
    for step in range(1, n_seq):
        to = lax.rem(seq + step, n_seq)
        to_rows.append(
            remote(
                grad_any.at[rows_of(to, pos)],
                grad_rows.at[rows_of(seq, pos)],
                gs_sem.at[step],
                gr_sem.at[step],
                (dp, to),
            )
        )
    for copy in to_rows:
        copy.start()
    own_rows = pltpu.make_async_copy(
        grad_any.at[rows_of(seq, pos)], grad_rows.at[rows_of(seq, pos)], own_sem.at[0]
    )
    own_rows.start()
    experts_c, experts_own = [], []
    for i, side in enumerate((1 - x, x)):
        for j, ref in enumerate((first_any, second_any)):
            k = i * 2 + j
            experts_c.append(
                remote(
                    ref.at[side * 2 + 1 - c],
                    recv_e.at[i, j],
                    es_sem.at[k],
                    er_sem.at[k],
                    core_peer,
                )
            )
            experts_own.append(
                pltpu.make_async_copy(ref.at[side * 2 + c], own_e.at[i, j], own_sem.at[1 + k])
            )
    for copy in experts_c + experts_own:
        copy.start()
    returns = []
    for step in range(n_dp - 1, 0, -1):
        to = other(dp, step)
        returns.append(
            remote(
                outs_any.at[rows_of(to, cap)],
                outs.at[rows_of(dp, cap)],
                os_sem.at[step],
                or_sem.at[step],
                (to, seq),
            )
        )
    for copy in returns:
        copy.start()
    own_outs = pltpu.make_async_copy(
        outs_any.at[rows_of(dp, cap)], outs.at[rows_of(dp, cap)], own_sem.at[5]
    )
    own_outs.start()
    biases = []
    for step in range(1, n_seq):
        to = lax.rem(seq + step, n_seq)
        biases.append(
            remote(bias_ref.at[to], recv_b.at[step], bs_sem.at[step], br_sem.at[step], (dp, to))
        )
    for copy in biases:
        copy.start()
    for load in loads[4:]:
        load.start()
    fetch(0).start()
    fetch(1).start()
    vec = lambda i: vectors_ref[i : i + 1, :]
    row_sum = lambda v: jnp.sum(v, axis=0, keepdims=True)

    def norm_back(grad_output, values, gain):
        normed, inv = norm_stats(values)
        sums_of = (row_sum(grad_output * normed), row_sum(grad_output))
        return norm_grad(grad_output, normed, inv, gain), *sums_of

    def piece_fill(i, value):
        half = value.shape[1] // 2
        for owner in range(n_dp * n_seq):
            oz, oy, ox, oc = owner // 8, owner // 4 % 2, owner // 2 % 2, owner % 2
            block = value[24 * owner : 24 * owner + 24].astype(bf)
            part[i, oc, 0, ox, oy, oz] = block[:, :half]
            part[i, oc, 1, oy, ox, oz] = block[:, half:]

    first_axis = ((x, x_peer), (y, y_peer))

    def piece_copies(i, stage):
        sems = lambda k: (ps_sem.at[i, k], pr_sem.at[i, k])
        if stage == 0:
            return [remote(part.at[i, 1 - c], recv_c.at[i], *sems(0), core_peer)]
        made = []
        for h in range(2):
            (f, f_peer), (g, g_peer) = first_axis[h], first_axis[1 - h]
            if stage == 1:
                made.append(
                    remote(part.at[i, c, h, 1 - f], recv_1.at[i, h], *sems(1 + h), f_peer)
                )
            elif stage == 2:
                made.append(
                    remote(part.at[i, c, h, f, 1 - g], recv_2.at[i, h], *sems(3 + h), g_peer)
                )
            else:
                for step in range(1, 4):
                    made.append(
                        remote(
                            part.at[i, c, h, f, g, lax.rem(z + step, 4)],
                            recv_3.at[i, h, step],
                            *sems(4 + h * 3 + step),
                            z_peer(step),
                        )
                    )
        return made

    def add(a, b):
        return (a.astype(f32) + b.astype(f32)).astype(bf)

    def piece_advance(i, stage):
        for copy in piece_copies(i, stage - 1):
            copy.wait_recv()
        if stage == 1:
            part[i, c] = add(part[i, c], recv_c[i])
        for h in range(2):
            f, g = first_axis[h][0], first_axis[1 - h][0]
            if stage == 2:
                part[i, c, h, f] = add(part[i, c, h, f], recv_1[i, h])
            elif stage == 3:
                part[i, c, h, f, g] = add(part[i, c, h, f, g], recv_2[i, h])
            elif stage == 4:
                total = part[i, c, h, f, g, z].astype(f32)
                for step in range(1, 4):
                    total = total + recv_3[i, h, step].astype(f32)
                half = total.shape[1]
                dense_ref[:, (2 * i + h) * half : (2 * i + h + 1) * half] = total
        if stage < 4:
            for copy in piece_copies(i, stage):
                copy.start()

    def small_copies(stage):
        peers = ([core_peer], [x_peer], [y_peer], [z_peer(1), z_peer(2), z_peer(3)])[stage]
        return [
            remote(
                sums.at[stage],
                recv_s.at[stage + k],
                ss_sem.at[stage + k],
                sr_sem.at[stage + k],
                peer,
            )
            for k, peer in enumerate(peers)
        ]

    def small_advance(stage):
        for copy in small_copies(stage - 1):
            copy.wait_recv()
        if stage < 4:
            sums[stage] = sums[stage - 1] + recv_s[stage - 1]
            for copy in small_copies(stage):
                copy.start()
        else:
            small_ref[...] = sums[3] + recv_s[3] + recv_s[4] + recv_s[5]

    own_e_copies = experts_own

    def experts_send_x():
        for j in range(2):
            experts_c[j].wait_recv()
            own_e_copies[j].wait()
            own_e[0, j] = add(own_e[0, j], recv_e[0, j])
            experts_x[j].start()

    experts_x = [
        remote(own_e.at[0, j], recv_x.at[j], xs_sem.at[j], xr_sem.at[j], x_peer) for j in range(2)
    ]

    def experts_end():
        for j in range(2):
            experts_c[2 + j].wait_recv()
            own_e_copies[2 + j].wait()
            experts_x[j].wait_recv()

            @pl.loop(0, 6)
            def _(k):
                at = rows_of(k, recv_x.shape[1] // 6)
                expert_ref[j, at, :] = (
                    own_e[1, j, at, :].astype(f32)
                    + recv_e[1, j, at, :].astype(f32)
                    + recv_x[j, at, :].astype(f32)
                )

        bias = bias_ref[seq]
        for step in range(1, n_seq):
            biases[step - 1].wait_recv()
            bias = bias + recv_b[step]
        bias_out_ref[...] = bias

    for load in loads[:3]:
        load.wait()
    own_rows.wait()
    for copy in to_rows:
        copy.wait_recv()
    grad_in, gain_two, shift_two = norm_back(grad_rows[...].astype(f32), resid[...], vec(3))
    grad_resid[...] = dy_row[...].astype(f32) + grad_in
    grad_branch = grad_resid[...].astype(bf)
    out_shift = row_sum(grad_branch.astype(f32))
    loads[3].wait()
    grad_att[...] = nt(grad_branch, w_out[...]).astype(bf)
    piece_fill(0, tn(att[...], grad_branch))
    for copy in piece_copies(0, 0):
        copy.start()
    loads[4].wait()
    loads[5].wait()
    x_normed, _ = norm_stats(x_row[...].astype(f32))
    h_one[...] = (x_normed * vec(0) + vec(1)).astype(bf)
    experts_send_x()
    lane = lax.broadcasted_iota(jnp.int32, (1, 128), 1) // HEAD
    scale = HEAD ** (-0.5)
    for pair in range(HEADS // 2):
        cols = slice(128 * pair, 128 * pair + 128)
        q, k, v = (qkv[:, D * i + 128 * pair : D * i + 128 * pair + 128] for i in range(3))
        go = grad_att[:, cols]
        both = go.astype(f32) * att[:, cols].astype(f32)
        grads = [jnp.zeros(q.shape, f32)] * 3
        for h in range(2):
            head = 2 * pair + h
            keep = (lane == h).astype(bf)
            fetch(head).wait()
            p = probs[head % 2]
            go_h = go * keep
            delta = jnp.sum(both * keep.astype(f32), axis=-1, keepdims=True)
            ds = (p.astype(f32) * (nt(go_h, v) - delta)).astype(bf)
            grads = [
                grads[0] + nn(ds, k * keep),
                grads[1] + tn(ds, q * keep),
                grads[2] + tn(p, go_h),
            ]
            if head + 2 < HEADS:
                fetch(head + 2).start()
        for i, factor in enumerate((scale, scale, 1.0)):
            at = (2 * 128) * (3 * (pair // 2) + i) + 128 * (pair % 2)
            grad_qkv[:, at : at + 128] = (grads[i] * factor).astype(bf)
        if pair < 4:
            piece_advance(0, pair + 1)
        if pair in (2, 3, 4, 5):
            piece_advance(1, pair - 1)
        if pair in (4, 5):
            piece_advance(2, pair - 3)
        if pair % 2 == 1:
            i = pair // 2 + 1
            piece_fill(i, tn(h_one[...], grad_qkv[:, D * (i - 1) : D * i]))
            for copy in piece_copies(i, 0):
                copy.start()
    loads[6].wait()
    grad_h1 = jnp.zeros(resid.shape, f32)
    for i in range(9):
        at = 256 * i
        col = D * (i % 3) + 256 * (i // 3)
        grad_h1 = grad_h1 + nt(grad_qkv[:, at : at + 256], w_qkv[:, col : col + 256])
    grad_in, gain_one, shift_one = norm_back(grad_h1, x_row[...].astype(f32), vec(0))
    sums[0] = jnp.concatenate(
        [gain_one, shift_one, out_shift, gain_two, shift_two, jnp.zeros((3, D), f32), router_grad_ref[...]], axis=0
    )
    for copy in small_copies(0):
        copy.start()
    grad_x[...] = (grad_resid[...] + grad_in).astype(bf)
    to_blocks = []
    for step in range(1, n_seq):
        to = lax.rem(seq + step, n_seq)
        to_blocks.append(
            remote(
                grad_x.at[rows_of(to, pos)],
                tokens_grad_ref.at[rows_of(seq, pos)],
                ts_sem.at[step],
                tr_sem.at[step],
                (dp, to),
            )
        )
    for copy in to_blocks:
        copy.start()
    tokens_grad_ref[rows_of(seq, pos), :] = grad_x[rows_of(seq, pos), :]
    piece_advance(3, 1)
    piece_advance(2, 3)
    small_advance(1)
    own_outs.wait()
    for copy in returns:
        copy.wait_recv()
    for load in loads[7:]:
        load.wait()
    block_out_ref[...] = (
        tokens[...].astype(f32) + branch[...].astype(f32) + nn(outof[...], outs[...])
    ).astype(bf)
    piece_advance(3, 2)
    small_advance(2)
    piece_advance(2, 4)
    experts_end()
    piece_advance(3, 3)
    small_advance(3)
    piece_advance(3, 4)
    small_advance(4)
    for copy in to_blocks:
        copy.wait_recv()
    for copy in to_rows + experts_c + returns + biases + experts_x + to_blocks:
        copy.wait_send()
    for stage in range(4):
        for i in range(4):
            for copy in piece_copies(i, stage):
                copy.wait_send()
        for copy in small_copies(stage):
            copy.wait_send()


def back(
    n_dp,
    n_seq,
    grad_h2,
    resid,
    x_row,
    dy_row,
    att,
    qkv,
    probs,
    packed,
    vectors,
    outs,
    outof,
    tokens,
    branch,
    first_grad,
    second_grad,
    biases,
    router_grad,
):
    bf, f32 = jnp.bfloat16, jnp.float32
    sds, dma, vmem = jax.ShapeDtypeStruct, pltpu.SemaphoreType.DMA, pltpu.VMEM
    tok, slots = outof.shape
    pos = tok // n_seq
    half = D // 2
    return pl.pallas_call(
        functools.partial(back_kernel, n_dp, n_seq),
        out_shape=(
            sds((tok, D), bf),
            sds((tok, D), bf),
            sds((D // (n_dp * n_seq), 4 * D), f32),
            sds((16, D), f32),
            sds((2,) + first_grad.shape[1:], f32),
            sds(biases.shape[1:], f32),
        ),
        in_specs=[ANY] * 8 + [VMEM] + [ANY] * 6 + [VMEM] * 2,
        out_specs=(VMEM,) * 6,
        scratch_shapes=[
            vmem((tok, D), bf),
            vmem((tok, D), f32),
            vmem((tok, D), bf),
            vmem((tok, D), bf),
            vmem((tok, D), bf),
            vmem((tok, 3 * D), bf),
            vmem((2,) + probs.shape[1:], bf),
            vmem((D, 3 * D), bf),
            vmem((D, D), bf),
            vmem((slots, D), bf),
            vmem((tok, slots), bf),
            vmem((tok, D), bf),
            vmem((tok, D), bf),
            vmem((2, 2, D, D), bf),
            vmem((2, 2, D, D), bf),
            vmem((2, D, D), bf),
            vmem((n_seq,) + biases.shape[1:], f32),
            vmem((tok, D), f32),
            vmem((tok, D), bf),
            vmem((tok, 3 * D), bf),
            vmem((tok, D), bf),
            vmem((tok, D), bf),
            vmem((4, 2, 2, 2, 2, 4, 24, half), bf),
            vmem((4, 2, 2, 2, 4, 24, half), bf),
            vmem((4, 2, 2, 4, 24, half), bf),
            vmem((4, 2, 4, 24, half), bf),
            vmem((4, 2, 4, 24, half), bf),
            vmem((4, 16, D), f32),
            vmem((6, 16, D), f32),
            dma((10,)),
            dma((2,)),
            dma((6,)),
            dma((n_seq,)),
            dma((n_seq,)),
            dma((n_dp,)),
            dma((n_dp,)),
            dma((4,)),
            dma((4,)),
            dma((2,)),
            dma((2,)),
            dma((n_seq,)),
            dma((n_seq,)),
            dma((4, 11)),
            dma((4, 11)),
            dma((6,)),
            dma((6,)),
            dma((n_seq,)),
            dma((n_seq,)),
        ],
        compiler_params=pltpu.CompilerParams(
            collective_id=2, has_side_effects=True, vmem_limit_bytes=61 * 2**20
        ),
        cost_estimate=pl.CostEstimate(
            flops=10**10, bytes_accessed=5 * 10**7, transcendentals=10**6
        ),
        name="back",
    )(
        grad_h2,
        resid,
        x_row,
        dy_row,
        att,
        qkv,
        probs,
        packed,
        vectors,
        outs,
        outof,
        tokens,
        branch,
        first_grad,
        second_grad,
        biases,
        router_grad,
    )


def to_row(block):
    return lax.all_to_all(block, "seq", split_axis=0, concat_axis=1, tiled=True)[0]


def to_block(row, rows_dev):
    split = row.reshape(rows_dev, row.shape[0] // rows_dev, row.shape[1])
    return lax.all_to_all(split, "seq", split_axis=0, concat_axis=0, tiled=True)


def shards_rows(
    tokens,
    cotangent,
    pad_mask,
    expert_ids,
    priority,
    ln1_gain,
    ln1_shift,
    w_qkv,
    w_out,
    out_bias,
    ln2_gain,
    ln2_shift,
    w_router,
    w_in,
    in_bias,
    w_exp_out,
    exp_out_bias,
):
    both = ("dp", "seq")
    rows_dev, pos_dev = pad_mask.shape
    tok = rows_dev * pos_dev
    experts = w_router.shape[1]
    cap = (21 * tok + 10 * experts - 1) // (10 * experts)
    n_seq = lax.axis_size("seq")
    bf, f32 = jnp.bfloat16, jnp.float32
    vectors = jnp.stack([ln1_gain, ln1_shift, out_bias, ln2_gain, ln2_shift], axis=1)
    pad = jnp.zeros((vectors.shape[0], 128 - 5 - experts), bf)
    packed = lax.all_gather(
        jnp.concatenate([w_qkv, w_out, vectors, w_router, pad], axis=1), both, axis=0, tiled=True
    )
    qkv_weight, out_weight = packed[:, : 3 * D], packed[:, 3 * D : 4 * D]
    vectors = packed[:, 4 * D : 4 * D + 5].T.astype(f32)
    gain_one, shift_one, out_shift, gain_two, shift_two = (vectors[i : i + 1] for i in range(5))
    router = packed[:, 4 * D + 5 : 4 * D + 5 + experts]
    bias_cols = exp_out_bias.shape[1]
    extra = jnp.zeros((16, D), bf).at[0].set(in_bias[0]).at[1, :bias_cols].set(exp_out_bias[0])
    expert_pack = lax.all_gather(
        jnp.concatenate([w_in[0], w_exp_out[0], extra], axis=0), "seq", axis=0
    )
    first, second = expert_pack[:, :D], expert_pack[:, D : 2 * D]
    first_bias = expert_pack[:, 2 * D].astype(f32)
    second_bias = expert_pack[:, 2 * D + 1, :bias_cols].reshape(1, D).astype(f32)
    held = -(-cap // 16) * 16
    picks = expert_ids.reshape(tok, 2)
    kept, slot = slot_ranks(priority.reshape(-1), picks, pad_mask.reshape(-1), experts, cap)
    place = jnp.where(kept, picks * held + slot, experts * held)
    where = jnp.arange(experts * held, dtype=jnp.int32)
    outof = ((place[:, :1] == where[None]) | (place[:, 1:] == where[None])).astype(bf)
    place = place.T
    into = ((place[:1] == where[:, None]) | (place[1:] == where[:, None])).astype(bf)
    dy_slots = mm(into, cotangent.reshape(tok, D), ((1,), (0,)), True).reshape(experts, held, D)
    dy_slots = lax.all_to_all(dy_slots, "dp", split_axis=0, concat_axis=0, tiled=True)
    dy_slots = dy_slots.reshape(-1, D)
    x_low, dy = to_row(tokens), to_row(cotangent)
    x = x_low.astype(f32)
    open_row = lax.all_to_all(
        jnp.broadcast_to(pad_mask[:, None], (rows_dev, 8, pos_dev)), "seq", 0, 2, tiled=True
    )[0, :1]
    normed_one, _ = norm_stats(x)
    h_one = (normed_one * gain_one + shift_one).astype(bf)
    qkv = mm(h_one, qkv_weight, ((1,), (0,)), True)
    q, k, v = (qkv[:, i * D : (i + 1) * D].reshape(-1, HEADS, HEAD) for i in range(3))
    scale = HEAD ** (-0.5)
    scores = jnp.einsum("qhd,khd->hqk", q, k, preferred_element_type=f32) * scale
    scores = jnp.where((open_row > 0)[:, None], scores, -1e30)
    weights = jnp.exp(scores - jnp.max(scores, axis=-1, keepdims=True))
    probs = weights / jnp.sum(weights, axis=-1, keepdims=True)
    probs_low = probs.astype(bf)
    attended = jnp.einsum("hqk,khd->qhd", probs_low, v, preferred_element_type=f32)
    attended = attended.astype(bf).reshape(-1, D)
    branch = mm(attended, out_weight, ((1,), (0,))) + out_shift
    resid = x + branch
    normed_two, _ = norm_stats(resid)
    h_two = (normed_two * gain_two + shift_two).astype(bf)
    h_block = to_block(h_two, rows_dev).reshape(tok, D)
    branch_block = to_block(branch.astype(bf), rows_dev).reshape(tok, D)
    wide_router = jnp.pad(router, ((0, 0), (0, 128 - experts)))
    grad_h2, made, first_grad, second_grad, router_grad, bias_grad = moe(
        h_block, into, outof, dy_slots, first, second, first_bias[:, None], second_bias, wide_router, experts
    )
    out, tokens_grad, dense, small, expert_grads, bias_grad = back(
        lax.axis_size("dp"),
        n_seq,
        grad_h2,
        resid,
        x_low,
        dy,
        attended,
        qkv,
        probs_low,
        packed,
        jnp.pad(vectors, ((0, 3), (0, 0))),
        made,
        outof,
        tokens.reshape(tok, D),
        branch_block,
        first_grad,
        second_grad,
        bias_grad,
        router_grad,
    )
    seq, own = lax.axis_index("seq"), D // (lax.axis_size("dp") * n_seq)
    small = lax.dynamic_slice_in_dim(
        small, (lax.axis_index("dp") * n_seq + seq) * own, own, 1
    )
    qkv_grad = dense[:, D:].reshape(own, 3, 3, 256).swapaxes(1, 2).reshape(own, 3 * D)
    return (
        out.reshape(rows_dev, pos_dev, D),
        tokens_grad.reshape(rows_dev, pos_dev, D),
        small[0],
        small[1],
        qkv_grad,
        dense[:, :D],
        small[2],
        small[3],
        small[4],
        small[8 : 8 + experts].T,
        expert_grads[None, 0],
        bias_grad[None, 0],
        expert_grads[None, 1],
        lax.dynamic_slice_in_dim(bias_grad[None, 8], seq * bias_cols, bias_cols, 1),
    )


def shards(*args):
    block_rows, local_experts, n_dp = args[2].shape[0], args[13].shape[0], lax.axis_size("dp")
    if block_rows == lax.axis_size("seq") and local_experts == 1 and n_dp == 8:
        return shards_rows(*args)
    return shards_general(*args)


def solution(mesh):
    return jax.shard_map(
        shards,
        mesh=mesh,
        in_specs=(
            P("dp", "seq", None),
            P("dp", "seq", None),
            P("dp", "seq"),
            P("dp", "seq", None),
            P("dp", "seq"),
            P(("dp", "seq")),
            P(("dp", "seq")),
            P(("dp", "seq"), None),
            P(("dp", "seq"), None),
            P(("dp", "seq")),
            P(("dp", "seq")),
            P(("dp", "seq")),
            P(("dp", "seq"), None),
            P("dp", None, "seq"),
            P("dp", "seq"),
            P("dp", "seq", None),
            P("dp", "seq"),
        ),
        out_specs=(
            P("dp", "seq", None),
            P("dp", "seq", None),
            P(("dp", "seq")),
            P(("dp", "seq")),
            P(("dp", "seq"), None),
            P(("dp", "seq"), None),
            P(("dp", "seq")),
            P(("dp", "seq")),
            P(("dp", "seq")),
            P(("dp", "seq"), None),
            P("dp", None, "seq"),
            P("dp", "seq"),
            P("dp", "seq", None),
            P("dp", "seq"),
        ),
        check_vma=False,
    )
```

```python
import functools

import jax
import jax.numpy as jnp
from jax import lax
from jax.experimental import pallas as pl
from jax.experimental.pallas import tpu as pltpu
from jax.sharding import PartitionSpec as P

D = 768
HEADS = 12
HEAD = 64


norm_eps = 1e-06


def norm_forward(values, norm_gain, norm_shift):
    average = jnp.mean(values, axis=-1, keepdims=True)
    centred = values - average
    inv_scale = lax.rsqrt(jnp.mean(centred * centred, axis=-1, keepdims=True) + norm_eps)
    normed = centred * inv_scale
    return (
        normed * norm_gain.astype(jnp.float32) + norm_shift.astype(jnp.float32),
        normed,
        inv_scale,
    )


def norm_backward(grad_output, normed, inv_scale, norm_gain):
    scaled = grad_output * norm_gain.astype(jnp.float32)
    grad_input = inv_scale * (
        scaled
        - jnp.mean(scaled, axis=-1, keepdims=True)
        - normed * jnp.mean(scaled * normed, axis=-1, keepdims=True)
    )
    return (
        grad_input,
        jnp.sum(grad_output * normed, axis=(0, 1)),
        jnp.sum(grad_output, axis=(0, 1)),
    )


def gelu_slope(values):
    return (
        0.5 * (1.0 + lax.erf(values * 0.7071067811865476))
        + values * jnp.exp(-0.5 * values * values) * 0.3989422804014327
    )


def slot_ranks(order, picks, valid, experts, capacity):
    count = order.shape[0]
    index = jnp.arange(count, dtype=jnp.int32)
    rank = jnp.sum(jnp.where(order[:, None] == index[None, :], index[:, None], 0), axis=0)
    earlier = (rank[None, :] < rank[:, None]).astype(jnp.bfloat16)
    chosen = picks[:, :, None] == jnp.arange(experts, dtype=jnp.int32)
    counted = chosen.astype(jnp.float32) * valid.astype(jnp.float32)[:, None, None]
    before = jnp.dot(
        earlier,
        counted.reshape(count, 2 * experts).astype(jnp.bfloat16),
        preferred_element_type=jnp.float32,
    ).reshape(count, 2, experts)
    firsts = jnp.sum(counted[:, 0], axis=0)
    before = before + jnp.stack([jnp.zeros_like(firsts), firsts])[None]
    slot = jnp.sum(jnp.where(chosen, before, 0.0), axis=2).astype(jnp.int32)
    kept = (valid[:, None] > 0) & (slot < capacity)
    return kept, slot


def pair_slots(order, expert_picks, valid_flags, expert_count, capacity):
    kept, slot = slot_ranks(order, expert_picks, valid_flags, expert_count, capacity)
    tokens = jnp.arange(order.shape[0], dtype=jnp.int32)
    return (
        jnp.concatenate([tokens, tokens]),
        expert_picks.T.reshape(-1),
        slot.T.reshape(-1),
        kept.T.reshape(-1).astype(jnp.int32),
    )


def shards_general(
    tokens,
    cotangent,
    pad_mask,
    expert_ids,
    priority,
    ln1_gain,
    ln1_shift,
    w_qkv,
    w_out,
    out_bias,
    ln2_gain,
    ln2_shift,
    w_router,
    w_in,
    in_bias,
    w_exp_out,
    exp_out_bias,
):
    rows_dev, pos_dev = pad_mask.shape
    tok_count = rows_dev * pos_dev
    expert_count = w_router.shape[1]
    local_experts = w_in.shape[0]
    capacity = (21 * tok_count + 10 * expert_count - 1) // (10 * expert_count)
    scale_factor = HEAD ** (-0.5)
    gain_one, shift_one, qkv_weight, out_weight, out_shift, gain_two, shift_two, router_weight = (
        lax.all_gather(ln1_gain, ("dp", "seq"), axis=0, tiled=True),
        lax.all_gather(ln1_shift, ("dp", "seq"), axis=0, tiled=True),
        lax.all_gather(w_qkv, ("dp", "seq"), axis=0, tiled=True),
        lax.all_gather(w_out, ("dp", "seq"), axis=0, tiled=True),
        lax.all_gather(out_bias, ("dp", "seq"), axis=0, tiled=True),
        lax.all_gather(ln2_gain, ("dp", "seq"), axis=0, tiled=True),
        lax.all_gather(ln2_shift, ("dp", "seq"), axis=0, tiled=True),
        lax.all_gather(w_router, ("dp", "seq"), axis=0, tiled=True),
    )
    x_float = tokens.astype(jnp.float32)
    h_one, normed_one, inv_one = norm_forward(x_float, gain_one, shift_one)
    h_one_low = h_one.astype(jnp.bfloat16)
    qkv_low = jnp.einsum(
        "rpd,de->rpe", h_one_low, qkv_weight, preferred_element_type=jnp.float32
    ).astype(jnp.bfloat16)
    queries = qkv_low[:, :, :D].reshape(rows_dev, pos_dev, HEADS, HEAD)
    kv_all, mask_all = (
        lax.all_gather(qkv_low[:, :, D:], "seq", axis=1, tiled=True),
        lax.all_gather(pad_mask.astype(jnp.bfloat16), "seq", axis=1, tiled=True),
    )
    full_len = kv_all.shape[1]
    keys_all = kv_all[:, :, :D].reshape(rows_dev, full_len, HEADS, HEAD)
    values_all = kv_all[:, :, D:].reshape(rows_dev, full_len, HEADS, HEAD)
    key_open = (mask_all > 0)[:, None, None, :]

    def score_block():
        raw_scores = (
            jnp.einsum("rphd,rkhd->rhpk", queries, keys_all, preferred_element_type=jnp.float32)
            * scale_factor
        )
        return jnp.where(key_open, raw_scores, -1e30)

    scores = score_block()
    row_max = jnp.max(scores, axis=-1, keepdims=True)
    exp_scores = jnp.exp(scores - row_max)
    row_total = jnp.sum(exp_scores, axis=-1, keepdims=True)
    log_total = row_max + jnp.log(row_total)
    probs_low = (exp_scores / row_total).astype(jnp.bfloat16)
    attended = (
        jnp.einsum("rhpk,rkhd->rphd", probs_low, values_all, preferred_element_type=jnp.float32)
        .reshape(rows_dev, pos_dev, D)
        .astype(jnp.bfloat16)
    )
    branch = jnp.einsum(
        "rpd,de->rpe", attended, out_weight, preferred_element_type=jnp.float32
    ) + out_shift.astype(jnp.float32)
    resid = x_float + branch
    h_two, normed_two, inv_two = norm_forward(resid, gain_two, shift_two)
    flat_low = h_two.astype(jnp.bfloat16).reshape(tok_count, D)
    logits = jnp.dot(flat_low, router_weight, preferred_element_type=jnp.float32)
    router_probs = jax.nn.softmax(logits, axis=-1)
    token_pairs, expert_pairs, slot_index, kept_flags = pair_slots(
        priority.reshape(-1),
        expert_ids.reshape(tok_count, 2),
        pad_mask.reshape(-1),
        expert_count,
        capacity,
    )
    dummy_row = expert_count * capacity
    destination = jnp.where(kept_flags > 0, expert_pairs * capacity + slot_index, dummy_row)
    kept_float = kept_flags.astype(jnp.float32)
    gate_pairs = router_probs[token_pairs, expert_pairs] * kept_float
    send_rows = (
        jnp.zeros((dummy_row + 1, D), jnp.bfloat16)
        .at[destination]
        .set(flat_low[token_pairs])[:-1]
        .reshape(expert_count, capacity, D)
    )
    received = lax.all_to_all(send_rows, "dp", split_axis=0, concat_axis=1, tiled=True)
    seq_index = lax.axis_index("seq")
    bias_cols = exp_out_bias.shape[1]
    rows_all = lax.all_gather(received, "seq", axis=1, tiled=True)
    pre_act = (
        jnp.einsum("erd,edf->erf", rows_all, w_in, preferred_element_type=jnp.float32)
        + in_bias.astype(jnp.float32)[:, None, :]
    )
    act_low = jax.nn.gelu(pre_act, approximate=False).astype(jnp.bfloat16)
    partial_out = jnp.einsum("erf,efd->erd", act_low, w_exp_out, preferred_element_type=jnp.float32)
    bias_full = lax.dynamic_update_slice_in_dim(
        jnp.zeros((local_experts, D), jnp.float32),
        exp_out_bias.astype(jnp.float32),
        seq_index * bias_cols,
        1,
    )
    partial_out = partial_out + bias_full[:, None, :]
    expert_out = lax.psum_scatter(
        partial_out.astype(jnp.bfloat16), "seq", scatter_dimension=1, tiled=True
    )
    returned_buf = lax.all_to_all(expert_out, "dp", split_axis=1, concat_axis=0, tiled=True)
    returned = jnp.concatenate(
        [returned_buf.reshape(-1, D), jnp.zeros((1, D), jnp.bfloat16)], axis=0
    )[destination].astype(jnp.float32)
    mixture = (
        jnp.zeros((tok_count, D), jnp.float32).at[token_pairs].add(gate_pairs[:, None] * returned)
    )
    block_output = (resid + mixture.reshape(rows_dev, pos_dev, D)).astype(jnp.bfloat16)
    grad_y = cotangent.astype(jnp.float32)
    grad_pairs = grad_y.reshape(tok_count, D)[token_pairs]
    grad_gates = jnp.sum(grad_pairs * returned, axis=-1) * kept_float
    grad_ret = (gate_pairs[:, None] * grad_pairs).astype(jnp.bfloat16)
    grad_send = (
        jnp.zeros((dummy_row + 1, D), jnp.bfloat16)
        .at[destination]
        .set(grad_ret)[:-1]
        .reshape(expert_count, capacity, D)
    )
    grad_recv = lax.all_to_all(grad_send, "dp", split_axis=0, concat_axis=1, tiled=True)
    grad_all = lax.all_gather(grad_recv, "seq", axis=1, tiled=True)
    pre_again = (
        jnp.einsum("erd,edf->erf", rows_all, w_in, preferred_element_type=jnp.float32)
        + in_bias.astype(jnp.float32)[:, None, :]
    )
    act_again = jax.nn.gelu(pre_again, approximate=False).astype(jnp.bfloat16)
    grad_act = jnp.einsum("erd,efd->erf", grad_all, w_exp_out, preferred_element_type=jnp.float32)
    grad_pre = (grad_act * gelu_slope(pre_again)).astype(jnp.bfloat16)
    w_exp_out_grad = jnp.einsum(
        "erf,erd->efd", act_again, grad_all, preferred_element_type=jnp.float32
    )
    bias_sums = jnp.sum(grad_all, axis=1, dtype=jnp.float32)
    exp_out_bias_grad = lax.dynamic_slice_in_dim(bias_sums, seq_index * bias_cols, bias_cols, 1)
    w_in_grad = jnp.einsum("erd,erf->edf", rows_all, grad_pre, preferred_element_type=jnp.float32)
    in_bias_grad = jnp.sum(grad_pre, axis=1, dtype=jnp.float32)
    grad_rows_part = jnp.einsum("erf,edf->erd", grad_pre, w_in, preferred_element_type=jnp.float32)
    grad_back = lax.psum_scatter(
        grad_rows_part.astype(jnp.bfloat16), "seq", scatter_dimension=1, tiled=True
    )
    grad_buf = lax.all_to_all(grad_back, "dp", split_axis=1, concat_axis=0, tiled=True)
    grad_rows_back = jnp.concatenate(
        [grad_buf.reshape(-1, D), jnp.zeros((1, D), jnp.bfloat16)], axis=0
    )[destination].astype(jnp.float32)
    grad_h2_experts = jnp.zeros((tok_count, D), jnp.float32).at[token_pairs].add(grad_rows_back)
    grad_probs = (
        jnp.zeros((tok_count, expert_count), jnp.float32)
        .at[token_pairs, expert_pairs]
        .add(grad_gates)
    )
    grad_logits = (
        router_probs * (grad_probs - jnp.sum(router_probs * grad_probs, axis=-1, keepdims=True))
    ).astype(jnp.bfloat16)
    router_grad = jnp.einsum("td,te->de", flat_low, grad_logits, preferred_element_type=jnp.float32)
    grad_h2 = grad_h2_experts + jnp.einsum(
        "te,de->td", grad_logits, router_weight, preferred_element_type=jnp.float32
    )
    grad_resid_norm, gain_two_grad, shift_two_grad = norm_backward(
        grad_h2.reshape(rows_dev, pos_dev, D), normed_two, inv_two, gain_two
    )
    grad_resid = grad_y + grad_resid_norm
    grad_branch = grad_resid.astype(jnp.bfloat16)
    out_weight_grad = jnp.einsum(
        "rpd,rpe->de", attended, grad_branch, preferred_element_type=jnp.float32
    )
    out_shift_grad = jnp.sum(grad_branch, axis=(0, 1), dtype=jnp.float32)
    grad_attended = jnp.einsum(
        "rpe,de->rpd", grad_branch, out_weight, preferred_element_type=jnp.float32
    ).astype(jnp.bfloat16)
    grad_att_heads = grad_attended.reshape(rows_dev, pos_dev, HEADS, HEAD)
    scores_again = score_block()
    probs_again = jnp.exp(scores_again - log_total)
    probs_again_low = probs_again.astype(jnp.bfloat16)
    grad_probs_att = jnp.einsum(
        "rphd,rkhd->rhpk", grad_att_heads, values_all, preferred_element_type=jnp.float32
    )
    row_delta = jnp.sum(probs_again * grad_probs_att, axis=-1, keepdims=True)
    grad_scores = (probs_again * (grad_probs_att - row_delta)).astype(jnp.bfloat16)
    grad_queries = (
        jnp.einsum("rhpk,rkhd->rphd", grad_scores, keys_all, preferred_element_type=jnp.float32)
        * scale_factor
    ).reshape(rows_dev, pos_dev, D)
    grad_keys = (
        jnp.einsum("rhpk,rphd->rkhd", grad_scores, queries, preferred_element_type=jnp.float32)
        * scale_factor
    ).reshape(rows_dev, full_len, D)
    grad_values = jnp.einsum(
        "rhpk,rphd->rkhd", probs_again_low, grad_att_heads, preferred_element_type=jnp.float32
    ).reshape(rows_dev, full_len, D)
    grad_kv = lax.psum_scatter(
        jnp.concatenate([grad_keys, grad_values], axis=-1).astype(jnp.bfloat16),
        "seq",
        scatter_dimension=1,
        tiled=True,
    )
    grad_qkv = jnp.concatenate([grad_queries.astype(jnp.bfloat16), grad_kv], axis=-1)
    qkv_weight_grad = jnp.einsum(
        "rpd,rpe->de", h_one_low, grad_qkv, preferred_element_type=jnp.float32
    )
    grad_h1 = jnp.einsum("rpe,de->rpd", grad_qkv, qkv_weight, preferred_element_type=jnp.float32)
    grad_x_norm, gain_one_grad, shift_one_grad = norm_backward(
        grad_h1, normed_one, inv_one, gain_one
    )
    tokens_grad = (grad_resid + grad_x_norm).astype(jnp.bfloat16)
    dense_parts = (
        lax.psum_scatter(gain_one_grad, ("dp", "seq"), scatter_dimension=0, tiled=True),
        lax.psum_scatter(shift_one_grad, ("dp", "seq"), scatter_dimension=0, tiled=True),
        lax.psum_scatter(qkv_weight_grad, ("dp", "seq"), scatter_dimension=0, tiled=True),
        lax.psum_scatter(out_weight_grad, ("dp", "seq"), scatter_dimension=0, tiled=True),
        lax.psum_scatter(out_shift_grad, ("dp", "seq"), scatter_dimension=0, tiled=True),
        lax.psum_scatter(gain_two_grad, ("dp", "seq"), scatter_dimension=0, tiled=True),
        lax.psum_scatter(shift_two_grad, ("dp", "seq"), scatter_dimension=0, tiled=True),
        lax.psum_scatter(router_grad, ("dp", "seq"), scatter_dimension=0, tiled=True),
    )
    return (
        block_output,
        tokens_grad,
        dense_parts[0],
        dense_parts[1],
        dense_parts[2],
        dense_parts[3],
        dense_parts[4],
        dense_parts[5],
        dense_parts[6],
        dense_parts[7],
        w_in_grad,
        in_bias_grad,
        w_exp_out_grad,
        exp_out_bias_grad,
    )


MESH = pl.DeviceIdType.MESH
VMEM = pl.BlockSpec(memory_space=pltpu.VMEM)
ANY = pl.BlockSpec(memory_space=pl.ANY)
ERF = (0.1274147955, -0.142248368, 0.7107068705, -0.7265760135, 0.5307027145)


def nn(a, b):
    return lax.dot_general(a, b, (((1,), (0,)), ((), ())), preferred_element_type=jnp.float32)


def nt(a, b):
    return lax.dot_general(a, b, (((1,), (1,)), ((), ())), preferred_element_type=jnp.float32)


def tn(a, b):
    return lax.dot_general(a, b, (((0,), (0,)), ((), ())), preferred_element_type=jnp.float32)


def gelu_parts(v):
    bell = jnp.exp(v * v * -0.5)
    t = 1.0 / (jnp.abs(v) * (0.3275911 * 0.7071067811865476) + 1.0)
    a, b, c, d, e = ERF
    tail = ((((e * t + d) * t + c) * t + b) * t + a) * t * bell
    cdf = jnp.where(v < 0.0, tail, 1.0 - tail)
    return v * cdf, cdf + v * (bell * 0.3989422804014327)


def other(me, step):
    bit = lambda k: lax.rem(me // k + step // k, 2) * k
    return bit(4) + bit(2) + bit(1)


def moe_kernel(
    experts,
    h_ref,
    into_ref,
    from_ref,
    dy_ref,
    first_any,
    second_any,
    bias_ref,
    router_ref,
    dy_any,
    branch_any,
    grad_ref,
    outs_ref,
    first_grad_ref,
    second_grad_ref,
    router_grad_ref,
    bias_grad_ref,
    dy_row_any,
    branch_block_any,
    sent,
    rows,
    rows_t,
    go,
    act,
    gp,
    back_sent,
    back,
    logit_grad,
    first,
    second,
    w_sem,
    send_sem,
    recv_sem,
    send_sem2,
    recv_sem2,
    send_sem3,
    recv_sem3,
    own_sem,
):
    n = experts
    cap = dy_ref.shape[0] // n
    bf, f32 = jnp.bfloat16, jnp.float32
    blocks = first.shape[0]
    me, seq = lax.axis_index("dp"), lax.axis_index("seq")
    n_seq = blocks
    pos = h_ref.shape[0] // n_seq
    load1 = pltpu.make_async_copy(first_any, first, w_sem.at[0])
    load2 = pltpu.make_async_copy(second_any, second, w_sem.at[1])
    load1.start()
    load2.start()
    at = lambda i: pl.ds(pl.multiple_of(i * cap, cap), cap)
    greet(n, n_seq)

    def dispatch(step, source, target, sems):
        to = other(me, step)
        return pltpu.make_async_remote_copy(
            source.at[at(to)],
            target.at[at(me)],
            sems[0].at[step],
            sems[1].at[step],
            device_id=(to, seq),
            device_id_type=MESH,
        )

    out_sems, back_sems = (send_sem, recv_sem), (send_sem2, recv_sem2)

    @pl.loop(0, n - 1)
    def _(i):
        step = n - 1 - i
        to = other(me, step)
        sent[at(to), :] = nn(into_ref[at(to), :], h_ref[...]).astype(bf)
        dispatch(step, sent, rows, out_sems).start()

    rows[at(me), :] = nn(into_ref[at(me), :], h_ref[...]).astype(bf)
    swaps, own_swaps = [], []
    for k, (source, target) in enumerate(((dy_any, dy_row_any), (branch_any, branch_block_any))):
        here = rows_of(seq, pos)
        own_swaps.append(pltpu.make_async_copy(source.at[here], target.at[here], own_sem.at[k]))
        for step in range(1, n_seq):
            to = lax.rem(seq + step, n_seq)
            swaps.append(
                remote(
                    source.at[rows_of(to, pos)],
                    target.at[here],
                    send_sem3.at[k, step],
                    recv_sem3.at[k, step],
                    (me, to),
                )
            )
    for copy in swaps + own_swaps:
        copy.start()
    load1.wait()
    load2.wait()
    lane = lax.broadcasted_iota(jnp.int32, (cap, 128), 1)

    @pl.loop(0, n)
    def _(step):
        peer = other(me, step)

        @pl.when(step > 0)
        def _():
            dispatch(step, sent, rows, out_sems).wait_recv()

        x = rows[at(peer), :]
        dy = dy_ref[at(peer), :].astype(f32)
        logits = jnp.where(lane < n, nn(x, router_ref[...]), -1e30)
        probs = jnp.exp(logits - jnp.max(logits, axis=-1, keepdims=True))
        probs = probs / jnp.sum(probs, axis=-1, keepdims=True)
        mine = (lane == me).astype(f32)
        gate = jnp.sum(probs * mine, axis=-1, keepdims=True)
        grad_out = (gate * dy).astype(bf)
        go[at(peer), :] = grad_out

        def block(q, sums):
            out, grad_row = sums
            value, slope = gelu_parts(nn(x, first[q]) + bias_ref[q, 0:1])
            value = value.astype(bf)
            act[q, at(peer), :] = value
            grad_pre = (nt(grad_out, second[q]) * slope).astype(bf)
            gp[q, at(peer), :] = grad_pre
            return out + nn(value, second[q]), grad_row + nt(grad_pre, first[q])

        zero = jnp.zeros((cap, x.shape[1]), f32)
        out, grad_row = lax.fori_loop(0, blocks, block, (zero, zero))
        made = (out + jnp.sum(bias_ref[:, 1, :], axis=0, keepdims=True)).astype(bf).astype(f32)
        grad_gate = jnp.sum(dy * made, axis=-1, keepdims=True)
        grad_logits = (grad_gate * gate * (mine - probs)).astype(bf)
        logit_grad[at(peer), :] = grad_logits
        grad_row = (grad_row + nt(grad_logits, router_ref[...])).astype(bf)
        outs_ref[at(peer), :] = (gate * made).astype(bf)

        @pl.when(step > 0)
        def _():
            back_sent[at(peer), :] = grad_row
            dispatch(step, back_sent, back, back_sems).start()

        @pl.when(step == 0)
        def _():
            back[at(peer), :] = grad_row

    rows_t[...] = rows[...].T
    ones = jnp.ones((8, rows.shape[0]), bf)

    @pl.loop(0, blocks)
    def _(q):
        first_grad_ref[q] = nn(rows_t[...], gp[q]).astype(bf)
        second_grad_ref[q] = tn(act[q], go[...]).astype(bf)
        bias_grad_ref[q, :8] = nn(ones, gp[q])
        bias_grad_ref[q, 8:] = nn(ones, go[...])

    router_grad_ref[...] = tn(logit_grad[...], rows[...])[: router_grad_ref.shape[0]]

    @pl.loop(1, n)
    def _(step):
        dispatch(step, back_sent, back, back_sems).wait()
        dispatch(step, sent, rows, out_sems).wait_send()

    grad_ref[...] = nn(from_ref[...], back[...]).astype(bf)
    for copy in swaps + own_swaps:
        copy.wait()


def moe(h_block, into, outof, dy_slots, first, second, bias, router, dy, branch, experts):
    bf, f32 = jnp.bfloat16, jnp.float32
    tok, width = h_block.shape
    slots = into.shape[0]
    blocks, hidden = first.shape[0], first.shape[2]
    sds = jax.ShapeDtypeStruct
    dma = pltpu.SemaphoreType.DMA
    big = (slots, width)
    return pl.pallas_call(
        functools.partial(moe_kernel, experts),
        out_shape=(
            sds((tok, width), bf),
            sds(big, bf),
            sds(first.shape, bf),
            sds(second.shape, bf),
            sds((8, width), f32),
            sds((blocks, 16, hidden), f32),
            sds((tok, width), bf),
            sds((tok, width), bf),
        ),
        in_specs=[VMEM] * 4 + [ANY] * 2 + [VMEM] * 2 + [ANY] * 2,
        out_specs=(VMEM,) * 6 + (ANY,) * 2,
        scratch_shapes=[
            pltpu.VMEM(big, bf),
            pltpu.VMEM(big, bf),
            pltpu.VMEM((width, slots), bf),
            pltpu.VMEM(big, bf),
            pltpu.VMEM((blocks, slots, hidden), bf),
            pltpu.VMEM((blocks, slots, hidden), bf),
            pltpu.VMEM(big, bf),
            pltpu.VMEM(big, bf),
            pltpu.VMEM((slots, 128), bf),
            pltpu.VMEM(first.shape, bf),
            pltpu.VMEM(second.shape, bf),
            dma((2,)),
            dma((experts,)),
            dma((experts,)),
            dma((experts,)),
            dma((experts,)),
            dma((2, blocks)),
            dma((2, blocks)),
            dma((2,)),
        ],
        compiler_params=pltpu.CompilerParams(
            collective_id=1, has_side_effects=True, vmem_limit_bytes=61 * 2**20
        ),
        cost_estimate=pl.CostEstimate(
            flops=12 * slots * width * hidden * blocks, bytes_accessed=4 * 10**7, transcendentals=slots * hidden * blocks
        ),
        name="moe",
    )(h_block, into, outof, dy_slots, first, second, bias, router, dy, branch)


def norm_stats(values):
    average = jnp.mean(values, axis=-1, keepdims=True)
    centred = values - average
    inv = lax.rsqrt(jnp.mean(centred * centred, axis=-1, keepdims=True) + norm_eps)
    return centred * inv, inv


def norm_grad(grad_output, normed, inv, gain):
    scaled = grad_output * gain
    return inv * (
        scaled
        - jnp.mean(scaled, axis=-1, keepdims=True)
        - normed * jnp.mean(scaled * normed, axis=-1, keepdims=True)
    )


def rows_of(i, size):
    return pl.ds(pl.multiple_of(i * size, size), size)


def split_axes():
    dp, seq = lax.axis_index("dp"), lax.axis_index("seq")
    return dp // 2, lax.rem(dp, 2), seq // 2, lax.rem(seq, 2)


def greet(n_dp, n_seq):
    dp, seq = lax.axis_index("dp"), lax.axis_index("seq")
    barrier = pltpu.get_barrier_semaphore()
    for step in range(1, n_dp):
        pl.semaphore_signal(
            barrier, inc=1, device_id=(other(dp, step), seq), device_id_type=MESH
        )
    for step in range(1, n_seq):
        pl.semaphore_signal(
            barrier, inc=1, device_id=(dp, lax.rem(seq + step, n_seq)), device_id_type=MESH
        )
    pl.semaphore_wait(barrier, n_dp - 1 + n_seq - 1)


def remote(source, target, send, recv, device):
    return pltpu.make_async_remote_copy(
        source, target, send, recv, device_id=device, device_id_type=MESH
    )


def back_kernel(
    n_dp,
    n_seq,
    grad_any,
    resid_any,
    x_any,
    dy_any,
    att_any,
    qkv_any,
    probs_any,
    packed_any,
    vectors_ref,
    outs_any,
    outof_any,
    tokens_any,
    branch_any,
    first_any,
    second_any,
    bias_ref,
    router_grad_ref,
    block_out_ref,
    tokens_grad_ref,
    dense_ref,
    small_ref,
    expert_ref,
    bias_out_ref,
    grad_rows,
    resid,
    x_row,
    dy_row,
    att,
    qkv,
    probs,
    w_qkv,
    w_out,
    outs,
    outof,
    tokens,
    branch,
    own_e,
    recv_e,
    recv_x,
    recv_b,
    grad_resid,
    grad_att,
    grad_qkv,
    h_one,
    grad_x,
    part,
    recv_c,
    recv_1,
    recv_2,
    recv_3,
    sums,
    recv_s,
    load_sem,
    probs_sem,
    own_sem,
    gs_sem,
    gr_sem,
    os_sem,
    or_sem,
    es_sem,
    er_sem,
    xs_sem,
    xr_sem,
    bs_sem,
    br_sem,
    ps_sem,
    pr_sem,
    ss_sem,
    sr_sem,
    ts_sem,
    tr_sem,
):
    bf, f32 = jnp.bfloat16, jnp.float32
    dp, seq = lax.axis_index("dp"), lax.axis_index("seq")
    z, y, x, c = split_axes()
    pos = grad_rows.shape[0] // n_seq
    cap = outs.shape[0] // n_dp
    core_peer, x_peer = (dp, x * 2 + 1 - c), (dp, (1 - x) * 2 + c)
    y_peer = (z * 2 + 1 - y, seq)
    z_peer = lambda step: (lax.rem(z + step, 4) * 2 + y, seq)
    loads = [
        pltpu.make_async_copy(a, b, load_sem.at[i])
        for i, (a, b) in enumerate(
            (
                (resid_any, resid),
                (dy_any, dy_row),
                (att_any, att),
                (packed_any.at[:, 3 * D : 4 * D], w_out),
                (qkv_any, qkv),
                (x_any, x_row),
                (packed_any.at[:, : 3 * D], w_qkv),
                (outof_any, outof),
                (tokens_any, tokens),
                (branch_any, branch),
            )
        )
    ]
    fetch = lambda head: pltpu.make_async_copy(
        probs_any.at[head], probs.at[head % 2], probs_sem.at[head % 2]
    )
    for load in loads[:4]:
        load.start()
    greet(n_dp, n_seq)
    to_rows = []
    for step in range(1, n_seq):
        to = lax.rem(seq + step, n_seq)
        to_rows.append(
            remote(
                grad_any.at[rows_of(to, pos)],
                grad_rows.at[rows_of(seq, pos)],
                gs_sem.at[step],
                gr_sem.at[step],
                (dp, to),
            )
        )
    for copy in to_rows:
        copy.start()
    own_rows = pltpu.make_async_copy(
        grad_any.at[rows_of(seq, pos)], grad_rows.at[rows_of(seq, pos)], own_sem.at[0]
    )
    own_rows.start()
    experts_c, experts_own = [], []
    for i, side in enumerate((1 - x, x)):
        for j, ref in enumerate((first_any, second_any)):
            k = i * 2 + j
            experts_c.append(
                remote(
                    ref.at[side * 2 + 1 - c],
                    recv_e.at[i, j],
                    es_sem.at[k],
                    er_sem.at[k],
                    core_peer,
                )
            )
            experts_own.append(
                pltpu.make_async_copy(ref.at[side * 2 + c], own_e.at[i, j], own_sem.at[1 + k])
            )
    for copy in experts_c + experts_own:
        copy.start()
    returns = []
    for step in range(n_dp - 1, 0, -1):
        to = other(dp, step)
        returns.append(
            remote(
                outs_any.at[rows_of(to, cap)],
                outs.at[rows_of(dp, cap)],
                os_sem.at[step],
                or_sem.at[step],
                (to, seq),
            )
        )
    for copy in returns:
        copy.start()
    own_outs = pltpu.make_async_copy(
        outs_any.at[rows_of(dp, cap)], outs.at[rows_of(dp, cap)], own_sem.at[5]
    )
    own_outs.start()
    biases = []
    for step in range(1, n_seq):
        to = lax.rem(seq + step, n_seq)
        biases.append(
            remote(bias_ref.at[to], recv_b.at[step], bs_sem.at[step], br_sem.at[step], (dp, to))
        )
    for copy in biases:
        copy.start()
    for load in loads[4:]:
        load.start()
    fetch(0).start()
    fetch(1).start()
    vec = lambda i: vectors_ref[i : i + 1, :]
    row_sum = lambda v: jnp.sum(v, axis=0, keepdims=True)

    def norm_back(grad_output, values, gain):
        normed, inv = norm_stats(values)
        sums_of = (row_sum(grad_output * normed), row_sum(grad_output))
        return norm_grad(grad_output, normed, inv, gain), *sums_of

    def piece_fill(i, value):
        half = value.shape[1] // 2
        for owner in range(n_dp * n_seq):
            oz, oy, ox, oc = owner // 8, owner // 4 % 2, owner // 2 % 2, owner % 2
            block = value[24 * owner : 24 * owner + 24].astype(bf)
            part[i, oc, 0, ox, oy, oz] = block[:, :half]
            part[i, oc, 1, oy, ox, oz] = block[:, half:]

    first_axis = ((x, x_peer), (y, y_peer))

    def piece_copies(i, stage):
        sems = lambda k: (ps_sem.at[i, k], pr_sem.at[i, k])
        if stage == 0:
            return [remote(part.at[i, 1 - c], recv_c.at[i], *sems(0), core_peer)]
        made = []
        for h in range(2):
            (f, f_peer), (g, g_peer) = first_axis[h], first_axis[1 - h]
            if stage == 1:
                made.append(
                    remote(part.at[i, c, h, 1 - f], recv_1.at[i, h], *sems(1 + h), f_peer)
                )
            elif stage == 2:
                made.append(
                    remote(part.at[i, c, h, f, 1 - g], recv_2.at[i, h], *sems(3 + h), g_peer)
                )
            else:
                for step in range(1, 4):
                    made.append(
                        remote(
                            part.at[i, c, h, f, g, lax.rem(z + step, 4)],
                            recv_3.at[i, h, step],
                            *sems(4 + h * 3 + step),
                            z_peer(step),
                        )
                    )
        return made

    def add(a, b):
        return (a.astype(f32) + b.astype(f32)).astype(bf)

    def piece_advance(i, stage):
        for copy in piece_copies(i, stage - 1):
            copy.wait_recv()
        if stage == 1:
            part[i, c] = add(part[i, c], recv_c[i])
        for h in range(2):
            f, g = first_axis[h][0], first_axis[1 - h][0]
            if stage == 2:
                part[i, c, h, f] = add(part[i, c, h, f], recv_1[i, h])
            elif stage == 3:
                part[i, c, h, f, g] = add(part[i, c, h, f, g], recv_2[i, h])
            elif stage == 4:
                total = part[i, c, h, f, g, z].astype(f32)
                for step in range(1, 4):
                    total = total + recv_3[i, h, step].astype(f32)
                half = total.shape[1]
                dense_ref[:, (2 * i + h) * half : (2 * i + h + 1) * half] = total
        if stage < 4:
            for copy in piece_copies(i, stage):
                copy.start()

    def small_copies(stage):
        peers = ([core_peer], [x_peer], [y_peer], [z_peer(1), z_peer(2), z_peer(3)])[stage]
        return [
            remote(
                sums.at[stage],
                recv_s.at[stage + k],
                ss_sem.at[stage + k],
                sr_sem.at[stage + k],
                peer,
            )
            for k, peer in enumerate(peers)
        ]

    def small_advance(stage):
        for copy in small_copies(stage - 1):
            copy.wait_recv()
        if stage < 4:
            sums[stage] = sums[stage - 1] + recv_s[stage - 1]
            for copy in small_copies(stage):
                copy.start()
        else:
            small_ref[...] = sums[3] + recv_s[3] + recv_s[4] + recv_s[5]

    own_e_copies = experts_own

    def experts_send_x():
        for j in range(2):
            experts_c[j].wait_recv()
            own_e_copies[j].wait()
            own_e[0, j] = add(own_e[0, j], recv_e[0, j])
            experts_x[j].start()

    experts_x = [
        remote(own_e.at[0, j], recv_x.at[j], xs_sem.at[j], xr_sem.at[j], x_peer) for j in range(2)
    ]

    def experts_end():
        for j in range(2):
            experts_c[2 + j].wait_recv()
            own_e_copies[2 + j].wait()
            experts_x[j].wait_recv()

            @pl.loop(0, 6)
            def _(k):
                at = rows_of(k, recv_x.shape[1] // 6)
                expert_ref[j, at, :] = (
                    own_e[1, j, at, :].astype(f32)
                    + recv_e[1, j, at, :].astype(f32)
                    + recv_x[j, at, :].astype(f32)
                )

        bias = bias_ref[seq]
        for step in range(1, n_seq):
            biases[step - 1].wait_recv()
            bias = bias + recv_b[step]
        bias_out_ref[...] = bias

    for load in loads[:3]:
        load.wait()
    own_rows.wait()
    for copy in to_rows:
        copy.wait_recv()
    grad_in, gain_two, shift_two = norm_back(grad_rows[...].astype(f32), resid[...], vec(3))
    grad_resid[...] = dy_row[...].astype(f32) + grad_in
    grad_branch = grad_resid[...].astype(bf)
    out_shift = row_sum(grad_branch.astype(f32))
    loads[3].wait()
    grad_att[...] = nt(grad_branch, w_out[...]).astype(bf)
    piece_fill(0, tn(att[...], grad_branch))
    for copy in piece_copies(0, 0):
        copy.start()
    loads[4].wait()
    loads[5].wait()
    x_normed, _ = norm_stats(x_row[...].astype(f32))
    h_one[...] = (x_normed * vec(0) + vec(1)).astype(bf)
    experts_send_x()
    lane = lax.broadcasted_iota(jnp.int32, (1, 128), 1) // HEAD
    scale = HEAD ** (-0.5)
    for pair in range(HEADS // 2):
        cols = slice(128 * pair, 128 * pair + 128)
        q, k, v = (qkv[:, D * i + 128 * pair : D * i + 128 * pair + 128] for i in range(3))
        go = grad_att[:, cols]
        both = go.astype(f32) * att[:, cols].astype(f32)
        grads = [jnp.zeros(q.shape, f32)] * 3
        for h in range(2):
            head = 2 * pair + h
            keep = (lane == h).astype(bf)
            fetch(head).wait()
            p = probs[head % 2]
            go_h = go * keep
            delta = jnp.sum(both * keep.astype(f32), axis=-1, keepdims=True)
            ds = (p.astype(f32) * (nt(go_h, v) - delta)).astype(bf)
            grads = [
                grads[0] + nn(ds, k * keep),
                grads[1] + tn(ds, q * keep),
                grads[2] + tn(p, go_h),
            ]
            if head + 2 < HEADS:
                fetch(head + 2).start()
        for i, factor in enumerate((scale, scale, 1.0)):
            at = (2 * 128) * (3 * (pair // 2) + i) + 128 * (pair % 2)
            grad_qkv[:, at : at + 128] = (grads[i] * factor).astype(bf)
        if pair < 4:
            piece_advance(0, pair + 1)
        if pair in (2, 3, 4, 5):
            piece_advance(1, pair - 1)
        if pair in (4, 5):
            piece_advance(2, pair - 3)
        if pair % 2 == 1:
            i = pair // 2 + 1
            piece_fill(i, tn(h_one[...], grad_qkv[:, D * (i - 1) : D * i]))
            for copy in piece_copies(i, 0):
                copy.start()
    loads[6].wait()
    grad_h1 = jnp.zeros(resid.shape, f32)
    for i in range(9):
        at = 256 * i
        col = D * (i % 3) + 256 * (i // 3)
        grad_h1 = grad_h1 + nt(grad_qkv[:, at : at + 256], w_qkv[:, col : col + 256])
    grad_in, gain_one, shift_one = norm_back(grad_h1, x_row[...].astype(f32), vec(0))
    sums[0] = jnp.concatenate(
        [gain_one, shift_one, out_shift, gain_two, shift_two, jnp.zeros((3, D), f32), router_grad_ref[...]], axis=0
    )
    for copy in small_copies(0):
        copy.start()
    grad_x[...] = (grad_resid[...] + grad_in).astype(bf)
    to_blocks = []
    for step in range(1, n_seq):
        to = lax.rem(seq + step, n_seq)
        to_blocks.append(
            remote(
                grad_x.at[rows_of(to, pos)],
                tokens_grad_ref.at[rows_of(seq, pos)],
                ts_sem.at[step],
                tr_sem.at[step],
                (dp, to),
            )
        )
    for copy in to_blocks:
        copy.start()
    tokens_grad_ref[rows_of(seq, pos), :] = grad_x[rows_of(seq, pos), :]
    piece_advance(3, 1)
    piece_advance(2, 3)
    small_advance(1)
    own_outs.wait()
    for copy in returns:
        copy.wait_recv()
    for load in loads[7:]:
        load.wait()
    block_out_ref[...] = (
        tokens[...].astype(f32) + branch[...].astype(f32) + nn(outof[...], outs[...])
    ).astype(bf)
    piece_advance(3, 2)
    small_advance(2)
    piece_advance(2, 4)
    experts_end()
    piece_advance(3, 3)
    small_advance(3)
    piece_advance(3, 4)
    small_advance(4)
    for copy in to_blocks:
        copy.wait_recv()
    for copy in to_rows + experts_c + returns + biases + experts_x + to_blocks:
        copy.wait_send()
    for stage in range(4):
        for i in range(4):
            for copy in piece_copies(i, stage):
                copy.wait_send()
        for copy in small_copies(stage):
            copy.wait_send()


def back(
    n_dp,
    n_seq,
    grad_h2,
    resid,
    x_row,
    dy_row,
    att,
    qkv,
    probs,
    packed,
    vectors,
    outs,
    outof,
    tokens,
    branch,
    first_grad,
    second_grad,
    biases,
    router_grad,
):
    bf, f32 = jnp.bfloat16, jnp.float32
    sds, dma, vmem = jax.ShapeDtypeStruct, pltpu.SemaphoreType.DMA, pltpu.VMEM
    tok, slots = outof.shape
    pos = tok // n_seq
    half = D // 2
    return pl.pallas_call(
        functools.partial(back_kernel, n_dp, n_seq),
        out_shape=(
            sds((tok, D), bf),
            sds((tok, D), bf),
            sds((D // (n_dp * n_seq), 4 * D), f32),
            sds((16, D), f32),
            sds((2,) + first_grad.shape[1:], f32),
            sds(biases.shape[1:], f32),
        ),
        in_specs=[ANY] * 8 + [VMEM] + [ANY] * 6 + [VMEM] * 2,
        out_specs=(VMEM,) * 6,
        scratch_shapes=[
            vmem((tok, D), bf),
            vmem((tok, D), f32),
            vmem((tok, D), bf),
            vmem((tok, D), bf),
            vmem((tok, D), bf),
            vmem((tok, 3 * D), bf),
            vmem((2,) + probs.shape[1:], bf),
            vmem((D, 3 * D), bf),
            vmem((D, D), bf),
            vmem((slots, D), bf),
            vmem((tok, slots), bf),
            vmem((tok, D), bf),
            vmem((tok, D), bf),
            vmem((2, 2, D, D), bf),
            vmem((2, 2, D, D), bf),
            vmem((2, D, D), bf),
            vmem((n_seq,) + biases.shape[1:], f32),
            vmem((tok, D), f32),
            vmem((tok, D), bf),
            vmem((tok, 3 * D), bf),
            vmem((tok, D), bf),
            vmem((tok, D), bf),
            vmem((4, 2, 2, 2, 2, 4, 24, half), bf),
            vmem((4, 2, 2, 2, 4, 24, half), bf),
            vmem((4, 2, 2, 4, 24, half), bf),
            vmem((4, 2, 4, 24, half), bf),
            vmem((4, 2, 4, 24, half), bf),
            vmem((4, 16, D), f32),
            vmem((6, 16, D), f32),
            dma((10,)),
            dma((2,)),
            dma((6,)),
            dma((n_seq,)),
            dma((n_seq,)),
            dma((n_dp,)),
            dma((n_dp,)),
            dma((4,)),
            dma((4,)),
            dma((2,)),
            dma((2,)),
            dma((n_seq,)),
            dma((n_seq,)),
            dma((4, 11)),
            dma((4, 11)),
            dma((6,)),
            dma((6,)),
            dma((n_seq,)),
            dma((n_seq,)),
        ],
        compiler_params=pltpu.CompilerParams(
            collective_id=2, has_side_effects=True, vmem_limit_bytes=61 * 2**20
        ),
        cost_estimate=pl.CostEstimate(
            flops=10**10, bytes_accessed=5 * 10**7, transcendentals=10**6
        ),
        name="back",
    )(
        grad_h2,
        resid,
        x_row,
        dy_row,
        att,
        qkv,
        probs,
        packed,
        vectors,
        outs,
        outof,
        tokens,
        branch,
        first_grad,
        second_grad,
        biases,
        router_grad,
    )


def front_kernel(
    n_dp,
    n_seq,
    cap,
    tokens_any,
    dy_any,
    w_qkv_any,
    w_out_any,
    narrow_any,
    first_any,
    second_any,
    cols_ref,
    order_ref,
    bias_ref,
    h_block_any,
    resid_any,
    x_any,
    att_any,
    qkv_any,
    probs_any,
    packed_any,
    vectors_ref,
    router_ref,
    branch_any,
    into_any,
    outof_any,
    dy_slots_any,
    first_all,
    second_all,
    bias_all,
    wide_a,
    wide_b,
    packed,
    x_row,
    dy,
    mask_out,
    mask_in,
    qkv,
    att,
    probs,
    resid,
    branch,
    h_two,
    into,
    outof,
    dy_sent,
    load_sem,
    store_sem,
    probs_sem,
    own_sem,
    gs_sem,
    gr_sem,
    xs_sem,
    xr_sem,
    ms_sem,
    mr_sem,
    ds_sem,
    dr_sem,
    es_sem,
    er_sem,
    bs_sem,
    br_sem,
    hs_sem,
    hr_sem,
):
    bf, f32, i32 = jnp.bfloat16, jnp.float32, jnp.int32
    dp, seq = lax.axis_index("dp"), lax.axis_index("seq")
    z, y, x, c = split_axes()
    tok = x_row.shape[0]
    pos, held, slots = tok // n_seq, into.shape[0] // n_dp, into.shape[0]
    core_peer, x_peer = (dp, x * 2 + 1 - c), (dp, (1 - x) * 2 + c)
    y_peer = (z * 2 + 1 - y, seq)
    z_peer = lambda step: (lax.rem(z + step, 4) * 2 + y, seq)
    wide = (wide_a, wide_b)
    axes = (((x, x_peer), (y, y_peer)), ((y, y_peer), (x, x_peer)))
    mine = [wide[h].at[c, axes[h][0][0], axes[h][1][0], z] for h in range(2)]
    shard = [
        pltpu.make_async_copy(a, b, load_sem.at[i])
        for i, (a, b) in enumerate(
            (
                (narrow_any, mine[0].at[:, :128]),
                (w_qkv_any.at[:, : 2 * D], mine[0].at[:, 128:]),
                (w_qkv_any.at[:, 2 * D :], mine[1].at[:, :D]),
                (w_out_any, mine[1].at[:, D:]),
                (dy_any, dy),
                (tokens_any.at[rows_of(seq, pos)], x_row.at[rows_of(seq, pos)]),
            )
        )
    ]
    for copy in shard:
        copy.start()
    mask_out[...] = jnp.broadcast_to(cols_ref[:, 3:4].astype(f32), mask_out.shape).astype(bf)
    for copy in shard[:4]:
        copy.wait()
    greet(n_dp, n_seq)
    seq_peers = [(step, lax.rem(seq + step, n_seq)) for step in range(1, n_seq)]

    def gather(h, stage):
        (f, f_peer), (g, g_peer) = axes[h]
        sems = lambda k: (gs_sem.at[h, k], gr_sem.at[h, k])
        same = lambda ref, k, peer: remote(ref, ref, *sems(k), peer)
        if stage == 0:
            return [same(mine[h], step, z_peer(step)) for step in range(1, 4)]
        if stage == 1:
            return [same(wide[h].at[c, f, g], 4, g_peer)]
        return [same(wide[h].at[c, f], 5, f_peer)]

    def hand_over(h, stage):
        (f, _), (g, _) = axes[h]
        ref = (wide[h].at[c, f, g], wide[h].at[c, f, 1 - g], wide[h].at[c, 1 - f])[stage]
        return remote(ref, ref, gs_sem.at[h, 6 + stage], gr_sem.at[h, 6 + stage], core_peer)

    def gather_take(stage):
        for h in range(2):
            for copy in gather(h, stage):
                copy.wait_recv()
            if stage < 2:
                gather(h, stage + 1)[0].start()
            hand_over(h, stage).start()

    for h in range(2):
        for copy in gather(h, 0):
            copy.start()
    exchange = []
    for step, to in seq_peers:
        for source, target, sems in (
            (tokens_any, x_row, (xs_sem, xr_sem)),
            (mask_out, mask_in, (ms_sem, mr_sem)),
        ):
            exchange.append(
                remote(
                    source.at[rows_of(to, pos)],
                    target.at[rows_of(seq, pos)],
                    sems[0].at[step],
                    sems[1].at[step],
                    (dp, to),
                )
            )
    for copy in exchange:
        copy.start()
    mask_in[rows_of(seq, pos), :] = mask_out[rows_of(seq, pos), :]
    biases = [
        remote(bias_ref, bias_all.at[seq], bs_sem.at[step], br_sem.at[step], (dp, to))
        for step, to in seq_peers
    ]
    for copy in biases:
        copy.start()
    bias_all[seq] = bias_ref[...]
    down = lax.broadcasted_iota(i32, (tok, tok), 0)
    across = lax.broadcasted_iota(i32, (tok, tok), 1)
    rank_row = jnp.sum(jnp.where(cols_ref[:, 0:1] == across, down.astype(f32), 0.0), axis=0, keepdims=True)
    rank_col = jnp.sum(jnp.where(order_ref[...] == down, across.astype(f32), 0.0), axis=1, keepdims=True)
    earlier = (rank_row < rank_col).astype(bf)
    lane = lax.broadcasted_iota(i32, (tok, 128), 1)
    ids = (cols_ref[:, 1:2], cols_ref[:, 2:3])
    valid = cols_ref[:, 3:4].astype(f32)
    chosen = (lane == ids[0], lane == ids[1] + n_dp)
    counted = jnp.where(chosen[0] | chosen[1], 1.0, 0.0) * valid
    before = nn(earlier, counted.astype(bf))
    firsts = jnp.sum(jnp.where(lane == ids[0] + n_dp, 1.0, 0.0) * valid, axis=0, keepdims=True)
    spot = lax.broadcasted_iota(i32, (tok, slots), 1).astype(f32)
    spot_down = lax.broadcasted_iota(i32, (slots, tok), 0).astype(f32)
    hits, hits_down = [], []
    for k in range(2):
        slot = jnp.sum(jnp.where(chosen[k], before + firsts * k, 0.0), axis=1, keepdims=True)
        place = ids[k].astype(f32) * held + slot
        place = jnp.where((slot < cap) & (valid > 0.0), place, 1.0 * slots)
        place_row = jnp.broadcast_to(place, (tok, 128)).T[:1]
        hits.append(place == spot)
        hits_down.append(place_row == spot_down)
    outof[...] = jnp.where(hits[0] | hits[1], 1.0, 0.0).astype(bf)
    into[...] = jnp.where(hits_down[0] | hits_down[1], 1.0, 0.0).astype(bf)
    stores = [
        pltpu.make_async_copy(a, b, store_sem.at[i])
        for i, (a, b) in enumerate(
            (
                (into, into_any),
                (outof, outof_any),
                (x_row, x_any),
                (packed, packed_any),
                (qkv, qkv_any),
                (att, att_any),
                (branch, branch_any),
                (resid, resid_any),
            )
        )
    ]
    stores[0].start()
    stores[1].start()
    gather_take(0)
    shard[4].wait()
    dy_sent[...] = nn(into[...], dy[...]).astype(bf)
    gather_take(1)
    shard[5].wait()
    for copy in exchange:
        copy.wait_recv()
    normed, _ = norm_stats(x_row[...].astype(f32))
    stores[2].start()
    gather_take(2)
    own_w, experts_x, experts_c, experts_f = [], [], [], []
    for j, (source, target) in enumerate(((first_any, first_all), (second_any, second_all))):
        far = (1 - x) * 2 + c
        sems = lambda k: (es_sem.at[j, k], er_sem.at[j, k])
        own_w.append(pltpu.make_async_copy(source, target.at[seq], own_sem.at[j]))
        experts_x.append(remote(source, target.at[seq], *sems(0), x_peer))
        experts_c.append(remote(source, target.at[seq], *sems(1), core_peer))
        experts_f.append(remote(target.at[far], target.at[far], *sems(2), core_peer))
    for copy in experts_x + own_w:
        copy.start()
    dy_copies = []
    for step in range(n_dp - 1, 0, -1):
        to = other(dp, step)
        dy_copies.append(
            remote(
                dy_sent.at[rows_of(to, held)],
                dy_slots_any.at[rows_of(dp, held)],
                ds_sem.at[step],
                dr_sem.at[step],
                (to, seq),
            )
        )
    for copy in dy_copies:
        copy.start()
    own_dy = pltpu.make_async_copy(
        dy_sent.at[rows_of(dp, held)], dy_slots_any.at[rows_of(dp, held)], own_sem.at[2]
    )
    own_dy.start()
    for stage in range(3):
        for h in range(2):
            hand_over(h, stage).wait_recv()
    for copy in experts_c:
        copy.start()
    starts = ((128, 0), (128 + D, D), (0, 2 * D), (D, 3 * D))

    def assemble(half, lanes, to=None):
        for oc in range(2):
            for ox in range(2):
                for oy in range(2):
                    for oz in range(4):
                        at = ((oz * 2 + oy) * 2 + ox) * 2 + oc
                        f, g = (ox, oy) if half == 0 else (oy, ox)
                        yield at, wide[half][oc, f, g, oz, :, lanes]

    narrow = dict(assemble(0, slice(0, 128)))
    narrow = jnp.concatenate([narrow[i].astype(f32) for i in range(n_dp * n_seq)], axis=0)
    router_ref[...] = narrow.astype(bf)
    vectors = narrow.T[8:16]
    vectors_ref[...] = vectors
    vec = lambda i: vectors[i : i + 1]
    for k, (start, col) in enumerate(starts):
        blocks = dict(assemble(k // 2, slice(start, start + D)))
        packed[:, col : col + D] = jnp.concatenate(
            [blocks[i].astype(f32) for i in range(n_dp * n_seq)], axis=0
        ).astype(bf)
    stores[3].start()
    h_one = (normed * vec(0) + vec(1)).astype(bf)
    for k in range(3):
        qkv[:, D * k : D * k + D] = nn(h_one, packed[:, D * k : D * k + D]).astype(bf)
    stores[4].start()
    lane = lax.broadcasted_iota(i32, (1, 128), 1)
    closed = jnp.where(mask_in[...].astype(f32) > 0.0, 0.0, -1e30).astype(bf)
    keep_out = lambda head: pltpu.make_async_copy(
        probs.at[head % 2], probs_any.at[head], probs_sem.at[head % 2]
    )
    for pair in range(HEADS // 2):
        q, k, v = (qkv[:, D * i + 128 * pair : D * i + 128 * pair + 128] for i in range(3))
        q = q * jnp.asarray(HEAD ** (-0.5), bf)
        out = jnp.zeros(q.shape, f32)
        for h in range(2):
            head = 2 * pair + h
            keep = (lane // HEAD == h).astype(bf)
            spare = (lane == HEAD * (1 - h)).astype(bf)
            scores = nt(q * keep + spare, k * keep + closed * spare)
            weights = jnp.exp(scores - jnp.max(scores, axis=-1, keepdims=True))
            weights = weights * (1.0 / jnp.sum(weights, axis=-1, keepdims=True))
            if head >= 2:
                keep_out(head - 2).wait()
            low = weights.astype(bf)
            probs[head % 2] = low
            keep_out(head).start()
            out = out + nn(low, v * keep)
        att[:, 128 * pair : 128 * pair + 128] = out.astype(bf)
    stores[5].start()
    made = nn(att[...], packed[:, 3 * D :]) + vec(2)
    branch[...] = made.astype(bf)
    resid[...] = x_row[...].astype(f32) + made
    normed, _ = norm_stats(resid[...])
    h_two[...] = (normed * vec(3) + vec(4)).astype(bf)
    to_blocks = [
        remote(
            h_two.at[rows_of(to, pos)],
            h_block_any.at[rows_of(seq, pos)],
            hs_sem.at[step],
            hr_sem.at[step],
            (dp, to),
        )
        for step, to in seq_peers
    ]
    for copy in to_blocks:
        copy.start()
    own_h = pltpu.make_async_copy(
        h_two.at[rows_of(seq, pos)], h_block_any.at[rows_of(seq, pos)], own_sem.at[3]
    )
    own_h.start()
    stores[6].start()
    stores[7].start()
    for j in range(2):
        experts_x[j].wait_recv()
        experts_f[j].start()
    for copy in to_blocks + dy_copies + biases + experts_c + experts_f:
        copy.wait_recv()
    keep_out(HEADS - 2).wait()
    keep_out(HEADS - 1).wait()
    for copy in stores + own_w + [own_dy, own_h]:
        copy.wait()
    for copy in exchange + to_blocks + dy_copies + biases + experts_x + experts_c + experts_f:
        copy.wait_send()
    for h in range(2):
        for stage in range(3):
            hand_over(h, stage).wait_send()
            for copy in gather(h, stage):
                copy.wait_send()


def front(n_dp, n_seq, cap, held, tokens, dy, w_qkv, w_out, narrow, first, second, cols, order, bias):
    bf, f32 = jnp.bfloat16, jnp.float32
    sds, dma, vmem = jax.ShapeDtypeStruct, pltpu.SemaphoreType.DMA, pltpu.VMEM
    tok = tokens.shape[0]
    slots = n_dp * held
    own = D // (n_dp * n_seq)
    block = (tok, D)
    return pl.pallas_call(
        functools.partial(front_kernel, n_dp, n_seq, cap),
        out_shape=(
            sds(block, bf),
            sds(block, f32),
            sds(block, bf),
            sds(block, bf),
            sds((tok, 3 * D), bf),
            sds((HEADS, tok, tok), bf),
            sds((D, 4 * D), bf),
            sds((8, D), f32),
            sds((D, 128), bf),
            sds(block, bf),
            sds((slots, tok), bf),
            sds((tok, slots), bf),
            sds((slots, D), bf),
            sds((n_seq,) + first.shape, bf),
            sds((n_seq,) + second.shape, bf),
            sds((n_seq,) + bias.shape, f32),
        ),
        in_specs=[ANY] * 7 + [VMEM] * 3,
        out_specs=(ANY,) * 7 + (VMEM,) * 2 + (ANY,) * 6 + (VMEM,),
        scratch_shapes=[
            vmem((2, 2, 2, 4, own, 128 + 2 * D), bf),
            vmem((2, 2, 2, 4, own, 2 * D), bf),
            vmem((D, 4 * D), bf),
            vmem(block, bf),
            vmem(block, bf),
            vmem((tok, 128), bf),
            vmem((tok, 128), bf),
            vmem((tok, 3 * D), bf),
            vmem(block, bf),
            vmem((2, tok, tok), bf),
            vmem(block, f32),
            vmem(block, bf),
            vmem(block, bf),
            vmem((slots, tok), bf),
            vmem((tok, slots), bf),
            vmem((slots, D), bf),
            dma((6,)),
            dma((8,)),
            dma((2,)),
            dma((4,)),
            dma((2, 9)),
            dma((2, 9)),
            dma((n_seq,)),
            dma((n_seq,)),
            dma((n_seq,)),
            dma((n_seq,)),
            dma((n_dp,)),
            dma((n_dp,)),
            dma((2, 3)),
            dma((2, 3)),
            dma((n_seq,)),
            dma((n_seq,)),
            dma((n_seq,)),
            dma((n_seq,)),
        ],
        compiler_params=pltpu.CompilerParams(
            collective_id=3, has_side_effects=True, vmem_limit_bytes=61 * 2**20
        ),
        cost_estimate=pl.CostEstimate(
            flops=6 * 10**9, bytes_accessed=5 * 10**7, transcendentals=4 * 10**6
        ),
        name="front",
    )(tokens, dy, w_qkv, w_out, narrow, first, second, cols, order, bias)


def shards_rows(
    tokens,
    cotangent,
    pad_mask,
    expert_ids,
    priority,
    ln1_gain,
    ln1_shift,
    w_qkv,
    w_out,
    out_bias,
    ln2_gain,
    ln2_shift,
    w_router,
    w_in,
    in_bias,
    w_exp_out,
    exp_out_bias,
):
    rows_dev, pos_dev = pad_mask.shape
    tok = rows_dev * pos_dev
    experts = w_router.shape[1]
    cap = (21 * tok + 10 * experts - 1) // (10 * experts)
    n_dp, n_seq = lax.axis_size("dp"), lax.axis_size("seq")
    seq, own = lax.axis_index("seq"), D // (n_dp * n_seq)
    bf, f32 = jnp.bfloat16, jnp.float32
    vectors = jnp.stack([ln1_gain, ln1_shift, out_bias, ln2_gain, ln2_shift], axis=1)
    narrow = jnp.concatenate([w_router, vectors], axis=1)
    narrow = jnp.pad(narrow, ((0, 0), (0, 128 - 5 - experts)))
    cols = jnp.stack(
        [
            priority.reshape(-1),
            expert_ids[:, :, 0].reshape(-1),
            expert_ids[:, :, 1].reshape(-1),
            pad_mask.reshape(-1),
        ],
        axis=1,
    )
    bias_cols = exp_out_bias.shape[1]
    second_bias = lax.dynamic_update_slice_in_dim(
        jnp.zeros((1, D), f32), exp_out_bias.astype(f32), seq * bias_cols, 1
    )
    bias = jnp.concatenate([in_bias.astype(f32), second_bias, jnp.zeros((14, D), f32)], axis=0)
    held = -(-cap // 16) * 16
    flat, dy_block = tokens.reshape(tok, D), cotangent.reshape(tok, D)
    (
        h_block,
        resid,
        x_row,
        attended,
        qkv,
        probs,
        packed,
        vectors,
        router,
        branch,
        into,
        outof,
        dy_slots,
        first,
        second,
        bias,
    ) = front(
        n_dp,
        n_seq,
        cap,
        held,
        flat,
        dy_block,
        w_qkv,
        w_out,
        narrow,
        w_in[0],
        w_exp_out[0],
        cols,
        priority.reshape(1, -1),
        bias,
    )
    grad_h2, made, first_grad, second_grad, router_grad, bias_grad, dy_row, branch_block = moe(
        h_block, into, outof, dy_slots, first, second, bias, router, dy_block, branch, experts
    )
    out, tokens_grad, dense, small, expert_grads, bias_grad = back(
        n_dp,
        n_seq,
        grad_h2,
        resid,
        x_row,
        dy_row,
        attended,
        qkv,
        probs,
        packed,
        vectors,
        made,
        outof,
        flat,
        branch_block,
        first_grad,
        second_grad,
        bias_grad,
        router_grad,
    )
    small = lax.dynamic_slice_in_dim(
        small, (lax.axis_index("dp") * n_seq + seq) * own, own, 1
    )
    qkv_grad = dense[:, D:].reshape(own, 3, 3, 256).swapaxes(1, 2).reshape(own, 3 * D)
    return (
        out.reshape(rows_dev, pos_dev, D),
        tokens_grad.reshape(rows_dev, pos_dev, D),
        small[0],
        small[1],
        qkv_grad,
        dense[:, :D],
        small[2],
        small[3],
        small[4],
        small[8 : 8 + experts].T,
        expert_grads[None, 0],
        bias_grad[None, 0],
        expert_grads[None, 1],
        lax.dynamic_slice_in_dim(bias_grad[None, 8], seq * bias_cols, bias_cols, 1),
    )


def shards(*args):
    block_rows, local_experts, n_dp = args[2].shape[0], args[13].shape[0], lax.axis_size("dp")
    if block_rows == lax.axis_size("seq") and local_experts == 1 and n_dp == 8:
        return shards_rows(*args)
    return shards_general(*args)


def solution(mesh):
    return jax.shard_map(
        shards,
        mesh=mesh,
        in_specs=(
            P("dp", "seq", None),
            P("dp", "seq", None),
            P("dp", "seq"),
            P("dp", "seq", None),
            P("dp", "seq"),
            P(("dp", "seq")),
            P(("dp", "seq")),
            P(("dp", "seq"), None),
            P(("dp", "seq"), None),
            P(("dp", "seq")),
            P(("dp", "seq")),
            P(("dp", "seq")),
            P(("dp", "seq"), None),
            P("dp", None, "seq"),
            P("dp", "seq"),
            P("dp", "seq", None),
            P("dp", "seq"),
        ),
        out_specs=(
            P("dp", "seq", None),
            P("dp", "seq", None),
            P(("dp", "seq")),
            P(("dp", "seq")),
            P(("dp", "seq"), None),
            P(("dp", "seq"), None),
            P(("dp", "seq")),
            P(("dp", "seq")),
            P(("dp", "seq")),
            P(("dp", "seq"), None),
            P("dp", None, "seq"),
            P("dp", "seq"),
            P("dp", "seq", None),
            P("dp", "seq"),
        ),
        check_vma=False,
    )
```

```python
import functools

import jax
import jax.numpy as jnp
from jax import lax
from jax.experimental import pallas as pl
from jax.experimental.pallas import tpu as pltpu
from jax.sharding import PartitionSpec as P

D = 768
HEADS = 12
HEAD = 64


norm_eps = 1e-06


def norm_forward(values, norm_gain, norm_shift):
    average = jnp.mean(values, axis=-1, keepdims=True)
    centred = values - average
    inv_scale = lax.rsqrt(jnp.mean(centred * centred, axis=-1, keepdims=True) + norm_eps)
    normed = centred * inv_scale
    return (
        normed * norm_gain.astype(jnp.float32) + norm_shift.astype(jnp.float32),
        normed,
        inv_scale,
    )


def norm_backward(grad_output, normed, inv_scale, norm_gain):
    scaled = grad_output * norm_gain.astype(jnp.float32)
    grad_input = inv_scale * (
        scaled
        - jnp.mean(scaled, axis=-1, keepdims=True)
        - normed * jnp.mean(scaled * normed, axis=-1, keepdims=True)
    )
    return (
        grad_input,
        jnp.sum(grad_output * normed, axis=(0, 1)),
        jnp.sum(grad_output, axis=(0, 1)),
    )


def gelu_slope(values):
    return (
        0.5 * (1.0 + lax.erf(values * 0.7071067811865476))
        + values * jnp.exp(-0.5 * values * values) * 0.3989422804014327
    )


def slot_ranks(order, picks, valid, experts, capacity):
    count = order.shape[0]
    index = jnp.arange(count, dtype=jnp.int32)
    rank = jnp.sum(jnp.where(order[:, None] == index[None, :], index[:, None], 0), axis=0)
    earlier = (rank[None, :] < rank[:, None]).astype(jnp.bfloat16)
    chosen = picks[:, :, None] == jnp.arange(experts, dtype=jnp.int32)
    counted = chosen.astype(jnp.float32) * valid.astype(jnp.float32)[:, None, None]
    before = jnp.dot(
        earlier,
        counted.reshape(count, 2 * experts).astype(jnp.bfloat16),
        preferred_element_type=jnp.float32,
    ).reshape(count, 2, experts)
    firsts = jnp.sum(counted[:, 0], axis=0)
    before = before + jnp.stack([jnp.zeros_like(firsts), firsts])[None]
    slot = jnp.sum(jnp.where(chosen, before, 0.0), axis=2).astype(jnp.int32)
    kept = (valid[:, None] > 0) & (slot < capacity)
    return kept, slot


def pair_slots(order, expert_picks, valid_flags, expert_count, capacity):
    kept, slot = slot_ranks(order, expert_picks, valid_flags, expert_count, capacity)
    tokens = jnp.arange(order.shape[0], dtype=jnp.int32)
    return (
        jnp.concatenate([tokens, tokens]),
        expert_picks.T.reshape(-1),
        slot.T.reshape(-1),
        kept.T.reshape(-1).astype(jnp.int32),
    )


def shards_general(
    tokens,
    cotangent,
    pad_mask,
    expert_ids,
    priority,
    ln1_gain,
    ln1_shift,
    w_qkv,
    w_out,
    out_bias,
    ln2_gain,
    ln2_shift,
    w_router,
    w_in,
    in_bias,
    w_exp_out,
    exp_out_bias,
):
    rows_dev, pos_dev = pad_mask.shape
    tok_count = rows_dev * pos_dev
    expert_count = w_router.shape[1]
    local_experts = w_in.shape[0]
    capacity = (21 * tok_count + 10 * expert_count - 1) // (10 * expert_count)
    scale_factor = HEAD ** (-0.5)
    gain_one, shift_one, qkv_weight, out_weight, out_shift, gain_two, shift_two, router_weight = (
        lax.all_gather(ln1_gain, ("dp", "seq"), axis=0, tiled=True),
        lax.all_gather(ln1_shift, ("dp", "seq"), axis=0, tiled=True),
        lax.all_gather(w_qkv, ("dp", "seq"), axis=0, tiled=True),
        lax.all_gather(w_out, ("dp", "seq"), axis=0, tiled=True),
        lax.all_gather(out_bias, ("dp", "seq"), axis=0, tiled=True),
        lax.all_gather(ln2_gain, ("dp", "seq"), axis=0, tiled=True),
        lax.all_gather(ln2_shift, ("dp", "seq"), axis=0, tiled=True),
        lax.all_gather(w_router, ("dp", "seq"), axis=0, tiled=True),
    )
    x_float = tokens.astype(jnp.float32)
    h_one, normed_one, inv_one = norm_forward(x_float, gain_one, shift_one)
    h_one_low = h_one.astype(jnp.bfloat16)
    qkv_low = jnp.einsum(
        "rpd,de->rpe", h_one_low, qkv_weight, preferred_element_type=jnp.float32
    ).astype(jnp.bfloat16)
    queries = qkv_low[:, :, :D].reshape(rows_dev, pos_dev, HEADS, HEAD)
    kv_all, mask_all = (
        lax.all_gather(qkv_low[:, :, D:], "seq", axis=1, tiled=True),
        lax.all_gather(pad_mask.astype(jnp.bfloat16), "seq", axis=1, tiled=True),
    )
    full_len = kv_all.shape[1]
    keys_all = kv_all[:, :, :D].reshape(rows_dev, full_len, HEADS, HEAD)
    values_all = kv_all[:, :, D:].reshape(rows_dev, full_len, HEADS, HEAD)
    key_open = (mask_all > 0)[:, None, None, :]

    def score_block():
        raw_scores = (
            jnp.einsum("rphd,rkhd->rhpk", queries, keys_all, preferred_element_type=jnp.float32)
            * scale_factor
        )
        return jnp.where(key_open, raw_scores, -1e30)

    scores = score_block()
    row_max = jnp.max(scores, axis=-1, keepdims=True)
    exp_scores = jnp.exp(scores - row_max)
    row_total = jnp.sum(exp_scores, axis=-1, keepdims=True)
    log_total = row_max + jnp.log(row_total)
    probs_low = (exp_scores / row_total).astype(jnp.bfloat16)
    attended = (
        jnp.einsum("rhpk,rkhd->rphd", probs_low, values_all, preferred_element_type=jnp.float32)
        .reshape(rows_dev, pos_dev, D)
        .astype(jnp.bfloat16)
    )
    branch = jnp.einsum(
        "rpd,de->rpe", attended, out_weight, preferred_element_type=jnp.float32
    ) + out_shift.astype(jnp.float32)
    resid = x_float + branch
    h_two, normed_two, inv_two = norm_forward(resid, gain_two, shift_two)
    flat_low = h_two.astype(jnp.bfloat16).reshape(tok_count, D)
    logits = jnp.dot(flat_low, router_weight, preferred_element_type=jnp.float32)
    router_probs = jax.nn.softmax(logits, axis=-1)
    token_pairs, expert_pairs, slot_index, kept_flags = pair_slots(
        priority.reshape(-1),
        expert_ids.reshape(tok_count, 2),
        pad_mask.reshape(-1),
        expert_count,
        capacity,
    )
    dummy_row = expert_count * capacity
    destination = jnp.where(kept_flags > 0, expert_pairs * capacity + slot_index, dummy_row)
    kept_float = kept_flags.astype(jnp.float32)
    gate_pairs = router_probs[token_pairs, expert_pairs] * kept_float
    send_rows = (
        jnp.zeros((dummy_row + 1, D), jnp.bfloat16)
        .at[destination]
        .set(flat_low[token_pairs])[:-1]
        .reshape(expert_count, capacity, D)
    )
    received = lax.all_to_all(send_rows, "dp", split_axis=0, concat_axis=1, tiled=True)
    seq_index = lax.axis_index("seq")
    bias_cols = exp_out_bias.shape[1]
    rows_all = lax.all_gather(received, "seq", axis=1, tiled=True)
    pre_act = (
        jnp.einsum("erd,edf->erf", rows_all, w_in, preferred_element_type=jnp.float32)
        + in_bias.astype(jnp.float32)[:, None, :]
    )
    act_low = jax.nn.gelu(pre_act, approximate=False).astype(jnp.bfloat16)
    partial_out = jnp.einsum("erf,efd->erd", act_low, w_exp_out, preferred_element_type=jnp.float32)
    bias_full = lax.dynamic_update_slice_in_dim(
        jnp.zeros((local_experts, D), jnp.float32),
        exp_out_bias.astype(jnp.float32),
        seq_index * bias_cols,
        1,
    )
    partial_out = partial_out + bias_full[:, None, :]
    expert_out = lax.psum_scatter(
        partial_out.astype(jnp.bfloat16), "seq", scatter_dimension=1, tiled=True
    )
    returned_buf = lax.all_to_all(expert_out, "dp", split_axis=1, concat_axis=0, tiled=True)
    returned = jnp.concatenate(
        [returned_buf.reshape(-1, D), jnp.zeros((1, D), jnp.bfloat16)], axis=0
    )[destination].astype(jnp.float32)
    mixture = (
        jnp.zeros((tok_count, D), jnp.float32).at[token_pairs].add(gate_pairs[:, None] * returned)
    )
    block_output = (resid + mixture.reshape(rows_dev, pos_dev, D)).astype(jnp.bfloat16)
    grad_y = cotangent.astype(jnp.float32)
    grad_pairs = grad_y.reshape(tok_count, D)[token_pairs]
    grad_gates = jnp.sum(grad_pairs * returned, axis=-1) * kept_float
    grad_ret = (gate_pairs[:, None] * grad_pairs).astype(jnp.bfloat16)
    grad_send = (
        jnp.zeros((dummy_row + 1, D), jnp.bfloat16)
        .at[destination]
        .set(grad_ret)[:-1]
        .reshape(expert_count, capacity, D)
    )
    grad_recv = lax.all_to_all(grad_send, "dp", split_axis=0, concat_axis=1, tiled=True)
    grad_all = lax.all_gather(grad_recv, "seq", axis=1, tiled=True)
    pre_again = (
        jnp.einsum("erd,edf->erf", rows_all, w_in, preferred_element_type=jnp.float32)
        + in_bias.astype(jnp.float32)[:, None, :]
    )
    act_again = jax.nn.gelu(pre_again, approximate=False).astype(jnp.bfloat16)
    grad_act = jnp.einsum("erd,efd->erf", grad_all, w_exp_out, preferred_element_type=jnp.float32)
    grad_pre = (grad_act * gelu_slope(pre_again)).astype(jnp.bfloat16)
    w_exp_out_grad = jnp.einsum(
        "erf,erd->efd", act_again, grad_all, preferred_element_type=jnp.float32
    )
    bias_sums = jnp.sum(grad_all, axis=1, dtype=jnp.float32)
    exp_out_bias_grad = lax.dynamic_slice_in_dim(bias_sums, seq_index * bias_cols, bias_cols, 1)
    w_in_grad = jnp.einsum("erd,erf->edf", rows_all, grad_pre, preferred_element_type=jnp.float32)
    in_bias_grad = jnp.sum(grad_pre, axis=1, dtype=jnp.float32)
    grad_rows_part = jnp.einsum("erf,edf->erd", grad_pre, w_in, preferred_element_type=jnp.float32)
    grad_back = lax.psum_scatter(
        grad_rows_part.astype(jnp.bfloat16), "seq", scatter_dimension=1, tiled=True
    )
    grad_buf = lax.all_to_all(grad_back, "dp", split_axis=1, concat_axis=0, tiled=True)
    grad_rows_back = jnp.concatenate(
        [grad_buf.reshape(-1, D), jnp.zeros((1, D), jnp.bfloat16)], axis=0
    )[destination].astype(jnp.float32)
    grad_h2_experts = jnp.zeros((tok_count, D), jnp.float32).at[token_pairs].add(grad_rows_back)
    grad_probs = (
        jnp.zeros((tok_count, expert_count), jnp.float32)
        .at[token_pairs, expert_pairs]
        .add(grad_gates)
    )
    grad_logits = (
        router_probs * (grad_probs - jnp.sum(router_probs * grad_probs, axis=-1, keepdims=True))
    ).astype(jnp.bfloat16)
    router_grad = jnp.einsum("td,te->de", flat_low, grad_logits, preferred_element_type=jnp.float32)
    grad_h2 = grad_h2_experts + jnp.einsum(
        "te,de->td", grad_logits, router_weight, preferred_element_type=jnp.float32
    )
    grad_resid_norm, gain_two_grad, shift_two_grad = norm_backward(
        grad_h2.reshape(rows_dev, pos_dev, D), normed_two, inv_two, gain_two
    )
    grad_resid = grad_y + grad_resid_norm
    grad_branch = grad_resid.astype(jnp.bfloat16)
    out_weight_grad = jnp.einsum(
        "rpd,rpe->de", attended, grad_branch, preferred_element_type=jnp.float32
    )
    out_shift_grad = jnp.sum(grad_branch, axis=(0, 1), dtype=jnp.float32)
    grad_attended = jnp.einsum(
        "rpe,de->rpd", grad_branch, out_weight, preferred_element_type=jnp.float32
    ).astype(jnp.bfloat16)
    grad_att_heads = grad_attended.reshape(rows_dev, pos_dev, HEADS, HEAD)
    scores_again = score_block()
    probs_again = jnp.exp(scores_again - log_total)
    probs_again_low = probs_again.astype(jnp.bfloat16)
    grad_probs_att = jnp.einsum(
        "rphd,rkhd->rhpk", grad_att_heads, values_all, preferred_element_type=jnp.float32
    )
    row_delta = jnp.sum(probs_again * grad_probs_att, axis=-1, keepdims=True)
    grad_scores = (probs_again * (grad_probs_att - row_delta)).astype(jnp.bfloat16)
    grad_queries = (
        jnp.einsum("rhpk,rkhd->rphd", grad_scores, keys_all, preferred_element_type=jnp.float32)
        * scale_factor
    ).reshape(rows_dev, pos_dev, D)
    grad_keys = (
        jnp.einsum("rhpk,rphd->rkhd", grad_scores, queries, preferred_element_type=jnp.float32)
        * scale_factor
    ).reshape(rows_dev, full_len, D)
    grad_values = jnp.einsum(
        "rhpk,rphd->rkhd", probs_again_low, grad_att_heads, preferred_element_type=jnp.float32
    ).reshape(rows_dev, full_len, D)
    grad_kv = lax.psum_scatter(
        jnp.concatenate([grad_keys, grad_values], axis=-1).astype(jnp.bfloat16),
        "seq",
        scatter_dimension=1,
        tiled=True,
    )
    grad_qkv = jnp.concatenate([grad_queries.astype(jnp.bfloat16), grad_kv], axis=-1)
    qkv_weight_grad = jnp.einsum(
        "rpd,rpe->de", h_one_low, grad_qkv, preferred_element_type=jnp.float32
    )
    grad_h1 = jnp.einsum("rpe,de->rpd", grad_qkv, qkv_weight, preferred_element_type=jnp.float32)
    grad_x_norm, gain_one_grad, shift_one_grad = norm_backward(
        grad_h1, normed_one, inv_one, gain_one
    )
    tokens_grad = (grad_resid + grad_x_norm).astype(jnp.bfloat16)
    dense_parts = (
        lax.psum_scatter(gain_one_grad, ("dp", "seq"), scatter_dimension=0, tiled=True),
        lax.psum_scatter(shift_one_grad, ("dp", "seq"), scatter_dimension=0, tiled=True),
        lax.psum_scatter(qkv_weight_grad, ("dp", "seq"), scatter_dimension=0, tiled=True),
        lax.psum_scatter(out_weight_grad, ("dp", "seq"), scatter_dimension=0, tiled=True),
        lax.psum_scatter(out_shift_grad, ("dp", "seq"), scatter_dimension=0, tiled=True),
        lax.psum_scatter(gain_two_grad, ("dp", "seq"), scatter_dimension=0, tiled=True),
        lax.psum_scatter(shift_two_grad, ("dp", "seq"), scatter_dimension=0, tiled=True),
        lax.psum_scatter(router_grad, ("dp", "seq"), scatter_dimension=0, tiled=True),
    )
    return (
        block_output,
        tokens_grad,
        dense_parts[0],
        dense_parts[1],
        dense_parts[2],
        dense_parts[3],
        dense_parts[4],
        dense_parts[5],
        dense_parts[6],
        dense_parts[7],
        w_in_grad,
        in_bias_grad,
        w_exp_out_grad,
        exp_out_bias_grad,
    )


MESH = pl.DeviceIdType.MESH
VMEM = pl.BlockSpec(memory_space=pltpu.VMEM)
ANY = pl.BlockSpec(memory_space=pl.ANY)
ERF = (0.1274147955, -0.142248368, 0.7107068705, -0.7265760135, 0.5307027145)


def nn(a, b):
    return lax.dot_general(a, b, (((1,), (0,)), ((), ())), preferred_element_type=jnp.float32)


def nt(a, b):
    return lax.dot_general(a, b, (((1,), (1,)), ((), ())), preferred_element_type=jnp.float32)


def tn(a, b):
    return lax.dot_general(a, b, (((0,), (0,)), ((), ())), preferred_element_type=jnp.float32)


def gelu_parts(v):
    bell = jnp.exp(v * v * -0.5)
    t = 1.0 / (jnp.abs(v) * (0.3275911 * 0.7071067811865476) + 1.0)
    a, b, c, d, e = ERF
    tail = ((((e * t + d) * t + c) * t + b) * t + a) * t * bell
    cdf = jnp.where(v < 0.0, tail, 1.0 - tail)
    return v * cdf, cdf + v * (bell * 0.3989422804014327)


def other(me, step):
    bit = lambda k: lax.rem(me // k + step // k, 2) * k
    return bit(4) + bit(2) + bit(1)


def moe_kernel(
    experts,
    h_ref,
    into_ref,
    from_ref,
    dy_ref,
    first_any,
    second_any,
    bias_ref,
    router_ref,
    dy_any,
    branch_any,
    grad_ref,
    outs_ref,
    first_grad_any,
    second_grad_ref,
    router_grad_ref,
    bias_grad_ref,
    dy_row_any,
    branch_block_any,
    sent,
    rows,
    go,
    act,
    gp,
    back_sent,
    back,
    logit_grad,
    first,
    second,
    w_sem,
    send_sem,
    recv_sem,
    send_sem2,
    recv_sem2,
    send_sem3,
    recv_sem3,
    own_sem,
    grad_sem,
    recv_e,
    recv_x,
    es_sem,
    er_sem,
):
    n = experts
    cap = dy_ref.shape[0] // n
    bf, f32 = jnp.bfloat16, jnp.float32
    blocks = first.shape[0]
    me, seq = lax.axis_index("dp"), lax.axis_index("seq")
    n_seq = blocks
    pos = h_ref.shape[0] // n_seq
    load1 = pltpu.make_async_copy(first_any, first, w_sem.at[0])
    load2 = pltpu.make_async_copy(second_any, second, w_sem.at[1])
    load1.start()
    load2.start()
    at = lambda i: pl.ds(pl.multiple_of(i * cap, cap), cap)
    greet(n, n_seq)

    def dispatch(step, source, target, sems):
        to = other(me, step)
        return pltpu.make_async_remote_copy(
            source.at[at(to)],
            target.at[at(me)],
            sems[0].at[step],
            sems[1].at[step],
            device_id=(to, seq),
            device_id_type=MESH,
        )

    out_sems, back_sems = (send_sem, recv_sem), (send_sem2, recv_sem2)

    @pl.loop(0, n - 1)
    def _(i):
        step = n - 1 - i
        to = other(me, step)
        sent[at(to), :] = nn(into_ref[at(to), :], h_ref[...]).astype(bf)
        dispatch(step, sent, rows, out_sems).start()

    rows[at(me), :] = nn(into_ref[at(me), :], h_ref[...]).astype(bf)
    swaps, own_swaps = [], []
    for k, (source, target) in enumerate(((dy_any, dy_row_any), (branch_any, branch_block_any))):
        here = rows_of(seq, pos)
        own_swaps.append(pltpu.make_async_copy(source.at[here], target.at[here], own_sem.at[k]))
        for step in range(1, n_seq):
            to = lax.rem(seq + step, n_seq)
            swaps.append(
                remote(
                    source.at[rows_of(to, pos)],
                    target.at[here],
                    send_sem3.at[k, step],
                    recv_sem3.at[k, step],
                    (me, to),
                )
            )
    for copy in swaps + own_swaps:
        copy.start()
    load1.wait()
    load2.wait()
    pair = 2 * cap
    lane = lax.broadcasted_iota(jnp.int32, (pair, 128), 1)
    second_bias = jnp.sum(bias_ref[:, 1, :], axis=0, keepdims=True)

    @pl.loop(0, n // 2)
    def _(plane):
        group = rows_of(other(me, 2 * plane) // 2, pair)

        @pl.when(plane > 0)
        def _():
            dispatch(2 * plane, sent, rows, out_sems).wait_recv()

        dispatch(2 * plane + 1, sent, rows, out_sems).wait_recv()
        x = rows[group, :]
        dy = dy_ref[group, :].astype(f32)
        logits = jnp.where(lane < n, nn(x, router_ref[...]), -1e30)
        probs = jnp.exp(logits - jnp.max(logits, axis=-1, keepdims=True))
        probs = probs / jnp.sum(probs, axis=-1, keepdims=True)
        mine = (lane == me).astype(f32)
        gate = jnp.sum(probs * mine, axis=-1, keepdims=True)
        grad_out = (gate * dy).astype(bf)
        go[group, :] = grad_out

        def block(q, sums):
            out, grad_row = sums
            value, slope = gelu_parts(nn(x, first[q]) + bias_ref[q, 0:1])
            value = value.astype(bf)
            act[q, group, :] = value
            grad_pre = (nt(grad_out, second[q]) * slope).astype(bf)
            gp[q, group, :] = grad_pre
            return out + nn(value, second[q]), grad_row + nt(grad_pre, first[q])

        zero = jnp.zeros((pair, x.shape[1]), f32)
        out, grad_row = lax.fori_loop(0, blocks, block, (zero, zero), unroll=True)
        made = (out + second_bias).astype(bf).astype(f32)
        grad_gate = jnp.sum(dy * made, axis=-1, keepdims=True)
        grad_logits = (grad_gate * gate * (mine - probs)).astype(bf)
        logit_grad[group, :] = grad_logits
        grad_row = (grad_row + nt(grad_logits, router_ref[...])).astype(bf)
        outs_ref[group, :] = (gate * made).astype(bf)
        back_sent[group, :] = grad_row

        @pl.when(plane > 0)
        def _():
            dispatch(2 * plane, back_sent, back, back_sems).start()

        dispatch(2 * plane + 1, back_sent, back, back_sems).start()

    back[at(me), :] = back_sent[at(me), :]
    _, _, x_at, c_at = split_axes()
    core_peer, x_peer = (me, x_at * 2 + 1 - c_at), (me, (1 - x_at) * 2 + c_at)
    far, near = (1 - x_at) * 2 + c_at, seq

    def to_core(k):
        side = lax.rem(x_at + 1 + k, 2)
        return remote(
            second.at[side * 2 + 1 - c_at], recv_e.at[k], es_sem.at[k], er_sem.at[k], core_peer
        )

    to_x = remote(second.at[far], recv_x, es_sem.at[2], er_sem.at[2], x_peer)

    @pl.loop(0, blocks)
    def _(k):
        q = lax.rem(x_at + 1 + k // 2, 2) * 2 + lax.rem(c_at + 1 + k, 2)
        second[q] = tn(act[q], go[...]).astype(bf)

        @pl.when(lax.rem(k, 2) == 0)
        def _():
            to_core(k // 2).start()

    to_core(0).wait_recv()
    second[far] = (second[far].astype(f32) + recv_e[0].astype(f32)).astype(bf)
    to_x.start()
    ones = jnp.ones((8, rows.shape[0]), bf)

    @pl.loop(0, blocks)
    def _(q):
        first[q] = tn(rows[...], gp[q]).astype(bf)
        pltpu.make_async_copy(first.at[q], first_grad_any.at[q], grad_sem.at[q]).start()
        bias_grad_ref[q, :8] = nn(ones, gp[q])
        bias_grad_ref[q, 8:] = nn(ones, go[...])

    router_grad_ref[...] = tn(logit_grad[...], rows[...])[: router_grad_ref.shape[0]]

    @pl.loop(1, n)
    def _(step):
        dispatch(step, back_sent, back, back_sems).wait()
        dispatch(step, sent, rows, out_sems).wait_send()

    grad_ref[...] = nn(from_ref[...], back[...]).astype(bf)
    for copy in swaps + own_swaps:
        copy.wait()

    @pl.loop(0, blocks)
    def _(q):
        pltpu.make_async_copy(first.at[q], first_grad_any.at[q], grad_sem.at[q]).wait()

    to_core(1).wait_recv()
    to_x.wait_recv()

    @pl.loop(0, 6)
    def _(k):
        at = rows_of(k, recv_x.shape[0] // 6)
        second_grad_ref[at, :] = (
            second[near, at, :].astype(f32) + recv_e[1, at, :].astype(f32) + recv_x[at, :].astype(f32)
        )

    to_core(0).wait_send()
    to_core(1).wait_send()
    to_x.wait_send()


def moe(h_block, into, outof, dy_slots, first, second, bias, router, dy, branch, experts):
    bf, f32 = jnp.bfloat16, jnp.float32
    tok, width = h_block.shape
    slots = into.shape[0]
    blocks, hidden = first.shape[0], first.shape[2]
    sds = jax.ShapeDtypeStruct
    dma = pltpu.SemaphoreType.DMA
    big = (slots, width)
    return pl.pallas_call(
        functools.partial(moe_kernel, experts),
        out_shape=(
            sds((tok, width), bf),
            sds(big, bf),
            sds(first.shape, bf),
            sds(second.shape[1:], f32),
            sds((8, width), f32),
            sds((blocks, 16, hidden), f32),
            sds((tok, width), bf),
            sds((tok, width), bf),
        ),
        in_specs=[VMEM] * 4 + [ANY] * 2 + [VMEM] * 2 + [ANY] * 2,
        out_specs=(VMEM,) * 2 + (ANY,) + (VMEM,) * 3 + (ANY,) * 2,
        scratch_shapes=[
            pltpu.VMEM(big, bf),
            pltpu.VMEM(big, bf),
            pltpu.VMEM(big, bf),
            pltpu.VMEM((blocks, slots, hidden), bf),
            pltpu.VMEM((blocks, slots, hidden), bf),
            pltpu.VMEM(big, bf),
            pltpu.VMEM(big, bf),
            pltpu.VMEM((slots, 128), bf),
            pltpu.VMEM(first.shape, bf),
            pltpu.VMEM(second.shape, bf),
            dma((2,)),
            dma((experts,)),
            dma((experts,)),
            dma((experts,)),
            dma((experts,)),
            dma((2, blocks)),
            dma((2, blocks)),
            dma((2,)),
            dma((blocks,)),
            pltpu.VMEM((2,) + second.shape[1:], bf),
            pltpu.VMEM(second.shape[1:], bf),
            dma((3,)),
            dma((3,)),
        ],
        compiler_params=pltpu.CompilerParams(
            collective_id=1, has_side_effects=True, vmem_limit_bytes=61 * 2**20
        ),
        cost_estimate=pl.CostEstimate(
            flops=12 * slots * width * hidden * blocks, bytes_accessed=4 * 10**7, transcendentals=slots * hidden * blocks
        ),
        name="moe",
    )(h_block, into, outof, dy_slots, first, second, bias, router, dy, branch)


def norm_stats(values):
    average = jnp.mean(values, axis=-1, keepdims=True)
    centred = values - average
    inv = lax.rsqrt(jnp.mean(centred * centred, axis=-1, keepdims=True) + norm_eps)
    return centred * inv, inv


def norm_grad(grad_output, normed, inv, gain):
    scaled = grad_output * gain
    return inv * (
        scaled
        - jnp.mean(scaled, axis=-1, keepdims=True)
        - normed * jnp.mean(scaled * normed, axis=-1, keepdims=True)
    )


def rows_of(i, size):
    return pl.ds(pl.multiple_of(i * size, size), size)


def split_axes():
    dp, seq = lax.axis_index("dp"), lax.axis_index("seq")
    return dp // 2, lax.rem(dp, 2), seq // 2, lax.rem(seq, 2)


def greet(n_dp, n_seq):
    dp, seq = lax.axis_index("dp"), lax.axis_index("seq")
    barrier = pltpu.get_barrier_semaphore()
    for step in range(1, n_dp):
        pl.semaphore_signal(
            barrier, inc=1, device_id=(other(dp, step), seq), device_id_type=MESH
        )
    for step in range(1, n_seq):
        pl.semaphore_signal(
            barrier, inc=1, device_id=(dp, lax.rem(seq + step, n_seq)), device_id_type=MESH
        )
    pl.semaphore_wait(barrier, n_dp - 1 + n_seq - 1)


def remote(source, target, send, recv, device):
    return pltpu.make_async_remote_copy(
        source, target, send, recv, device_id=device, device_id_type=MESH
    )


def back_kernel(
    n_dp,
    n_seq,
    grad_any,
    resid_any,
    x_any,
    dy_any,
    att_any,
    qkv_any,
    probs_any,
    packed_any,
    vectors_ref,
    outs_any,
    outof_any,
    tokens_any,
    branch_any,
    first_any,
    bias_ref,
    router_grad_ref,
    block_out_ref,
    tokens_grad_ref,
    qkv_grad_ref,
    out_grad_ref,
    small_ref,
    first_out_ref,
    bias_out_ref,
    grad_rows,
    resid,
    x_row,
    dy_row,
    att,
    qkv,
    probs,
    w_qkv,
    w_out,
    outs,
    outof,
    tokens,
    branch,
    own_e,
    recv_e,
    recv_x,
    recv_b,
    grad_resid,
    grad_att,
    grad_qkv,
    h_one,
    grad_x,
    part,
    recv_c,
    recv_1,
    recv_2,
    recv_3,
    sums,
    recv_s,
    load_sem,
    probs_sem,
    own_sem,
    gs_sem,
    gr_sem,
    os_sem,
    or_sem,
    es_sem,
    er_sem,
    xs_sem,
    xr_sem,
    bs_sem,
    br_sem,
    ps_sem,
    pr_sem,
    ss_sem,
    sr_sem,
    ts_sem,
    tr_sem,
):
    bf, f32 = jnp.bfloat16, jnp.float32
    dp, seq = lax.axis_index("dp"), lax.axis_index("seq")
    z, y, x, c = split_axes()
    pos = grad_rows.shape[0] // n_seq
    cap = outs.shape[0] // n_dp
    core_peer, x_peer = (dp, x * 2 + 1 - c), (dp, (1 - x) * 2 + c)
    y_peer = (z * 2 + 1 - y, seq)
    z_peer = lambda step: (lax.rem(z + step, 4) * 2 + y, seq)
    loads = [
        pltpu.make_async_copy(a, b, load_sem.at[i])
        for i, (a, b) in enumerate(
            (
                (resid_any, resid),
                (dy_any, dy_row),
                (att_any, att),
                (packed_any.at[:, 3 * D : 4 * D], w_out),
                (qkv_any, qkv),
                (x_any, x_row),
                (packed_any.at[:, : 3 * D], w_qkv),
                (outof_any, outof),
                (tokens_any, tokens),
                (branch_any, branch),
            )
        )
    ]
    fetch = lambda head: pltpu.make_async_copy(
        probs_any.at[head], probs.at[head % 2], probs_sem.at[head % 2]
    )
    for load in loads[:4]:
        load.start()
    greet(n_dp, n_seq)
    to_rows = []
    for step in range(1, n_seq):
        to = lax.rem(seq + step, n_seq)
        to_rows.append(
            remote(
                grad_any.at[rows_of(to, pos)],
                grad_rows.at[rows_of(seq, pos)],
                gs_sem.at[step],
                gr_sem.at[step],
                (dp, to),
            )
        )
    for copy in to_rows:
        copy.start()
    own_rows = pltpu.make_async_copy(
        grad_any.at[rows_of(seq, pos)], grad_rows.at[rows_of(seq, pos)], own_sem.at[0]
    )
    own_rows.start()
    experts_c, experts_own = [], []
    for k, side in enumerate((1 - x, x)):
        experts_c.append(
            remote(
                first_any.at[side * 2 + 1 - c], recv_e.at[k], es_sem.at[k], er_sem.at[k], core_peer
            )
        )
        experts_own.append(
            pltpu.make_async_copy(first_any.at[side * 2 + c], own_e.at[k], own_sem.at[1 + k])
        )
    for copy in experts_c + experts_own:
        copy.start()
    returns = []
    for step in range(n_dp - 1, 0, -1):
        to = other(dp, step)
        returns.append(
            remote(
                outs_any.at[rows_of(to, cap)],
                outs.at[rows_of(dp, cap)],
                os_sem.at[step],
                or_sem.at[step],
                (to, seq),
            )
        )
    for copy in returns:
        copy.start()
    own_outs = pltpu.make_async_copy(
        outs_any.at[rows_of(dp, cap)], outs.at[rows_of(dp, cap)], own_sem.at[3]
    )
    own_outs.start()
    biases = []
    for step in range(1, n_seq):
        to = lax.rem(seq + step, n_seq)
        biases.append(
            remote(bias_ref.at[to], recv_b.at[step], bs_sem.at[step], br_sem.at[step], (dp, to))
        )
    for copy in biases:
        copy.start()
    for load in loads[4:]:
        load.start()
    fetch(0).start()
    fetch(1).start()
    vec = lambda i: vectors_ref[i : i + 1, :]
    row_sum = lambda v: jnp.sum(v, axis=0, keepdims=True)

    def norm_back(grad_output, values, gain):
        normed, inv = norm_stats(values)
        sums_of = (row_sum(grad_output * normed), row_sum(grad_output))
        return norm_grad(grad_output, normed, inv, gain), *sums_of

    def piece_fill(i, value):
        half = value.shape[1] // 2
        for owner in range(n_dp * n_seq):
            oz, oy, ox, oc = owner // 8, owner // 4 % 2, owner // 2 % 2, owner % 2
            block = value[24 * owner : 24 * owner + 24].astype(bf)
            part[i, oc, 0, ox, oy, oz] = block[:, :half]
            part[i, oc, 1, oy, ox, oz] = block[:, half:]

    first_axis = ((x, x_peer), (y, y_peer))

    def piece_copies(i, stage):
        sems = lambda k: (ps_sem.at[i, k], pr_sem.at[i, k])
        if stage == 0:
            return [remote(part.at[i, 1 - c], recv_c.at[i], *sems(0), core_peer)]
        made = []
        for h in range(2):
            (f, f_peer), (g, g_peer) = first_axis[h], first_axis[1 - h]
            if stage == 1:
                made.append(
                    remote(part.at[i, c, h, 1 - f], recv_1.at[i, h], *sems(1 + h), f_peer)
                )
            elif stage == 2:
                made.append(
                    remote(part.at[i, c, h, f, 1 - g], recv_2.at[i, h], *sems(3 + h), g_peer)
                )
            else:
                for step in range(1, 4):
                    made.append(
                        remote(
                            part.at[i, c, h, f, g, lax.rem(z + step, 4)],
                            recv_3.at[i, h, step],
                            *sems(4 + h * 3 + step),
                            z_peer(step),
                        )
                    )
        return made

    def add(a, b):
        return (a.astype(f32) + b.astype(f32)).astype(bf)

    def piece_advance(i, stage):
        for copy in piece_copies(i, stage - 1):
            copy.wait_recv()
        if stage == 1:
            part[i, c] = add(part[i, c], recv_c[i])
        for h in range(2):
            f, g = first_axis[h][0], first_axis[1 - h][0]
            if stage == 2:
                part[i, c, h, f] = add(part[i, c, h, f], recv_1[i, h])
            elif stage == 3:
                part[i, c, h, f, g] = add(part[i, c, h, f, g], recv_2[i, h])
            elif stage == 4:
                total = part[i, c, h, f, g, z].astype(f32)
                for step in range(1, 4):
                    total = total + recv_3[i, h, step].astype(f32)
                half = total.shape[1]
                for k in range(3):
                    at = h * half + k * 128
                    lanes = total[:, k * 128 : k * 128 + 128]
                    if i == 0:
                        out_grad_ref[:, at : at + 128] = lanes
                    else:
                        to = D * (at // 256) + 256 * (i - 1) + at % 256
                        qkv_grad_ref[:, to : to + 128] = lanes
        if stage < 4:
            for copy in piece_copies(i, stage):
                copy.start()

    def small_copies(stage):
        peers = ([core_peer], [x_peer], [y_peer], [z_peer(1), z_peer(2), z_peer(3)])[stage]
        return [
            remote(
                sums.at[stage],
                recv_s.at[stage + k],
                ss_sem.at[stage + k],
                sr_sem.at[stage + k],
                peer,
            )
            for k, peer in enumerate(peers)
        ]

    def small_advance(stage):
        for copy in small_copies(stage - 1):
            copy.wait_recv()
        if stage < 4:
            sums[stage] = sums[stage - 1] + recv_s[stage - 1]
            for copy in small_copies(stage):
                copy.start()
        else:
            small_ref[...] = sums[3] + recv_s[3] + recv_s[4] + recv_s[5]

    experts_x = remote(own_e.at[0], recv_x, xs_sem, xr_sem, x_peer)

    def experts_send_x():
        experts_c[0].wait_recv()
        experts_own[0].wait()
        own_e[0] = add(own_e[0], recv_e[0])
        experts_x.start()

    def experts_end():
        experts_c[1].wait_recv()
        experts_own[1].wait()
        experts_x.wait_recv()

        @pl.loop(0, 6)
        def _(k):
            at = rows_of(k, recv_x.shape[0] // 6)
            first_out_ref[at, :] = (
                own_e[1, at, :].astype(f32)
                + recv_e[1, at, :].astype(f32)
                + recv_x[at, :].astype(f32)
            )

        bias = bias_ref[seq]
        for step in range(1, n_seq):
            biases[step - 1].wait_recv()
            bias = bias + recv_b[step]
        bias_out_ref[...] = bias

    for load in loads[:3]:
        load.wait()
    own_rows.wait()
    for copy in to_rows:
        copy.wait_recv()
    experts_send_x()
    grad_in, gain_two, shift_two = norm_back(grad_rows[...].astype(f32), resid[...], vec(3))
    grad_resid[...] = dy_row[...].astype(f32) + grad_in
    grad_branch = grad_resid[...].astype(bf)
    out_shift = row_sum(grad_branch.astype(f32))
    loads[3].wait()
    grad_att[...] = nt(grad_branch, w_out[...]).astype(bf)
    piece_fill(0, tn(att[...], grad_branch))
    for copy in piece_copies(0, 0):
        copy.start()
    loads[4].wait()
    loads[5].wait()
    x_normed, _ = norm_stats(x_row[...].astype(f32))
    h_one[...] = (x_normed * vec(0) + vec(1)).astype(bf)
    lane = lax.broadcasted_iota(jnp.int32, (1, 128), 1) // HEAD
    scale = HEAD ** (-0.5)
    for pair in range(HEADS // 2):
        cols = slice(128 * pair, 128 * pair + 128)
        q, k, v = (qkv[:, D * i + 128 * pair : D * i + 128 * pair + 128] for i in range(3))
        go = grad_att[:, cols]
        both = go.astype(f32) * att[:, cols].astype(f32)
        grads = [jnp.zeros(q.shape, f32)] * 3
        for h in range(2):
            head = 2 * pair + h
            keep = (lane == h).astype(bf)
            fetch(head).wait()
            p = probs[head % 2]
            go_h = go * keep
            delta = jnp.sum(both * keep.astype(f32), axis=-1, keepdims=True)
            ds = (p.astype(f32) * (nt(go_h, v) - delta)).astype(bf)
            grads = [
                grads[0] + nn(ds, k * keep),
                grads[1] + tn(ds, q * keep),
                grads[2] + tn(p, go_h),
            ]
            if head + 2 < HEADS:
                fetch(head + 2).start()
        for i, factor in enumerate((scale, scale, 1.0)):
            at = (2 * 128) * (3 * (pair // 2) + i) + 128 * (pair % 2)
            grad_qkv[:, at : at + 128] = (grads[i] * factor).astype(bf)
        if pair < 4:
            piece_advance(0, pair + 1)
        if pair in (2, 3, 4, 5):
            piece_advance(1, pair - 1)
        if pair in (4, 5):
            piece_advance(2, pair - 3)
        if pair % 2 == 1:
            i = pair // 2 + 1
            piece_fill(i, tn(h_one[...], grad_qkv[:, D * (i - 1) : D * i]))
            for copy in piece_copies(i, 0):
                copy.start()
    loads[6].wait()
    grad_h1 = jnp.zeros(resid.shape, f32)
    for i in range(9):
        at = 256 * i
        col = D * (i % 3) + 256 * (i // 3)
        grad_h1 = grad_h1 + nt(grad_qkv[:, at : at + 256], w_qkv[:, col : col + 256])
    grad_in, gain_one, shift_one = norm_back(grad_h1, x_row[...].astype(f32), vec(0))
    sums[0] = jnp.concatenate(
        [gain_one, shift_one, out_shift, gain_two, shift_two, jnp.zeros((3, D), f32), router_grad_ref[...]], axis=0
    )
    for copy in small_copies(0):
        copy.start()
    grad_x[...] = (grad_resid[...] + grad_in).astype(bf)
    to_blocks = []
    for step in range(1, n_seq):
        to = lax.rem(seq + step, n_seq)
        to_blocks.append(
            remote(
                grad_x.at[rows_of(to, pos)],
                tokens_grad_ref.at[rows_of(seq, pos)],
                ts_sem.at[step],
                tr_sem.at[step],
                (dp, to),
            )
        )
    for copy in to_blocks:
        copy.start()
    tokens_grad_ref[rows_of(seq, pos), :] = grad_x[rows_of(seq, pos), :]
    piece_advance(3, 1)
    piece_advance(2, 3)
    small_advance(1)
    own_outs.wait()
    for copy in returns:
        copy.wait_recv()
    for load in loads[7:]:
        load.wait()
    block_out_ref[...] = (
        tokens[...].astype(f32) + branch[...].astype(f32) + nn(outof[...], outs[...])
    ).astype(bf)
    piece_advance(3, 2)
    small_advance(2)
    piece_advance(2, 4)
    experts_end()
    piece_advance(3, 3)
    small_advance(3)
    piece_advance(3, 4)
    small_advance(4)
    for copy in to_blocks:
        copy.wait_recv()
    for copy in to_rows + experts_c + returns + biases + [experts_x] + to_blocks:
        copy.wait_send()
    for stage in range(4):
        for i in range(4):
            for copy in piece_copies(i, stage):
                copy.wait_send()
        for copy in small_copies(stage):
            copy.wait_send()


def back(
    n_dp,
    n_seq,
    grad_h2,
    resid,
    x_row,
    dy_row,
    att,
    qkv,
    probs,
    packed,
    vectors,
    outs,
    outof,
    tokens,
    branch,
    first_grad,
    biases,
    router_grad,
):
    bf, f32 = jnp.bfloat16, jnp.float32
    sds, dma, vmem = jax.ShapeDtypeStruct, pltpu.SemaphoreType.DMA, pltpu.VMEM
    tok, slots = outof.shape
    pos = tok // n_seq
    half = D // 2
    return pl.pallas_call(
        functools.partial(back_kernel, n_dp, n_seq),
        out_shape=(
            sds((tok, D), bf),
            sds((tok, D), bf),
            sds((D // (n_dp * n_seq), 3 * D), f32),
            sds((D // (n_dp * n_seq), D), f32),
            sds((16, D), f32),
            sds(first_grad.shape[1:], f32),
            sds(biases.shape[1:], f32),
        ),
        in_specs=[ANY] * 8 + [VMEM] + [ANY] * 5 + [VMEM] * 2,
        out_specs=(VMEM,) * 7,
        scratch_shapes=[
            vmem((tok, D), bf),
            vmem((tok, D), f32),
            vmem((tok, D), bf),
            vmem((tok, D), bf),
            vmem((tok, D), bf),
            vmem((tok, 3 * D), bf),
            vmem((2,) + probs.shape[1:], bf),
            vmem((D, 3 * D), bf),
            vmem((D, D), bf),
            vmem((slots, D), bf),
            vmem((tok, slots), bf),
            vmem((tok, D), bf),
            vmem((tok, D), bf),
            vmem((2, D, D), bf),
            vmem((2, D, D), bf),
            vmem((D, D), bf),
            vmem((n_seq,) + biases.shape[1:], f32),
            vmem((tok, D), f32),
            vmem((tok, D), bf),
            vmem((tok, 3 * D), bf),
            vmem((tok, D), bf),
            vmem((tok, D), bf),
            vmem((4, 2, 2, 2, 2, 4, 24, half), bf),
            vmem((4, 2, 2, 2, 4, 24, half), bf),
            vmem((4, 2, 2, 4, 24, half), bf),
            vmem((4, 2, 4, 24, half), bf),
            vmem((4, 2, 4, 24, half), bf),
            vmem((4, 16, D), f32),
            vmem((6, 16, D), f32),
            dma((10,)),
            dma((2,)),
            dma((4,)),
            dma((n_seq,)),
            dma((n_seq,)),
            dma((n_dp,)),
            dma((n_dp,)),
            dma((2,)),
            dma((2,)),
            dma,
            dma,
            dma((n_seq,)),
            dma((n_seq,)),
            dma((4, 11)),
            dma((4, 11)),
            dma((6,)),
            dma((6,)),
            dma((n_seq,)),
            dma((n_seq,)),
        ],
        compiler_params=pltpu.CompilerParams(
            collective_id=2, has_side_effects=True, vmem_limit_bytes=61 * 2**20
        ),
        cost_estimate=pl.CostEstimate(
            flops=10**10, bytes_accessed=5 * 10**7, transcendentals=10**6
        ),
        name="back",
    )(
        grad_h2,
        resid,
        x_row,
        dy_row,
        att,
        qkv,
        probs,
        packed,
        vectors,
        outs,
        outof,
        tokens,
        branch,
        first_grad,
        biases,
        router_grad,
    )


def front_kernel(
    n_dp,
    n_seq,
    cap,
    tokens_any,
    dy_any,
    w_qkv_any,
    w_out_any,
    first_any,
    second_any,
    router_in_ref,
    vectors_in_ref,
    order_ref,
    picks_ref,
    open_ref,
    bias1_ref,
    bias2_ref,
    h_block_any,
    resid_any,
    x_any,
    att_any,
    qkv_any,
    probs_any,
    packed_any,
    vectors_ref,
    router_ref,
    branch_any,
    into_any,
    outof_any,
    dy_slots_any,
    first_all,
    second_all,
    bias_all,
    wide_a,
    wide_b,
    packed,
    x_row,
    dy,
    mask_out,
    mask_in,
    qkv,
    att,
    probs,
    resid,
    branch,
    h_two,
    into,
    outof,
    dy_sent,
    weights,
    bias_ref,
    load_sem,
    store_sem,
    probs_sem,
    own_sem,
    keep_sem,
    gs_sem,
    gr_sem,
    xs_sem,
    xr_sem,
    ms_sem,
    mr_sem,
    ds_sem,
    dr_sem,
    es_sem,
    er_sem,
    bs_sem,
    br_sem,
    hs_sem,
    hr_sem,
):
    bf, f32, i32 = jnp.bfloat16, jnp.float32, jnp.int32
    dp, seq = lax.axis_index("dp"), lax.axis_index("seq")
    z, y, x, c = split_axes()
    tok = x_row.shape[0]
    pos, held, slots = tok // n_seq, into.shape[0] // n_dp, into.shape[0]
    core_peer, x_peer = (dp, x * 2 + 1 - c), (dp, (1 - x) * 2 + c)
    y_peer = (z * 2 + 1 - y, seq)
    z_peer = lambda step: (lax.rem(z + step, 4) * 2 + y, seq)
    wide = (wide_a, wide_b)
    axes = (((x, x_peer), (y, y_peer)), ((y, y_peer), (x, x_peer)))
    mine = [wide[h].at[c, axes[h][0][0], axes[h][1][0], z] for h in range(2)]
    shard = [
        pltpu.make_async_copy(a, b, load_sem.at[i])
        for i, (a, b) in enumerate(
            (
                (w_qkv_any.at[:, : 2 * D], mine[0].at[:, 128:]),
                (w_qkv_any.at[:, 2 * D :], mine[1].at[:, :D]),
                (w_out_any, mine[1].at[:, D:]),
                (dy_any, dy),
                (tokens_any.at[rows_of(seq, pos)], x_row.at[rows_of(seq, pos)]),
            )
        )
    ]
    own_w = [
        pltpu.make_async_copy(ref, weights.at[j, seq], own_sem.at[j])
        for j, ref in enumerate((first_any, second_any))
    ]
    for copy in shard + own_w:
        copy.start()
    unit = lambda rows, shift: (
        lax.broadcasted_iota(i32, (rows, 128), 0) + shift
        == lax.broadcasted_iota(i32, (rows, 128), 1)
    ).astype(f32).astype(bf)
    narrow = nn(router_in_ref[...], unit(n_dp, 0)) + tn(vectors_in_ref[...], unit(8, n_dp))
    wide_a[c, x, y, z, :, :128] = narrow.astype(bf)

    def column(block):
        turned = jnp.concatenate([block.astype(f32)] * 2, axis=0).T
        return jnp.concatenate([turned[:, r : r + 1] for r in range(n_seq)], axis=0)

    order, valid = column(order_ref[...]), column(open_ref[...])
    ids = [column(picks_ref[k]).astype(i32) for k in range(2)]
    mask_out[...] = jnp.broadcast_to(valid, mask_out.shape).astype(bf)
    spots = lax.broadcasted_iota(i32, (bias2_ref.shape[1], D), 1)
    here = lax.broadcasted_iota(i32, spots.shape, 0) + seq * bias2_ref.shape[1]
    placed = nn(bias2_ref[...], (spots == here).astype(f32).astype(bf))
    bias_ref[...] = jnp.concatenate(
        [bias1_ref[...].astype(f32), placed, jnp.zeros((14, D), f32)], axis=0
    )
    for copy in shard[:3]:
        copy.wait()
    greet(n_dp, n_seq)
    seq_peers = [(step, lax.rem(seq + step, n_seq)) for step in range(1, n_seq)]

    def gather(h, stage):
        (f, f_peer), (g, g_peer) = axes[h]
        sems = lambda k: (gs_sem.at[h, k], gr_sem.at[h, k])
        same = lambda ref, k, peer: remote(ref, ref, *sems(k), peer)
        if stage == 0:
            return [same(mine[h], step, z_peer(step)) for step in range(1, 4)]
        if stage == 1:
            return [same(wide[h].at[c, f, g], 4, g_peer)]
        return [same(wide[h].at[c, f], 5, f_peer)]

    def hand_over(h, stage):
        (f, _), (g, _) = axes[h]
        ref = (wide[h].at[c, f, g], wide[h].at[c, f, 1 - g], wide[h].at[c, 1 - f])[stage]
        return remote(ref, ref, gs_sem.at[h, 6 + stage], gr_sem.at[h, 6 + stage], core_peer)

    def gather_take(stage):
        for h in range(2):
            for copy in gather(h, stage):
                copy.wait_recv()
            if stage < 2:
                gather(h, stage + 1)[0].start()
            hand_over(h, stage).start()

    for h in range(2):
        for copy in gather(h, 0):
            copy.start()
    exchange = []
    for step, to in seq_peers:
        for source, target, sems in (
            (tokens_any, x_row, (xs_sem, xr_sem)),
            (mask_out, mask_in, (ms_sem, mr_sem)),
        ):
            exchange.append(
                remote(
                    source.at[rows_of(to, pos)],
                    target.at[rows_of(seq, pos)],
                    sems[0].at[step],
                    sems[1].at[step],
                    (dp, to),
                )
            )
    for copy in exchange:
        copy.start()
    mask_in[rows_of(seq, pos), :] = mask_out[rows_of(seq, pos), :]
    biases = [
        remote(bias_ref, bias_all.at[seq], bs_sem.at[step], br_sem.at[step], (dp, to))
        for step, to in seq_peers
    ]
    for copy in biases:
        copy.start()
    bias_all[seq] = bias_ref[...]
    down = lax.broadcasted_iota(i32, (tok, tok), 0)
    across = lax.broadcasted_iota(i32, (tok, tok), 1)
    order_row = jnp.broadcast_to(order, (tok, 128)).T[:1].astype(i32)
    hit = order.astype(i32) == across
    rank_row = jnp.sum(jnp.where(hit, down.astype(f32), 0.0), axis=0, keepdims=True)
    hit = order_row == down
    rank_col = jnp.sum(jnp.where(hit, across.astype(f32), 0.0), axis=1, keepdims=True)
    earlier = (rank_row < rank_col).astype(bf)
    lane = lax.broadcasted_iota(i32, (tok, 128), 1)
    chosen = (lane == ids[0], lane == ids[1] + n_dp)
    counted = jnp.where(chosen[0] | chosen[1], 1.0, 0.0) * valid
    before = nn(earlier, counted.astype(bf))
    firsts = jnp.sum(jnp.where(lane == ids[0] + n_dp, 1.0, 0.0) * valid, axis=0, keepdims=True)
    spot = lax.broadcasted_iota(i32, (tok, slots), 1).astype(f32)
    spot_down = lax.broadcasted_iota(i32, (slots, tok), 0).astype(f32)
    hits, hits_down = [], []
    for k in range(2):
        slot = jnp.sum(jnp.where(chosen[k], before + firsts * k, 0.0), axis=1, keepdims=True)
        place = ids[k].astype(f32) * held + slot
        place = jnp.where((slot < cap) & (valid > 0.0), place, 1.0 * slots)
        place_row = jnp.broadcast_to(place, (tok, 128)).T[:1]
        hits.append(place == spot)
        hits_down.append(place_row == spot_down)
    outof[...] = jnp.where(hits[0] | hits[1], 1.0, 0.0).astype(bf)
    into[...] = jnp.where(hits_down[0] | hits_down[1], 1.0, 0.0).astype(bf)
    stores = [
        pltpu.make_async_copy(a, b, store_sem.at[i])
        for i, (a, b) in enumerate(
            (
                (into, into_any),
                (outof, outof_any),
                (x_row, x_any),
                (packed, packed_any),
                (qkv, qkv_any),
                (att, att_any),
                (branch, branch_any),
                (resid, resid_any),
            )
        )
    ]
    stores[0].start()
    stores[1].start()
    gather_take(0)
    shard[3].wait()
    dy_sent[...] = nn(into[...], dy[...]).astype(bf)
    gather_take(1)
    shard[4].wait()
    for copy in exchange:
        copy.wait_recv()
    normed, _ = norm_stats(x_row[...].astype(f32))
    stores[2].start()
    gather_take(2)
    experts_x, experts_c, experts_f, kept_w = [], [], [], []
    for j, target in enumerate((first_all, second_all)):
        far = (1 - x) * 2 + c
        held_w = weights.at[j]
        sems = lambda k: (es_sem.at[j, k], er_sem.at[j, k])
        own_w[j].wait()
        experts_x.append(remote(held_w.at[seq], held_w.at[seq], *sems(0), x_peer))
        experts_c.append(remote(held_w.at[seq], held_w.at[seq], *sems(1), core_peer))
        experts_f.append(remote(held_w.at[far], held_w.at[far], *sems(2), core_peer))
        kept_w.append([])
        for k, block in enumerate((seq, x * 2 + 1 - c, far, (1 - x) * 2 + 1 - c)):
            kept_w[j].append(
                pltpu.make_async_copy(held_w.at[block], target.at[block], keep_sem.at[j, k])
            )
        kept_w[j][0].start()
    for copy in experts_x:
        copy.start()
    dy_copies = []
    for step in range(n_dp - 1, 0, -1):
        to = other(dp, step)
        dy_copies.append(
            remote(
                dy_sent.at[rows_of(to, held)],
                dy_slots_any.at[rows_of(dp, held)],
                ds_sem.at[step],
                dr_sem.at[step],
                (to, seq),
            )
        )
    for copy in dy_copies:
        copy.start()
    own_dy = pltpu.make_async_copy(
        dy_sent.at[rows_of(dp, held)], dy_slots_any.at[rows_of(dp, held)], own_sem.at[2]
    )
    own_dy.start()
    for stage in range(3):
        for h in range(2):
            hand_over(h, stage).wait_recv()
    for copy in experts_c:
        copy.start()
    starts = ((128, 0), (128 + D, D), (0, 2 * D), (D, 3 * D))

    def assemble(half, lanes, to=None):
        for oc in range(2):
            for ox in range(2):
                for oy in range(2):
                    for oz in range(4):
                        at = ((oz * 2 + oy) * 2 + ox) * 2 + oc
                        f, g = (ox, oy) if half == 0 else (oy, ox)
                        yield at, wide[half][oc, f, g, oz, :, lanes]

    narrow = dict(assemble(0, slice(0, 128)))
    narrow = jnp.concatenate([narrow[i].astype(f32) for i in range(n_dp * n_seq)], axis=0)
    router_ref[...] = narrow.astype(bf)
    vectors = narrow.T[8:16]
    vectors_ref[...] = vectors
    vec = lambda i: vectors[i : i + 1]
    for k, (start, col) in enumerate(starts):
        blocks = dict(assemble(k // 2, slice(start, start + D)))
        packed[:, col : col + D] = jnp.concatenate(
            [blocks[i].astype(f32) for i in range(n_dp * n_seq)], axis=0
        ).astype(bf)
    stores[3].start()
    h_one = (normed * vec(0) + vec(1)).astype(bf)
    for k in range(3):
        qkv[:, D * k : D * k + D] = nn(h_one, packed[:, D * k : D * k + D]).astype(bf)
    stores[4].start()
    lane = lax.broadcasted_iota(i32, (1, 128), 1)
    closed = jnp.where(mask_in[...].astype(f32) > 0.0, 0.0, -1e30).astype(bf)
    keep_out = lambda head: pltpu.make_async_copy(
        probs.at[head % 2], probs_any.at[head], probs_sem.at[head % 2]
    )
    for pair in range(HEADS // 2):
        q, k, v = (qkv[:, D * i + 128 * pair : D * i + 128 * pair + 128] for i in range(3))
        q = q * jnp.asarray(HEAD ** (-0.5), bf)
        out = jnp.zeros(q.shape, f32)
        for h in range(2):
            head = 2 * pair + h
            keep = (lane // HEAD == h).astype(bf)
            spare = (lane == HEAD * (1 - h)).astype(bf)
            scores = nt(q * keep + spare, k * keep + closed * spare)
            soft = jnp.exp(scores - jnp.max(scores, axis=-1, keepdims=True))
            soft = soft * (1.0 / jnp.sum(soft, axis=-1, keepdims=True))
            if head >= 2:
                keep_out(head - 2).wait()
            low = soft.astype(bf)
            probs[head % 2] = low
            keep_out(head).start()
            out = out + nn(low, v * keep)
        att[:, 128 * pair : 128 * pair + 128] = out.astype(bf)
    stores[5].start()
    made = nn(att[...], packed[:, 3 * D :]) + vec(2)
    branch[...] = made.astype(bf)
    resid[...] = x_row[...].astype(f32) + made
    normed, _ = norm_stats(resid[...])
    h_two[...] = (normed * vec(3) + vec(4)).astype(bf)
    to_blocks = [
        remote(
            h_two.at[rows_of(to, pos)],
            h_block_any.at[rows_of(seq, pos)],
            hs_sem.at[step],
            hr_sem.at[step],
            (dp, to),
        )
        for step, to in seq_peers
    ]
    for copy in to_blocks:
        copy.start()
    own_h = pltpu.make_async_copy(
        h_two.at[rows_of(seq, pos)], h_block_any.at[rows_of(seq, pos)], own_sem.at[3]
    )
    own_h.start()
    stores[6].start()
    stores[7].start()
    for j in range(2):
        experts_x[j].wait_recv()
        experts_f[j].start()
        kept_w[j][2].start()
        experts_c[j].wait_recv()
        kept_w[j][1].start()
    for j in range(2):
        experts_f[j].wait_recv()
        kept_w[j][3].start()
    for copy in to_blocks + dy_copies + biases:
        copy.wait_recv()
    keep_out(HEADS - 2).wait()
    keep_out(HEADS - 1).wait()
    for copy in stores + kept_w[0] + kept_w[1] + [own_dy, own_h]:
        copy.wait()
    for copy in exchange + to_blocks + dy_copies + biases + experts_x + experts_c + experts_f:
        copy.wait_send()
    for h in range(2):
        for stage in range(3):
            hand_over(h, stage).wait_send()
            for copy in gather(h, stage):
                copy.wait_send()


def front(
    n_dp,
    n_seq,
    cap,
    held,
    tokens,
    dy,
    w_qkv,
    w_out,
    first,
    second,
    w_router,
    vectors,
    order,
    picks,
    mask,
    bias1,
    bias2,
):
    bf, f32 = jnp.bfloat16, jnp.float32
    sds, dma, vmem = jax.ShapeDtypeStruct, pltpu.SemaphoreType.DMA, pltpu.VMEM
    tok = tokens.shape[0]
    slots = n_dp * held
    own = D // (n_dp * n_seq)
    block = (tok, D)
    return pl.pallas_call(
        functools.partial(front_kernel, n_dp, n_seq, cap),
        out_shape=(
            sds(block, bf),
            sds(block, f32),
            sds(block, bf),
            sds(block, bf),
            sds((tok, 3 * D), bf),
            sds((HEADS, tok, tok), bf),
            sds((D, 4 * D), bf),
            sds((8, D), f32),
            sds((D, 128), bf),
            sds(block, bf),
            sds((slots, tok), bf),
            sds((tok, slots), bf),
            sds((slots, D), bf),
            sds((n_seq,) + first.shape, bf),
            sds((n_seq,) + second.shape, bf),
            sds((n_seq, 16, D), f32),
        ),
        in_specs=[ANY] * 6 + [VMEM] * 7,
        out_specs=(ANY,) * 7 + (VMEM,) * 2 + (ANY,) * 6 + (VMEM,),
        scratch_shapes=[
            vmem((2, 2, 2, 4, own, 128 + 2 * D), bf),
            vmem((2, 2, 2, 4, own, 2 * D), bf),
            vmem((D, 4 * D), bf),
            vmem(block, bf),
            vmem(block, bf),
            vmem((tok, 128), bf),
            vmem((tok, 128), bf),
            vmem((tok, 3 * D), bf),
            vmem(block, bf),
            vmem((2, tok, tok), bf),
            vmem(block, f32),
            vmem(block, bf),
            vmem(block, bf),
            vmem((slots, tok), bf),
            vmem((tok, slots), bf),
            vmem((slots, D), bf),
            vmem((2, n_seq) + first.shape, bf),
            vmem((16, D), f32),
            dma((5,)),
            dma((8,)),
            dma((2,)),
            dma((4,)),
            dma((2, 4)),
            dma((2, 9)),
            dma((2, 9)),
            dma((n_seq,)),
            dma((n_seq,)),
            dma((n_seq,)),
            dma((n_seq,)),
            dma((n_dp,)),
            dma((n_dp,)),
            dma((2, 3)),
            dma((2, 3)),
            dma((n_seq,)),
            dma((n_seq,)),
            dma((n_seq,)),
            dma((n_seq,)),
        ],
        compiler_params=pltpu.CompilerParams(
            collective_id=3, has_side_effects=True, vmem_limit_bytes=61 * 2**20
        ),
        cost_estimate=pl.CostEstimate(
            flops=6 * 10**9, bytes_accessed=5 * 10**7, transcendentals=4 * 10**6
        ),
        name="front",
    )(
        tokens,
        dy,
        w_qkv,
        w_out,
        first,
        second,
        w_router,
        vectors,
        order,
        picks,
        mask,
        bias1,
        bias2,
    )


def shards_rows(
    tokens,
    cotangent,
    pad_mask,
    expert_ids,
    priority,
    ln1_gain,
    ln1_shift,
    w_qkv,
    w_out,
    out_bias,
    ln2_gain,
    ln2_shift,
    w_router,
    w_in,
    in_bias,
    w_exp_out,
    exp_out_bias,
):
    rows_dev, pos_dev = pad_mask.shape
    tok = rows_dev * pos_dev
    experts = w_router.shape[1]
    cap = (21 * tok + 10 * experts - 1) // (10 * experts)
    n_dp, n_seq = lax.axis_size("dp"), lax.axis_size("seq")
    seq, own = lax.axis_index("seq"), D // (n_dp * n_seq)
    bf, f32 = jnp.bfloat16, jnp.float32
    held = -(-cap // 16) * 16
    flat, dy_block = tokens.reshape(tok, D), cotangent.reshape(tok, D)
    (
        h_block,
        resid,
        x_row,
        attended,
        qkv,
        probs,
        packed,
        vectors,
        router,
        branch,
        into,
        outof,
        dy_slots,
        first,
        second,
        bias,
    ) = front(
        n_dp,
        n_seq,
        cap,
        held,
        flat,
        dy_block,
        w_qkv,
        w_out,
        w_in[0],
        w_exp_out[0],
        w_router,
        jnp.stack([ln1_gain, ln1_shift, out_bias, ln2_gain, ln2_shift] + [ln2_shift] * 3),
        priority,
        jnp.moveaxis(expert_ids, 2, 0),
        pad_mask,
        in_bias,
        exp_out_bias,
    )
    grad_h2, made, first_grad, second_grad, router_grad, bias_grad, dy_row, branch_block = moe(
        h_block, into, outof, dy_slots, first, second, bias, router, dy_block, branch, experts
    )
    out, tokens_grad, qkv_grad, out_grad, small, first_grad, bias_grad = back(
        n_dp,
        n_seq,
        grad_h2,
        resid,
        x_row,
        dy_row,
        attended,
        qkv,
        probs,
        packed,
        vectors,
        made,
        outof,
        flat,
        branch_block,
        first_grad,
        bias_grad,
        router_grad,
    )
    small = lax.dynamic_slice_in_dim(
        small, (lax.axis_index("dp") * n_seq + seq) * own, own, 1
    )
    return (
        out.reshape(rows_dev, pos_dev, D),
        tokens_grad.reshape(rows_dev, pos_dev, D),
        small[0],
        small[1],
        qkv_grad,
        out_grad,
        small[2],
        small[3],
        small[4],
        small[8 : 8 + experts].T,
        first_grad[None],
        bias_grad[None, 0],
        second_grad[None],
        lax.dynamic_slice_in_dim(bias_grad[None, 8], seq * exp_out_bias.shape[1], exp_out_bias.shape[1], 1),
    )


def shards(*args):
    block_rows, local_experts, n_dp = args[2].shape[0], args[13].shape[0], lax.axis_size("dp")
    if block_rows == lax.axis_size("seq") and local_experts == 1 and n_dp == 8:
        return shards_rows(*args)
    return shards_general(*args)


def solution(mesh):
    return jax.shard_map(
        shards,
        mesh=mesh,
        in_specs=(
            P("dp", "seq", None),
            P("dp", "seq", None),
            P("dp", "seq"),
            P("dp", "seq", None),
            P("dp", "seq"),
            P(("dp", "seq")),
            P(("dp", "seq")),
            P(("dp", "seq"), None),
            P(("dp", "seq"), None),
            P(("dp", "seq")),
            P(("dp", "seq")),
            P(("dp", "seq")),
            P(("dp", "seq"), None),
            P("dp", None, "seq"),
            P("dp", "seq"),
            P("dp", "seq", None),
            P("dp", "seq"),
        ),
        out_specs=(
            P("dp", "seq", None),
            P("dp", "seq", None),
            P(("dp", "seq")),
            P(("dp", "seq")),
            P(("dp", "seq"), None),
            P(("dp", "seq"), None),
            P(("dp", "seq")),
            P(("dp", "seq")),
            P(("dp", "seq")),
            P(("dp", "seq"), None),
            P("dp", None, "seq"),
            P("dp", "seq"),
            P("dp", "seq", None),
            P("dp", "seq"),
        ),
        check_vma=False,
    )
```

```python
import functools

import jax
import jax.numpy as jnp
from jax import lax
from jax.experimental import pallas as pl
from jax.experimental.pallas import tpu as pltpu
from jax.sharding import PartitionSpec as P

D = 768
HEADS = 12
HEAD = 64


norm_eps = 1e-06


def norm_forward(values, norm_gain, norm_shift):
    average = jnp.mean(values, axis=-1, keepdims=True)
    centred = values - average
    inv_scale = lax.rsqrt(jnp.mean(centred * centred, axis=-1, keepdims=True) + norm_eps)
    normed = centred * inv_scale
    return (
        normed * norm_gain.astype(jnp.float32) + norm_shift.astype(jnp.float32),
        normed,
        inv_scale,
    )


def norm_backward(grad_output, normed, inv_scale, norm_gain):
    scaled = grad_output * norm_gain.astype(jnp.float32)
    grad_input = inv_scale * (
        scaled
        - jnp.mean(scaled, axis=-1, keepdims=True)
        - normed * jnp.mean(scaled * normed, axis=-1, keepdims=True)
    )
    return (
        grad_input,
        jnp.sum(grad_output * normed, axis=(0, 1)),
        jnp.sum(grad_output, axis=(0, 1)),
    )


def gelu_slope(values):
    return (
        0.5 * (1.0 + lax.erf(values * 0.7071067811865476))
        + values * jnp.exp(-0.5 * values * values) * 0.3989422804014327
    )


def slot_ranks(order, picks, valid, experts, capacity):
    count = order.shape[0]
    index = jnp.arange(count, dtype=jnp.int32)
    rank = jnp.sum(jnp.where(order[:, None] == index[None, :], index[:, None], 0), axis=0)
    earlier = (rank[None, :] < rank[:, None]).astype(jnp.bfloat16)
    chosen = picks[:, :, None] == jnp.arange(experts, dtype=jnp.int32)
    counted = chosen.astype(jnp.float32) * valid.astype(jnp.float32)[:, None, None]
    before = jnp.dot(
        earlier,
        counted.reshape(count, 2 * experts).astype(jnp.bfloat16),
        preferred_element_type=jnp.float32,
    ).reshape(count, 2, experts)
    firsts = jnp.sum(counted[:, 0], axis=0)
    before = before + jnp.stack([jnp.zeros_like(firsts), firsts])[None]
    slot = jnp.sum(jnp.where(chosen, before, 0.0), axis=2).astype(jnp.int32)
    kept = (valid[:, None] > 0) & (slot < capacity)
    return kept, slot


def pair_slots(order, expert_picks, valid_flags, expert_count, capacity):
    kept, slot = slot_ranks(order, expert_picks, valid_flags, expert_count, capacity)
    tokens = jnp.arange(order.shape[0], dtype=jnp.int32)
    return (
        jnp.concatenate([tokens, tokens]),
        expert_picks.T.reshape(-1),
        slot.T.reshape(-1),
        kept.T.reshape(-1).astype(jnp.int32),
    )


def shards_general(
    tokens,
    cotangent,
    pad_mask,
    expert_ids,
    priority,
    ln1_gain,
    ln1_shift,
    w_qkv,
    w_out,
    out_bias,
    ln2_gain,
    ln2_shift,
    w_router,
    w_in,
    in_bias,
    w_exp_out,
    exp_out_bias,
):
    rows_dev, pos_dev = pad_mask.shape
    tok_count = rows_dev * pos_dev
    expert_count = w_router.shape[1]
    local_experts = w_in.shape[0]
    capacity = (21 * tok_count + 10 * expert_count - 1) // (10 * expert_count)
    scale_factor = HEAD ** (-0.5)
    gain_one, shift_one, qkv_weight, out_weight, out_shift, gain_two, shift_two, router_weight = (
        lax.all_gather(ln1_gain, ("dp", "seq"), axis=0, tiled=True),
        lax.all_gather(ln1_shift, ("dp", "seq"), axis=0, tiled=True),
        lax.all_gather(w_qkv, ("dp", "seq"), axis=0, tiled=True),
        lax.all_gather(w_out, ("dp", "seq"), axis=0, tiled=True),
        lax.all_gather(out_bias, ("dp", "seq"), axis=0, tiled=True),
        lax.all_gather(ln2_gain, ("dp", "seq"), axis=0, tiled=True),
        lax.all_gather(ln2_shift, ("dp", "seq"), axis=0, tiled=True),
        lax.all_gather(w_router, ("dp", "seq"), axis=0, tiled=True),
    )
    x_float = tokens.astype(jnp.float32)
    h_one, normed_one, inv_one = norm_forward(x_float, gain_one, shift_one)
    h_one_low = h_one.astype(jnp.bfloat16)
    qkv_low = jnp.einsum(
        "rpd,de->rpe", h_one_low, qkv_weight, preferred_element_type=jnp.float32
    ).astype(jnp.bfloat16)
    queries = qkv_low[:, :, :D].reshape(rows_dev, pos_dev, HEADS, HEAD)
    kv_all, mask_all = (
        lax.all_gather(qkv_low[:, :, D:], "seq", axis=1, tiled=True),
        lax.all_gather(pad_mask.astype(jnp.bfloat16), "seq", axis=1, tiled=True),
    )
    full_len = kv_all.shape[1]
    keys_all = kv_all[:, :, :D].reshape(rows_dev, full_len, HEADS, HEAD)
    values_all = kv_all[:, :, D:].reshape(rows_dev, full_len, HEADS, HEAD)
    key_open = (mask_all > 0)[:, None, None, :]

    def score_block():
        raw_scores = (
            jnp.einsum("rphd,rkhd->rhpk", queries, keys_all, preferred_element_type=jnp.float32)
            * scale_factor
        )
        return jnp.where(key_open, raw_scores, -1e30)

    scores = score_block()
    row_max = jnp.max(scores, axis=-1, keepdims=True)
    exp_scores = jnp.exp(scores - row_max)
    row_total = jnp.sum(exp_scores, axis=-1, keepdims=True)
    log_total = row_max + jnp.log(row_total)
    probs_low = (exp_scores / row_total).astype(jnp.bfloat16)
    attended = (
        jnp.einsum("rhpk,rkhd->rphd", probs_low, values_all, preferred_element_type=jnp.float32)
        .reshape(rows_dev, pos_dev, D)
        .astype(jnp.bfloat16)
    )
    branch = jnp.einsum(
        "rpd,de->rpe", attended, out_weight, preferred_element_type=jnp.float32
    ) + out_shift.astype(jnp.float32)
    resid = x_float + branch
    h_two, normed_two, inv_two = norm_forward(resid, gain_two, shift_two)
    flat_low = h_two.astype(jnp.bfloat16).reshape(tok_count, D)
    logits = jnp.dot(flat_low, router_weight, preferred_element_type=jnp.float32)
    router_probs = jax.nn.softmax(logits, axis=-1)
    token_pairs, expert_pairs, slot_index, kept_flags = pair_slots(
        priority.reshape(-1),
        expert_ids.reshape(tok_count, 2),
        pad_mask.reshape(-1),
        expert_count,
        capacity,
    )
    dummy_row = expert_count * capacity
    destination = jnp.where(kept_flags > 0, expert_pairs * capacity + slot_index, dummy_row)
    kept_float = kept_flags.astype(jnp.float32)
    gate_pairs = router_probs[token_pairs, expert_pairs] * kept_float
    send_rows = (
        jnp.zeros((dummy_row + 1, D), jnp.bfloat16)
        .at[destination]
        .set(flat_low[token_pairs])[:-1]
        .reshape(expert_count, capacity, D)
    )
    received = lax.all_to_all(send_rows, "dp", split_axis=0, concat_axis=1, tiled=True)
    seq_index = lax.axis_index("seq")
    bias_cols = exp_out_bias.shape[1]
    rows_all = lax.all_gather(received, "seq", axis=1, tiled=True)
    pre_act = (
        jnp.einsum("erd,edf->erf", rows_all, w_in, preferred_element_type=jnp.float32)
        + in_bias.astype(jnp.float32)[:, None, :]
    )
    act_low = jax.nn.gelu(pre_act, approximate=False).astype(jnp.bfloat16)
    partial_out = jnp.einsum("erf,efd->erd", act_low, w_exp_out, preferred_element_type=jnp.float32)
    bias_full = lax.dynamic_update_slice_in_dim(
        jnp.zeros((local_experts, D), jnp.float32),
        exp_out_bias.astype(jnp.float32),
        seq_index * bias_cols,
        1,
    )
    partial_out = partial_out + bias_full[:, None, :]
    expert_out = lax.psum_scatter(
        partial_out.astype(jnp.bfloat16), "seq", scatter_dimension=1, tiled=True
    )
    returned_buf = lax.all_to_all(expert_out, "dp", split_axis=1, concat_axis=0, tiled=True)
    returned = jnp.concatenate(
        [returned_buf.reshape(-1, D), jnp.zeros((1, D), jnp.bfloat16)], axis=0
    )[destination].astype(jnp.float32)
    mixture = (
        jnp.zeros((tok_count, D), jnp.float32).at[token_pairs].add(gate_pairs[:, None] * returned)
    )
    block_output = (resid + mixture.reshape(rows_dev, pos_dev, D)).astype(jnp.bfloat16)
    grad_y = cotangent.astype(jnp.float32)
    grad_pairs = grad_y.reshape(tok_count, D)[token_pairs]
    grad_gates = jnp.sum(grad_pairs * returned, axis=-1) * kept_float
    grad_ret = (gate_pairs[:, None] * grad_pairs).astype(jnp.bfloat16)
    grad_send = (
        jnp.zeros((dummy_row + 1, D), jnp.bfloat16)
        .at[destination]
        .set(grad_ret)[:-1]
        .reshape(expert_count, capacity, D)
    )
    grad_recv = lax.all_to_all(grad_send, "dp", split_axis=0, concat_axis=1, tiled=True)
    grad_all = lax.all_gather(grad_recv, "seq", axis=1, tiled=True)
    pre_again = (
        jnp.einsum("erd,edf->erf", rows_all, w_in, preferred_element_type=jnp.float32)
        + in_bias.astype(jnp.float32)[:, None, :]
    )
    act_again = jax.nn.gelu(pre_again, approximate=False).astype(jnp.bfloat16)
    grad_act = jnp.einsum("erd,efd->erf", grad_all, w_exp_out, preferred_element_type=jnp.float32)
    grad_pre = (grad_act * gelu_slope(pre_again)).astype(jnp.bfloat16)
    w_exp_out_grad = jnp.einsum(
        "erf,erd->efd", act_again, grad_all, preferred_element_type=jnp.float32
    )
    bias_sums = jnp.sum(grad_all, axis=1, dtype=jnp.float32)
    exp_out_bias_grad = lax.dynamic_slice_in_dim(bias_sums, seq_index * bias_cols, bias_cols, 1)
    w_in_grad = jnp.einsum("erd,erf->edf", rows_all, grad_pre, preferred_element_type=jnp.float32)
    in_bias_grad = jnp.sum(grad_pre, axis=1, dtype=jnp.float32)
    grad_rows_part = jnp.einsum("erf,edf->erd", grad_pre, w_in, preferred_element_type=jnp.float32)
    grad_back = lax.psum_scatter(
        grad_rows_part.astype(jnp.bfloat16), "seq", scatter_dimension=1, tiled=True
    )
    grad_buf = lax.all_to_all(grad_back, "dp", split_axis=1, concat_axis=0, tiled=True)
    grad_rows_back = jnp.concatenate(
        [grad_buf.reshape(-1, D), jnp.zeros((1, D), jnp.bfloat16)], axis=0
    )[destination].astype(jnp.float32)
    grad_h2_experts = jnp.zeros((tok_count, D), jnp.float32).at[token_pairs].add(grad_rows_back)
    grad_probs = (
        jnp.zeros((tok_count, expert_count), jnp.float32)
        .at[token_pairs, expert_pairs]
        .add(grad_gates)
    )
    grad_logits = (
        router_probs * (grad_probs - jnp.sum(router_probs * grad_probs, axis=-1, keepdims=True))
    ).astype(jnp.bfloat16)
    router_grad = jnp.einsum("td,te->de", flat_low, grad_logits, preferred_element_type=jnp.float32)
    grad_h2 = grad_h2_experts + jnp.einsum(
        "te,de->td", grad_logits, router_weight, preferred_element_type=jnp.float32
    )
    grad_resid_norm, gain_two_grad, shift_two_grad = norm_backward(
        grad_h2.reshape(rows_dev, pos_dev, D), normed_two, inv_two, gain_two
    )
    grad_resid = grad_y + grad_resid_norm
    grad_branch = grad_resid.astype(jnp.bfloat16)
    out_weight_grad = jnp.einsum(
        "rpd,rpe->de", attended, grad_branch, preferred_element_type=jnp.float32
    )
    out_shift_grad = jnp.sum(grad_branch, axis=(0, 1), dtype=jnp.float32)
    grad_attended = jnp.einsum(
        "rpe,de->rpd", grad_branch, out_weight, preferred_element_type=jnp.float32
    ).astype(jnp.bfloat16)
    grad_att_heads = grad_attended.reshape(rows_dev, pos_dev, HEADS, HEAD)
    scores_again = score_block()
    probs_again = jnp.exp(scores_again - log_total)
    probs_again_low = probs_again.astype(jnp.bfloat16)
    grad_probs_att = jnp.einsum(
        "rphd,rkhd->rhpk", grad_att_heads, values_all, preferred_element_type=jnp.float32
    )
    row_delta = jnp.sum(probs_again * grad_probs_att, axis=-1, keepdims=True)
    grad_scores = (probs_again * (grad_probs_att - row_delta)).astype(jnp.bfloat16)
    grad_queries = (
        jnp.einsum("rhpk,rkhd->rphd", grad_scores, keys_all, preferred_element_type=jnp.float32)
        * scale_factor
    ).reshape(rows_dev, pos_dev, D)
    grad_keys = (
        jnp.einsum("rhpk,rphd->rkhd", grad_scores, queries, preferred_element_type=jnp.float32)
        * scale_factor
    ).reshape(rows_dev, full_len, D)
    grad_values = jnp.einsum(
        "rhpk,rphd->rkhd", probs_again_low, grad_att_heads, preferred_element_type=jnp.float32
    ).reshape(rows_dev, full_len, D)
    grad_kv = lax.psum_scatter(
        jnp.concatenate([grad_keys, grad_values], axis=-1).astype(jnp.bfloat16),
        "seq",
        scatter_dimension=1,
        tiled=True,
    )
    grad_qkv = jnp.concatenate([grad_queries.astype(jnp.bfloat16), grad_kv], axis=-1)
    qkv_weight_grad = jnp.einsum(
        "rpd,rpe->de", h_one_low, grad_qkv, preferred_element_type=jnp.float32
    )
    grad_h1 = jnp.einsum("rpe,de->rpd", grad_qkv, qkv_weight, preferred_element_type=jnp.float32)
    grad_x_norm, gain_one_grad, shift_one_grad = norm_backward(
        grad_h1, normed_one, inv_one, gain_one
    )
    tokens_grad = (grad_resid + grad_x_norm).astype(jnp.bfloat16)
    dense_parts = (
        lax.psum_scatter(gain_one_grad, ("dp", "seq"), scatter_dimension=0, tiled=True),
        lax.psum_scatter(shift_one_grad, ("dp", "seq"), scatter_dimension=0, tiled=True),
        lax.psum_scatter(qkv_weight_grad, ("dp", "seq"), scatter_dimension=0, tiled=True),
        lax.psum_scatter(out_weight_grad, ("dp", "seq"), scatter_dimension=0, tiled=True),
        lax.psum_scatter(out_shift_grad, ("dp", "seq"), scatter_dimension=0, tiled=True),
        lax.psum_scatter(gain_two_grad, ("dp", "seq"), scatter_dimension=0, tiled=True),
        lax.psum_scatter(shift_two_grad, ("dp", "seq"), scatter_dimension=0, tiled=True),
        lax.psum_scatter(router_grad, ("dp", "seq"), scatter_dimension=0, tiled=True),
    )
    return (
        block_output,
        tokens_grad,
        dense_parts[0],
        dense_parts[1],
        dense_parts[2],
        dense_parts[3],
        dense_parts[4],
        dense_parts[5],
        dense_parts[6],
        dense_parts[7],
        w_in_grad,
        in_bias_grad,
        w_exp_out_grad,
        exp_out_bias_grad,
    )


MESH = pl.DeviceIdType.MESH
VMEM = pl.BlockSpec(memory_space=pltpu.VMEM)
ANY = pl.BlockSpec(memory_space=pl.ANY)
ERF = (0.1274147955, -0.142248368, 0.7107068705, -0.7265760135, 0.5307027145)


def nn(a, b):
    return lax.dot_general(a, b, (((1,), (0,)), ((), ())), preferred_element_type=jnp.float32)


def nt(a, b):
    return lax.dot_general(a, b, (((1,), (1,)), ((), ())), preferred_element_type=jnp.float32)


def tn(a, b):
    return lax.dot_general(a, b, (((0,), (0,)), ((), ())), preferred_element_type=jnp.float32)


def gelu_parts(v):
    bell = jnp.exp(v * v * -0.5)
    t = 1.0 / (jnp.abs(v) * (0.3275911 * 0.7071067811865476) + 1.0)
    a, b, c, d, e = ERF
    tail = ((((e * t + d) * t + c) * t + b) * t + a) * t * bell
    cdf = jnp.where(v < 0.0, tail, 1.0 - tail)
    return v * cdf, cdf + v * (bell * 0.3989422804014327)


def other(me, step):
    bit = lambda k: lax.rem(me // k + step // k, 2) * k
    return bit(4) + bit(2) + bit(1)


def moe_kernel(
    experts,
    h_ref,
    into_ref,
    from_ref,
    dy_ref,
    first_any,
    second_any,
    bias_ref,
    router_ref,
    dy_any,
    branch_any,
    grad_ref,
    outs_ref,
    first_grad_any,
    second_grad_ref,
    router_grad_ref,
    bias_grad_ref,
    dy_row_any,
    branch_block_any,
    sent,
    rows,
    go,
    act,
    gp,
    back_sent,
    back,
    logit_grad,
    first,
    second,
    w_sem,
    send_sem,
    recv_sem,
    send_sem2,
    recv_sem2,
    send_sem3,
    recv_sem3,
    own_sem,
    grad_sem,
    recv_e,
    recv_x,
    es_sem,
    er_sem,
):
    n = experts
    cap = dy_ref.shape[0] // n
    bf, f32 = jnp.bfloat16, jnp.float32
    blocks = first.shape[0]
    me, seq = lax.axis_index("dp"), lax.axis_index("seq")
    n_seq = blocks
    pos = h_ref.shape[0] // n_seq
    load1 = pltpu.make_async_copy(first_any, first, w_sem.at[0])
    load2 = pltpu.make_async_copy(second_any, second, w_sem.at[1])
    load1.start()
    load2.start()
    at = lambda i: pl.ds(pl.multiple_of(i * cap, cap), cap)
    greet(n, n_seq)

    def dispatch(step, source, target, sems):
        to = other(me, step)
        return pltpu.make_async_remote_copy(
            source.at[at(to)],
            target.at[at(me)],
            sems[0].at[step],
            sems[1].at[step],
            device_id=(to, seq),
            device_id_type=MESH,
        )

    out_sems, back_sems = (send_sem, recv_sem), (send_sem2, recv_sem2)

    for step in (1, 4, 5, 2, 3, 6, 7):
        to = other(me, step)
        sent[at(to), :] = nn(into_ref[at(to), :], h_ref[...]).astype(bf)
        dispatch(step, sent, rows, out_sems).start()

    rows[at(me), :] = nn(into_ref[at(me), :], h_ref[...]).astype(bf)
    swaps, own_swaps = [], []
    for k, (source, target) in enumerate(((dy_any, dy_row_any), (branch_any, branch_block_any))):
        here = rows_of(seq, pos)
        own_swaps.append(pltpu.make_async_copy(source.at[here], target.at[here], own_sem.at[k]))
        for step in range(1, n_seq):
            to = lax.rem(seq + step, n_seq)
            swaps.append(
                remote(
                    source.at[rows_of(to, pos)],
                    target.at[here],
                    send_sem3.at[k, step],
                    recv_sem3.at[k, step],
                    (me, to),
                )
            )
    for copy in swaps + own_swaps:
        copy.start()
    load1.wait()
    load2.wait()
    pair = 2 * cap
    lane = lax.broadcasted_iota(jnp.int32, (pair, 128), 1)
    second_bias = jnp.sum(bias_ref[:, 1, :], axis=0, keepdims=True)

    @pl.loop(0, n // 2)
    def _(plane):
        group = rows_of(other(me, 2 * plane) // 2, pair)

        @pl.when(plane > 0)
        def _():
            dispatch(2 * plane, sent, rows, out_sems).wait_recv()

        dispatch(2 * plane + 1, sent, rows, out_sems).wait_recv()
        x = rows[group, :]
        dy = dy_ref[group, :].astype(f32)
        logits = jnp.where(lane < n, nn(x, router_ref[...]), -1e30)
        probs = jnp.exp(logits - jnp.max(logits, axis=-1, keepdims=True))
        probs = probs / jnp.sum(probs, axis=-1, keepdims=True)
        mine = (lane == me).astype(f32)
        gate = jnp.sum(probs * mine, axis=-1, keepdims=True)
        grad_out = (gate * dy).astype(bf)
        go[group, :] = grad_out

        def block(q, sums):
            out, grad_row = sums
            value, slope = gelu_parts(nn(x, first[q]) + bias_ref[q, 0:1])
            value = value.astype(bf)
            act[q, group, :] = value
            grad_pre = (nt(grad_out, second[q]) * slope).astype(bf)
            gp[q, group, :] = grad_pre
            return out + nn(value, second[q]), grad_row + nt(grad_pre, first[q])

        zero = jnp.zeros((pair, x.shape[1]), f32)
        out, grad_row = lax.fori_loop(0, blocks, block, (zero, zero), unroll=True)
        made = (out + second_bias).astype(bf).astype(f32)
        grad_gate = jnp.sum(dy * made, axis=-1, keepdims=True)
        grad_logits = (grad_gate * gate * (mine - probs)).astype(bf)
        logit_grad[group, :] = grad_logits
        grad_row = (grad_row + nt(grad_logits, router_ref[...])).astype(bf)
        outs_ref[group, :] = (gate * made).astype(bf)
        back_sent[group, :] = grad_row

        @pl.when(plane > 0)
        def _():
            dispatch(2 * plane, back_sent, back, back_sems).start()

        dispatch(2 * plane + 1, back_sent, back, back_sems).start()

    back[at(me), :] = back_sent[at(me), :]
    _, _, x_at, c_at = split_axes()
    core_peer, x_peer = (me, x_at * 2 + 1 - c_at), (me, (1 - x_at) * 2 + c_at)
    far, near = (1 - x_at) * 2 + c_at, seq

    def to_core(k):
        side = lax.rem(x_at + 1 + k, 2)
        return remote(
            second.at[side * 2 + 1 - c_at], recv_e.at[k], es_sem.at[k], er_sem.at[k], core_peer
        )

    to_x = remote(second.at[far], recv_x, es_sem.at[2], er_sem.at[2], x_peer)

    @pl.loop(0, blocks)
    def _(k):
        q = lax.rem(x_at + 1 + k // 2, 2) * 2 + lax.rem(c_at + 1 + k, 2)
        second[q] = tn(act[q], go[...]).astype(bf)

        @pl.when(lax.rem(k, 2) == 0)
        def _():
            to_core(k // 2).start()

    to_core(0).wait_recv()
    second[far] = (second[far].astype(f32) + recv_e[0].astype(f32)).astype(bf)
    to_x.start()
    ones = jnp.ones((8, rows.shape[0]), bf)

    @pl.loop(0, blocks)
    def _(q):
        first[q] = tn(rows[...], gp[q]).astype(bf)
        pltpu.make_async_copy(first.at[q], first_grad_any.at[q], grad_sem.at[q]).start()
        bias_grad_ref[q, :8] = nn(ones, gp[q])
        bias_grad_ref[q, 8:] = nn(ones, go[...])

    router_grad_ref[...] = tn(logit_grad[...], rows[...])[: router_grad_ref.shape[0]]

    @pl.loop(1, n)
    def _(step):
        dispatch(step, back_sent, back, back_sems).wait()
        dispatch(step, sent, rows, out_sems).wait_send()

    grad_ref[...] = nn(from_ref[...], back[...]).astype(bf)
    for copy in swaps + own_swaps:
        copy.wait()

    @pl.loop(0, blocks)
    def _(q):
        pltpu.make_async_copy(first.at[q], first_grad_any.at[q], grad_sem.at[q]).wait()

    to_core(1).wait_recv()
    to_x.wait_recv()

    @pl.loop(0, 6)
    def _(k):
        at = rows_of(k, recv_x.shape[0] // 6)
        second_grad_ref[at, :] = (
            second[near, at, :].astype(f32) + recv_e[1, at, :].astype(f32) + recv_x[at, :].astype(f32)
        )

    to_core(0).wait_send()
    to_core(1).wait_send()
    to_x.wait_send()


def moe(h_block, into, outof, dy_slots, first, second, bias, router, dy, branch, experts):
    bf, f32 = jnp.bfloat16, jnp.float32
    tok, width = h_block.shape
    slots = into.shape[0]
    blocks, hidden = first.shape[0], first.shape[2]
    sds = jax.ShapeDtypeStruct
    dma = pltpu.SemaphoreType.DMA
    big = (slots, width)
    return pl.pallas_call(
        functools.partial(moe_kernel, experts),
        out_shape=(
            sds((tok, width), bf),
            sds(big, bf),
            sds(first.shape, bf),
            sds(second.shape[1:], f32),
            sds((8, width), f32),
            sds((blocks, 16, hidden), f32),
            sds((tok, width), bf),
            sds((tok, width), bf),
        ),
        in_specs=[VMEM] * 4 + [ANY] * 2 + [VMEM] * 2 + [ANY] * 2,
        out_specs=(VMEM,) * 2 + (ANY,) + (VMEM,) * 3 + (ANY,) * 2,
        scratch_shapes=[
            pltpu.VMEM(big, bf),
            pltpu.VMEM(big, bf),
            pltpu.VMEM(big, bf),
            pltpu.VMEM((blocks, slots, hidden), bf),
            pltpu.VMEM((blocks, slots, hidden), bf),
            pltpu.VMEM(big, bf),
            pltpu.VMEM(big, bf),
            pltpu.VMEM((slots, 128), bf),
            pltpu.VMEM(first.shape, bf),
            pltpu.VMEM(second.shape, bf),
            dma((2,)),
            dma((experts,)),
            dma((experts,)),
            dma((experts,)),
            dma((experts,)),
            dma((2, blocks)),
            dma((2, blocks)),
            dma((2,)),
            dma((blocks,)),
            pltpu.VMEM((2,) + second.shape[1:], bf),
            pltpu.VMEM(second.shape[1:], bf),
            dma((3,)),
            dma((3,)),
        ],
        compiler_params=pltpu.CompilerParams(
            collective_id=1, has_side_effects=True, vmem_limit_bytes=61 * 2**20
        ),
        cost_estimate=pl.CostEstimate(
            flops=12 * slots * width * hidden * blocks, bytes_accessed=4 * 10**7, transcendentals=slots * hidden * blocks
        ),
        name="moe",
    )(h_block, into, outof, dy_slots, first, second, bias, router, dy, branch)


def norm_stats(values):
    average = jnp.mean(values, axis=-1, keepdims=True)
    centred = values - average
    inv = lax.rsqrt(jnp.mean(centred * centred, axis=-1, keepdims=True) + norm_eps)
    return centred * inv, inv


def norm_grad(grad_output, normed, inv, gain):
    scaled = grad_output * gain
    return inv * (
        scaled
        - jnp.mean(scaled, axis=-1, keepdims=True)
        - normed * jnp.mean(scaled * normed, axis=-1, keepdims=True)
    )


def rows_of(i, size):
    return pl.ds(pl.multiple_of(i * size, size), size)


def split_axes():
    dp, seq = lax.axis_index("dp"), lax.axis_index("seq")
    return dp // 2, lax.rem(dp, 2), seq // 2, lax.rem(seq, 2)


def greet(n_dp, n_seq):
    dp, seq = lax.axis_index("dp"), lax.axis_index("seq")
    barrier = pltpu.get_barrier_semaphore()
    for step in range(1, n_dp):
        pl.semaphore_signal(
            barrier, inc=1, device_id=(other(dp, step), seq), device_id_type=MESH
        )
    for step in range(1, n_seq):
        pl.semaphore_signal(
            barrier, inc=1, device_id=(dp, lax.rem(seq + step, n_seq)), device_id_type=MESH
        )
    pl.semaphore_wait(barrier, n_dp - 1 + n_seq - 1)


def remote(source, target, send, recv, device):
    return pltpu.make_async_remote_copy(
        source, target, send, recv, device_id=device, device_id_type=MESH
    )


def back_kernel(
    n_dp,
    n_seq,
    grad_any,
    resid_any,
    x_any,
    dy_any,
    att_any,
    qkv_any,
    probs_any,
    packed_any,
    vectors_ref,
    outs_any,
    outof_any,
    tokens_any,
    branch_any,
    first_any,
    bias_ref,
    router_grad_ref,
    block_out_ref,
    tokens_grad_ref,
    qkv_grad_ref,
    out_grad_ref,
    small_ref,
    first_out_ref,
    bias_out_ref,
    grad_rows,
    resid,
    x_row,
    dy_row,
    att,
    qkv,
    probs,
    w_qkv,
    w_out,
    outs,
    outof,
    tokens,
    branch,
    own_e,
    recv_e,
    recv_x,
    recv_b,
    grad_resid,
    grad_att,
    grad_qkv,
    h_one,
    grad_x,
    part,
    recv_c,
    recv_1,
    recv_2,
    recv_3,
    sums,
    recv_s,
    load_sem,
    probs_sem,
    own_sem,
    gs_sem,
    gr_sem,
    os_sem,
    or_sem,
    es_sem,
    er_sem,
    xs_sem,
    xr_sem,
    bs_sem,
    br_sem,
    ps_sem,
    pr_sem,
    ss_sem,
    sr_sem,
    ts_sem,
    tr_sem,
):
    bf, f32 = jnp.bfloat16, jnp.float32
    dp, seq = lax.axis_index("dp"), lax.axis_index("seq")
    z, y, x, c = split_axes()
    pos = grad_rows.shape[0] // n_seq
    cap = outs.shape[0] // n_dp
    core_peer, x_peer = (dp, x * 2 + 1 - c), (dp, (1 - x) * 2 + c)
    y_peer = (z * 2 + 1 - y, seq)
    z_peer = lambda step: (lax.rem(z + step, 4) * 2 + y, seq)
    loads = [
        pltpu.make_async_copy(a, b, load_sem.at[i])
        for i, (a, b) in enumerate(
            (
                (resid_any, resid),
                (dy_any, dy_row),
                (att_any, att),
                (packed_any.at[:, 3 * D : 4 * D], w_out),
                (qkv_any, qkv),
                (x_any, x_row),
                (packed_any.at[:, : 3 * D], w_qkv),
                (outof_any, outof),
                (tokens_any, tokens),
                (branch_any, branch),
            )
        )
    ]
    fetch = lambda head: pltpu.make_async_copy(
        probs_any.at[head], probs.at[head % 2], probs_sem.at[head % 2]
    )
    for load in loads[:4]:
        load.start()
    greet(n_dp, n_seq)
    to_rows = []
    for step in range(1, n_seq):
        to = lax.rem(seq + step, n_seq)
        to_rows.append(
            remote(
                grad_any.at[rows_of(to, pos)],
                grad_rows.at[rows_of(seq, pos)],
                gs_sem.at[step],
                gr_sem.at[step],
                (dp, to),
            )
        )
    for copy in to_rows:
        copy.start()
    own_rows = pltpu.make_async_copy(
        grad_any.at[rows_of(seq, pos)], grad_rows.at[rows_of(seq, pos)], own_sem.at[0]
    )
    own_rows.start()
    experts_c, experts_own = [], []
    for k, side in enumerate((1 - x, x)):
        experts_c.append(
            remote(
                first_any.at[side * 2 + 1 - c], recv_e.at[k], es_sem.at[k], er_sem.at[k], core_peer
            )
        )
        experts_own.append(
            pltpu.make_async_copy(first_any.at[side * 2 + c], own_e.at[k], own_sem.at[1 + k])
        )
    for copy in experts_c + experts_own:
        copy.start()
    returns = []
    for step in range(n_dp - 1, 0, -1):
        to = other(dp, step)
        returns.append(
            remote(
                outs_any.at[rows_of(to, cap)],
                outs.at[rows_of(dp, cap)],
                os_sem.at[step],
                or_sem.at[step],
                (to, seq),
            )
        )
    for copy in returns:
        copy.start()
    own_outs = pltpu.make_async_copy(
        outs_any.at[rows_of(dp, cap)], outs.at[rows_of(dp, cap)], own_sem.at[3]
    )
    own_outs.start()
    biases = []
    for step in range(1, n_seq):
        to = lax.rem(seq + step, n_seq)
        biases.append(
            remote(bias_ref.at[to], recv_b.at[step], bs_sem.at[step], br_sem.at[step], (dp, to))
        )
    for copy in biases:
        copy.start()
    for load in loads[4:]:
        load.start()
    fetch(0).start()
    fetch(1).start()
    vec = lambda i: vectors_ref[i : i + 1, :]
    row_sum = lambda v: jnp.sum(v, axis=0, keepdims=True)

    def norm_back(grad_output, values, gain):
        normed, inv = norm_stats(values)
        sums_of = (row_sum(grad_output * normed), row_sum(grad_output))
        return norm_grad(grad_output, normed, inv, gain), *sums_of

    def piece_fill(i, value):
        half = value.shape[1] // 2
        for owner in range(n_dp * n_seq):
            oz, oy, ox, oc = owner // 8, owner // 4 % 2, owner // 2 % 2, owner % 2
            block = value[24 * owner : 24 * owner + 24].astype(bf)
            part[i, oc, 0, ox, oy, oz] = block[:, :half]
            part[i, oc, 1, oy, ox, oz] = block[:, half:]

    first_axis = ((x, x_peer), (y, y_peer))

    def piece_copies(i, stage):
        sems = lambda k: (ps_sem.at[i, k], pr_sem.at[i, k])
        if stage == 0:
            return [remote(part.at[i, 1 - c], recv_c.at[i], *sems(0), core_peer)]
        made = []
        for h in range(2):
            (f, f_peer), (g, g_peer) = first_axis[h], first_axis[1 - h]
            if stage == 1:
                made.append(
                    remote(part.at[i, c, h, 1 - f], recv_1.at[i, h], *sems(1 + h), f_peer)
                )
            elif stage == 2:
                made.append(
                    remote(part.at[i, c, h, f, 1 - g], recv_2.at[i, h], *sems(3 + h), g_peer)
                )
            else:
                for step in range(1, 4):
                    made.append(
                        remote(
                            part.at[i, c, h, f, g, lax.rem(z + step, 4)],
                            recv_3.at[i, h, step],
                            *sems(4 + h * 3 + step),
                            z_peer(step),
                        )
                    )
        return made

    def add(a, b):
        return (a.astype(f32) + b.astype(f32)).astype(bf)

    def piece_advance(i, stage):
        for copy in piece_copies(i, stage - 1):
            copy.wait_recv()
        if stage == 1:
            part[i, c] = add(part[i, c], recv_c[i])
        for h in range(2):
            f, g = first_axis[h][0], first_axis[1 - h][0]
            if stage == 2:
                part[i, c, h, f] = add(part[i, c, h, f], recv_1[i, h])
            elif stage == 3:
                part[i, c, h, f, g] = add(part[i, c, h, f, g], recv_2[i, h])
            elif stage == 4:
                total = part[i, c, h, f, g, z].astype(f32)
                for step in range(1, 4):
                    total = total + recv_3[i, h, step].astype(f32)
                half = total.shape[1]
                for k in range(3):
                    at = h * half + k * 128
                    lanes = total[:, k * 128 : k * 128 + 128]
                    if i == 0:
                        out_grad_ref[:, at : at + 128] = lanes
                    else:
                        to = D * (at // 256) + 256 * (i - 1) + at % 256
                        qkv_grad_ref[:, to : to + 128] = lanes
        if stage < 4:
            for copy in piece_copies(i, stage):
                copy.start()

    def small_copies(stage):
        peers = ([core_peer], [x_peer], [y_peer], [z_peer(1), z_peer(2), z_peer(3)])[stage]
        return [
            remote(
                sums.at[stage],
                recv_s.at[stage + k],
                ss_sem.at[stage + k],
                sr_sem.at[stage + k],
                peer,
            )
            for k, peer in enumerate(peers)
        ]

    def small_advance(stage):
        for copy in small_copies(stage - 1):
            copy.wait_recv()
        if stage < 4:
            sums[stage] = sums[stage - 1] + recv_s[stage - 1]
            for copy in small_copies(stage):
                copy.start()
        else:
            small_ref[...] = sums[3] + recv_s[3] + recv_s[4] + recv_s[5]

    experts_x = remote(own_e.at[0], recv_x, xs_sem, xr_sem, x_peer)

    def experts_send_x():
        experts_c[0].wait_recv()
        experts_own[0].wait()
        own_e[0] = add(own_e[0], recv_e[0])
        experts_x.start()

    def experts_end():
        experts_c[1].wait_recv()
        experts_own[1].wait()
        experts_x.wait_recv()

        @pl.loop(0, 6)
        def _(k):
            at = rows_of(k, recv_x.shape[0] // 6)
            first_out_ref[at, :] = (
                own_e[1, at, :].astype(f32)
                + recv_e[1, at, :].astype(f32)
                + recv_x[at, :].astype(f32)
            )

        bias = bias_ref[seq]
        for step in range(1, n_seq):
            biases[step - 1].wait_recv()
            bias = bias + recv_b[step]
        bias_out_ref[...] = bias

    for load in loads[:3]:
        load.wait()
    own_rows.wait()
    for copy in to_rows:
        copy.wait_recv()
    experts_send_x()
    grad_in, gain_two, shift_two = norm_back(grad_rows[...].astype(f32), resid[...], vec(3))
    grad_resid[...] = dy_row[...].astype(f32) + grad_in
    grad_branch = grad_resid[...].astype(bf)
    out_shift = row_sum(grad_branch.astype(f32))
    loads[3].wait()
    grad_att[...] = nt(grad_branch, w_out[...]).astype(bf)
    piece_fill(0, tn(att[...], grad_branch))
    for copy in piece_copies(0, 0):
        copy.start()
    loads[4].wait()
    loads[5].wait()
    x_normed, _ = norm_stats(x_row[...].astype(f32))
    h_one[...] = (x_normed * vec(0) + vec(1)).astype(bf)
    ahead = (((0, 1),), (), ((1, 1),), ((0, 2),), ((2, 1),), ((0, 3), (1, 2)))
    lane = lax.broadcasted_iota(jnp.int32, (1, 128), 1) // HEAD
    scale = HEAD ** (-0.5)
    for pair in range(HEADS // 2):
        cols = slice(128 * pair, 128 * pair + 128)
        q, k, v = (qkv[:, D * i + 128 * pair : D * i + 128 * pair + 128] for i in range(3))
        go = grad_att[:, cols]
        both = go.astype(f32) * att[:, cols].astype(f32)
        grads = [jnp.zeros(q.shape, f32)] * 3
        for h in range(2):
            head = 2 * pair + h
            keep = (lane == h).astype(bf)
            fetch(head).wait()
            p = probs[head % 2]
            go_h = go * keep
            delta = jnp.sum(both * keep.astype(f32), axis=-1, keepdims=True)
            ds = (p.astype(f32) * (nt(go_h, v) - delta)).astype(bf)
            grads = [
                grads[0] + nn(ds, k * keep),
                grads[1] + tn(ds, q * keep),
                grads[2] + tn(p, go_h),
            ]
            if head + 2 < HEADS:
                fetch(head + 2).start()
        for i, factor in enumerate((scale, scale, 1.0)):
            at = (2 * 128) * (3 * (pair // 2) + i) + 128 * (pair % 2)
            grad_qkv[:, at : at + 128] = (grads[i] * factor).astype(bf)
        for i, stage in ahead[pair]:
            piece_advance(i, stage)
        if pair % 2 == 1:
            i = pair // 2 + 1
            piece_fill(i, tn(h_one[...], grad_qkv[:, D * (i - 1) : D * i]))
            for copy in piece_copies(i, 0):
                copy.start()
    loads[6].wait()
    grad_h1 = jnp.zeros(resid.shape, f32)
    for i in range(9):
        at = 256 * i
        col = D * (i % 3) + 256 * (i // 3)
        grad_h1 = grad_h1 + nt(grad_qkv[:, at : at + 256], w_qkv[:, col : col + 256])
    piece_advance(3, 1)
    piece_advance(2, 2)
    piece_advance(1, 3)
    grad_in, gain_one, shift_one = norm_back(grad_h1, x_row[...].astype(f32), vec(0))
    sums[0] = jnp.concatenate(
        [gain_one, shift_one, out_shift, gain_two, shift_two, jnp.zeros((3, D), f32), router_grad_ref[...]], axis=0
    )
    for copy in small_copies(0):
        copy.start()
    grad_x[...] = (grad_resid[...] + grad_in).astype(bf)
    to_blocks = []
    for step in range(1, n_seq):
        to = lax.rem(seq + step, n_seq)
        to_blocks.append(
            remote(
                grad_x.at[rows_of(to, pos)],
                tokens_grad_ref.at[rows_of(seq, pos)],
                ts_sem.at[step],
                tr_sem.at[step],
                (dp, to),
            )
        )
    for copy in to_blocks:
        copy.start()
    tokens_grad_ref[rows_of(seq, pos), :] = grad_x[rows_of(seq, pos), :]
    small_advance(1)
    own_outs.wait()
    for copy in returns:
        copy.wait_recv()
    for load in loads[7:]:
        load.wait()
    block_out_ref[...] = (
        tokens[...].astype(f32) + branch[...].astype(f32) + nn(outof[...], outs[...])
    ).astype(bf)
    piece_advance(0, 4)
    piece_advance(3, 2)
    piece_advance(2, 3)
    small_advance(2)
    piece_advance(1, 4)
    experts_end()
    piece_advance(3, 3)
    small_advance(3)
    piece_advance(2, 4)
    piece_advance(3, 4)
    small_advance(4)
    for copy in to_blocks:
        copy.wait_recv()
    for copy in to_rows + experts_c + returns + biases + [experts_x] + to_blocks:
        copy.wait_send()
    for stage in range(4):
        for i in range(4):
            for copy in piece_copies(i, stage):
                copy.wait_send()
        for copy in small_copies(stage):
            copy.wait_send()


def back(
    n_dp,
    n_seq,
    grad_h2,
    resid,
    x_row,
    dy_row,
    att,
    qkv,
    probs,
    packed,
    vectors,
    outs,
    outof,
    tokens,
    branch,
    first_grad,
    biases,
    router_grad,
):
    bf, f32 = jnp.bfloat16, jnp.float32
    sds, dma, vmem = jax.ShapeDtypeStruct, pltpu.SemaphoreType.DMA, pltpu.VMEM
    tok, slots = outof.shape
    pos = tok // n_seq
    half = D // 2
    return pl.pallas_call(
        functools.partial(back_kernel, n_dp, n_seq),
        out_shape=(
            sds((tok, D), bf),
            sds((tok, D), bf),
            sds((D // (n_dp * n_seq), 3 * D), f32),
            sds((D // (n_dp * n_seq), D), f32),
            sds((16, D), f32),
            sds(first_grad.shape[1:], f32),
            sds(biases.shape[1:], f32),
        ),
        in_specs=[ANY] * 8 + [VMEM] + [ANY] * 5 + [VMEM] * 2,
        out_specs=(VMEM,) * 7,
        scratch_shapes=[
            vmem((tok, D), bf),
            vmem((tok, D), f32),
            vmem((tok, D), bf),
            vmem((tok, D), bf),
            vmem((tok, D), bf),
            vmem((tok, 3 * D), bf),
            vmem((2,) + probs.shape[1:], bf),
            vmem((D, 3 * D), bf),
            vmem((D, D), bf),
            vmem((slots, D), bf),
            vmem((tok, slots), bf),
            vmem((tok, D), bf),
            vmem((tok, D), bf),
            vmem((2, D, D), bf),
            vmem((2, D, D), bf),
            vmem((D, D), bf),
            vmem((n_seq,) + biases.shape[1:], f32),
            vmem((tok, D), f32),
            vmem((tok, D), bf),
            vmem((tok, 3 * D), bf),
            vmem((tok, D), bf),
            vmem((tok, D), bf),
            vmem((4, 2, 2, 2, 2, 4, 24, half), bf),
            vmem((4, 2, 2, 2, 4, 24, half), bf),
            vmem((4, 2, 2, 4, 24, half), bf),
            vmem((4, 2, 4, 24, half), bf),
            vmem((4, 2, 4, 24, half), bf),
            vmem((4, 16, D), f32),
            vmem((6, 16, D), f32),
            dma((10,)),
            dma((2,)),
            dma((4,)),
            dma((n_seq,)),
            dma((n_seq,)),
            dma((n_dp,)),
            dma((n_dp,)),
            dma((2,)),
            dma((2,)),
            dma,
            dma,
            dma((n_seq,)),
            dma((n_seq,)),
            dma((4, 11)),
            dma((4, 11)),
            dma((6,)),
            dma((6,)),
            dma((n_seq,)),
            dma((n_seq,)),
        ],
        compiler_params=pltpu.CompilerParams(
            collective_id=2, has_side_effects=True, vmem_limit_bytes=61 * 2**20
        ),
        cost_estimate=pl.CostEstimate(
            flops=10**10, bytes_accessed=5 * 10**7, transcendentals=10**6
        ),
        name="back",
    )(
        grad_h2,
        resid,
        x_row,
        dy_row,
        att,
        qkv,
        probs,
        packed,
        vectors,
        outs,
        outof,
        tokens,
        branch,
        first_grad,
        biases,
        router_grad,
    )


def finish_kernel(count, *refs):
    sources, targets, held = refs[:count], refs[count : 2 * count], refs[2 * count : 3 * count]
    in_sem, out_sem = refs[3 * count :]
    reads = [
        pltpu.make_async_copy(a, b, in_sem.at[i]) for i, (a, b) in enumerate(zip(sources, held))
    ]
    writes = [
        pltpu.make_async_copy(a, b, out_sem.at[i]) for i, (a, b) in enumerate(zip(held, targets))
    ]
    for copy in reads:
        copy.start()
    for read, write in zip(reads, writes):
        read.wait()
        write.start()
    for copy in writes:
        copy.wait()


def finish(*arrays):
    count = len(arrays)
    return pl.pallas_call(
        functools.partial(finish_kernel, count),
        out_shape=tuple(jax.ShapeDtypeStruct(a.shape, a.dtype) for a in arrays),
        in_specs=[ANY] * count,
        out_specs=(ANY,) * count,
        scratch_shapes=[pltpu.VMEM(a.shape, a.dtype) for a in arrays]
        + [pltpu.SemaphoreType.DMA((count,))] * 2,
        compiler_params=pltpu.CompilerParams(vmem_limit_bytes=61 * 2**20),
        name="finish",
    )(*arrays)


def front_kernel(
    n_dp,
    n_seq,
    cap,
    tokens_any,
    dy_any,
    w_qkv_any,
    w_out_any,
    first_any,
    second_any,
    router_in_ref,
    vectors_in_ref,
    order_ref,
    picks_ref,
    open_ref,
    bias1_ref,
    bias2_ref,
    h_block_any,
    resid_any,
    x_any,
    att_any,
    qkv_any,
    probs_any,
    packed_any,
    vectors_ref,
    router_ref,
    branch_any,
    into_any,
    outof_any,
    dy_slots_any,
    first_all,
    second_all,
    bias_all,
    wide_q,
    wide_k,
    wide_v,
    wide_o,
    packed,
    x_row,
    dy,
    mask_out,
    mask_in,
    qkv,
    att,
    probs,
    resid,
    branch,
    h_two,
    into,
    outof,
    dy_sent,
    weights,
    bias_ref,
    load_sem,
    store_sem,
    probs_sem,
    own_sem,
    keep_sem,
    gs_sem,
    gr_sem,
    xs_sem,
    xr_sem,
    ms_sem,
    mr_sem,
    ds_sem,
    dr_sem,
    es_sem,
    er_sem,
    bs_sem,
    br_sem,
    hs_sem,
    hr_sem,
):
    bf, f32, i32 = jnp.bfloat16, jnp.float32, jnp.int32
    dp, seq = lax.axis_index("dp"), lax.axis_index("seq")
    z, y, x, c = split_axes()
    tok = x_row.shape[0]
    pos, held, slots = tok // n_seq, into.shape[0] // n_dp, into.shape[0]
    core_peer, x_peer = (dp, x * 2 + 1 - c), (dp, (1 - x) * 2 + c)
    y_peer = (z * 2 + 1 - y, seq)
    z_peer = lambda step: (lax.rem(z + step, 4) * 2 + y, seq)
    wide = (wide_q, wide_k, wide_v, wide_o)
    mine = [ref.at[c, y, x, z] for ref in wide]
    shard = [
        pltpu.make_async_copy(a, b, load_sem.at[i])
        for i, (a, b) in enumerate(
            (
                (w_qkv_any.at[:, :D], mine[0].at[:, 128:]),
                (w_qkv_any.at[:, D : 2 * D], mine[1]),
                (w_qkv_any.at[:, 2 * D :], mine[2]),
                (w_out_any, mine[3]),
                (dy_any, dy),
                (tokens_any.at[rows_of(seq, pos)], x_row.at[rows_of(seq, pos)]),
            )
        )
    ]
    own_w = [
        pltpu.make_async_copy(ref, weights.at[j, seq], own_sem.at[j])
        for j, ref in enumerate((first_any, second_any))
    ]
    for copy in shard + own_w:
        copy.start()
    unit = lambda rows, shift: (
        lax.broadcasted_iota(i32, (rows, 128), 0) + shift
        == lax.broadcasted_iota(i32, (rows, 128), 1)
    ).astype(f32).astype(bf)
    narrow = nn(router_in_ref[...], unit(n_dp, 0)) + tn(vectors_in_ref[...], unit(8, n_dp))
    wide_q[c, y, x, z, :, :128] = narrow.astype(bf)

    def column(block):
        turned = jnp.concatenate([block.astype(f32)] * 2, axis=0).T
        return jnp.concatenate([turned[:, r : r + 1] for r in range(n_seq)], axis=0)

    order, valid = column(order_ref[...]), column(open_ref[...])
    ids = [column(picks_ref[k]).astype(i32) for k in range(2)]
    mask_out[...] = jnp.broadcast_to(valid, mask_out.shape).astype(bf)
    spots = lax.broadcasted_iota(i32, (bias2_ref.shape[1], D), 1)
    here = lax.broadcasted_iota(i32, spots.shape, 0) + seq * bias2_ref.shape[1]
    placed = nn(bias2_ref[...], (spots == here).astype(f32).astype(bf))
    bias_ref[...] = jnp.concatenate(
        [bias1_ref[...].astype(f32), placed, jnp.zeros((14, D), f32)], axis=0
    )
    for copy in shard[:4]:
        copy.wait()
    greet(n_dp, n_seq)
    seq_peers = [(step, lax.rem(seq + step, n_seq)) for step in range(1, n_seq)]

    def over(k, stage):
        sems = lambda i: (gs_sem.at[k, i], gr_sem.at[k, i])
        same = lambda ref, i, peer: remote(ref, ref, *sems(i), peer)
        if stage == 0:
            return [same(mine[k], step, z_peer(step)) for step in range(1, 4)]
        if stage == 1:
            return [same(wide[k].at[c, y, x], 0, x_peer)]
        if stage == 2:
            return [same(wide[k].at[c, y], 4, y_peer)]
        return [same(wide[k].at[c, (y, 1 - y)[stage - 3]], 2 + stage, core_peer)]

    def begin(k, *stages):
        for stage in stages:
            for copy in over(k, stage):
                copy.start()

    def arrived(k, stage):
        for copy in over(k, stage):
            copy.wait_recv()

    begin(0, 0)
    begin(1, 0)
    exchange = []
    for step, to in seq_peers:
        for source, target, sems in (
            (tokens_any, x_row, (xs_sem, xr_sem)),
            (mask_out, mask_in, (ms_sem, mr_sem)),
        ):
            exchange.append(
                remote(
                    source.at[rows_of(to, pos)],
                    target.at[rows_of(seq, pos)],
                    sems[0].at[step],
                    sems[1].at[step],
                    (dp, to),
                )
            )
    for copy in exchange:
        copy.start()
    mask_in[rows_of(seq, pos), :] = mask_out[rows_of(seq, pos), :]
    biases = [
        remote(bias_ref, bias_all.at[seq], bs_sem.at[step], br_sem.at[step], (dp, to))
        for step, to in seq_peers
    ]
    for copy in biases:
        copy.start()
    bias_all[seq] = bias_ref[...]
    for k in range(2):
        arrived(k, 0)
        begin(k, 1)
        begin(k + 2, 0)
    down = lax.broadcasted_iota(i32, (tok, tok), 0)
    across = lax.broadcasted_iota(i32, (tok, tok), 1)
    order_row = jnp.broadcast_to(order, (tok, 128)).T[:1].astype(i32)
    hit = order.astype(i32) == across
    rank_row = jnp.sum(jnp.where(hit, down.astype(f32), 0.0), axis=0, keepdims=True)
    hit = order_row == down
    rank_col = jnp.sum(jnp.where(hit, across.astype(f32), 0.0), axis=1, keepdims=True)
    earlier = (rank_row < rank_col).astype(bf)
    lane = lax.broadcasted_iota(i32, (tok, 128), 1)
    chosen = (lane == ids[0], lane == ids[1] + n_dp)
    counted = jnp.where(chosen[0] | chosen[1], 1.0, 0.0) * valid
    before = nn(earlier, counted.astype(bf))
    firsts = jnp.sum(jnp.where(lane == ids[0] + n_dp, 1.0, 0.0) * valid, axis=0, keepdims=True)
    spot = lax.broadcasted_iota(i32, (tok, slots), 1).astype(f32)
    spot_down = lax.broadcasted_iota(i32, (slots, tok), 0).astype(f32)
    hits, hits_down = [], []
    for k in range(2):
        slot = jnp.sum(jnp.where(chosen[k], before + firsts * k, 0.0), axis=1, keepdims=True)
        place = ids[k].astype(f32) * held + slot
        place = jnp.where((slot < cap) & (valid > 0.0), place, 1.0 * slots)
        place_row = jnp.broadcast_to(place, (tok, 128)).T[:1]
        hits.append(place == spot)
        hits_down.append(place_row == spot_down)
    outof[...] = jnp.where(hits[0] | hits[1], 1.0, 0.0).astype(bf)
    into[...] = jnp.where(hits_down[0] | hits_down[1], 1.0, 0.0).astype(bf)
    stores = [
        pltpu.make_async_copy(a, b, store_sem.at[i])
        for i, (a, b) in enumerate(
            (
                (into, into_any),
                (outof, outof_any),
                (x_row, x_any),
                (packed, packed_any),
                (qkv, qkv_any),
                (att, att_any),
                (branch, branch_any),
                (resid, resid_any),
            )
        )
    ]
    stores[0].start()
    stores[1].start()
    arrived(2, 0)
    begin(2, 1)
    arrived(0, 1)
    begin(0, 2, 3)
    arrived(3, 0)
    begin(3, 1)
    shard[4].wait()
    dy_sent[...] = nn(into[...], dy[...]).astype(bf)
    dy_copies = []
    for step in range(n_dp - 1, 0, -1):
        to = other(dp, step)
        dy_copies.append(
            remote(
                dy_sent.at[rows_of(to, held)],
                dy_slots_any.at[rows_of(dp, held)],
                ds_sem.at[step],
                dr_sem.at[step],
                (to, seq),
            )
        )
    for copy in dy_copies:
        copy.start()
    own_dy = pltpu.make_async_copy(
        dy_sent.at[rows_of(dp, held)], dy_slots_any.at[rows_of(dp, held)], own_sem.at[2]
    )
    own_dy.start()
    arrived(1, 1)
    begin(1, 2, 3)
    experts_x, experts_c, experts_f, kept_w = [], [], [], []
    for j, target in enumerate((first_all, second_all)):
        far = (1 - x) * 2 + c
        held_w = weights.at[j]
        sems = lambda k: (es_sem.at[j, k], er_sem.at[j, k])
        own_w[j].wait()
        experts_x.append(remote(held_w.at[seq], held_w.at[seq], *sems(0), x_peer))
        experts_c.append(remote(held_w.at[seq], held_w.at[seq], *sems(1), core_peer))
        experts_f.append(remote(held_w.at[far], held_w.at[far], *sems(2), core_peer))
        kept_w.append([])
        for k, block in enumerate((seq, x * 2 + 1 - c, far, (1 - x) * 2 + 1 - c)):
            kept_w[j].append(
                pltpu.make_async_copy(held_w.at[block], target.at[block], keep_sem.at[j, k])
            )
        kept_w[j][0].start()
    for copy in experts_x:
        copy.start()
    shard[5].wait()
    for copy in exchange:
        copy.wait_recv()
    normed, _ = norm_stats(x_row[...].astype(f32))
    stores[2].start()
    arrived(2, 1)
    begin(2, 2, 3)
    arrived(0, 2)
    begin(0, 4)
    arrived(3, 1)
    begin(3, 2, 3)

    def assemble(k, lanes):
        arrived(k, 3)
        arrived(k, 4)
        return gathered(k, lanes)

    def gathered(k, lanes):
        blocks = []
        for at in range(n_dp * n_seq):
            oz, oy, ox, oc = at // 8, at // 4 % 2, at // 2 % 2, at % 2
            blocks.append(wide[k][oc, oy, ox, oz, :, lanes].astype(f32))
        return jnp.concatenate(blocks, axis=0)

    narrow = assemble(0, slice(0, 128))
    router_ref[...] = narrow.astype(bf)
    vectors = narrow.T[8:16]
    vectors_ref[...] = vectors
    vec = lambda i: vectors[i : i + 1]
    h_one = (normed * vec(0) + vec(1)).astype(bf)
    for k in range(3):
        here = slice(D * k, D * k + D)
        arrived(k + 1, 2)
        begin(k + 1, 4)
        block = gathered(0, slice(128, 128 + D)) if k == 0 else assemble(k, slice(0, D))
        packed[:, here] = block.astype(bf)
        qkv[:, here] = nn(h_one, packed[:, here]).astype(bf)
    stores[4].start()
    for copy in experts_c:
        copy.start()
    lane = lax.broadcasted_iota(i32, (1, 128), 1)
    closed = jnp.where(mask_in[...].astype(f32) > 0.0, 0.0, -1e30).astype(bf)
    keep_out = lambda head: pltpu.make_async_copy(
        probs.at[head % 2], probs_any.at[head], probs_sem.at[head % 2]
    )
    for pair in range(HEADS // 2):
        q, k, v = (qkv[:, D * i + 128 * pair : D * i + 128 * pair + 128] for i in range(3))
        q = q * jnp.asarray(HEAD ** (-0.5), bf)
        out = jnp.zeros(q.shape, f32)
        for h in range(2):
            head = 2 * pair + h
            keep = (lane // HEAD == h).astype(bf)
            spare = (lane == HEAD * (1 - h)).astype(bf)
            scores = nt(q * keep + spare, k * keep + closed * spare)
            soft = jnp.exp(scores - jnp.max(scores, axis=-1, keepdims=True))
            soft = soft * (1.0 / jnp.sum(soft, axis=-1, keepdims=True))
            if head >= 2:
                keep_out(head - 2).wait()
            low = soft.astype(bf)
            probs[head % 2] = low
            keep_out(head).start()
            out = out + nn(low, v * keep)
        att[:, 128 * pair : 128 * pair + 128] = out.astype(bf)
        if pair > 3:
            j = pair - 4
            experts_x[j].wait_recv()
            experts_f[j].start()
            kept_w[j][2].start()
    stores[5].start()
    packed[:, 3 * D :] = assemble(3, slice(0, D)).astype(bf)
    stores[3].start()
    made = nn(att[...], packed[:, 3 * D :]) + vec(2)
    branch[...] = made.astype(bf)
    resid[...] = x_row[...].astype(f32) + made
    normed, _ = norm_stats(resid[...])
    h_two[...] = (normed * vec(3) + vec(4)).astype(bf)
    to_blocks = [
        remote(
            h_two.at[rows_of(to, pos)],
            h_block_any.at[rows_of(seq, pos)],
            hs_sem.at[step],
            hr_sem.at[step],
            (dp, to),
        )
        for step, to in seq_peers
    ]
    for copy in to_blocks:
        copy.start()
    own_h = pltpu.make_async_copy(
        h_two.at[rows_of(seq, pos)], h_block_any.at[rows_of(seq, pos)], own_sem.at[3]
    )
    own_h.start()
    stores[6].start()
    stores[7].start()
    for j in range(2):
        experts_c[j].wait_recv()
        kept_w[j][1].start()
    for j in range(2):
        experts_f[j].wait_recv()
        kept_w[j][3].start()
    for copy in to_blocks + dy_copies + biases:
        copy.wait_recv()
    keep_out(HEADS - 2).wait()
    keep_out(HEADS - 1).wait()
    for copy in stores + kept_w[0] + kept_w[1] + [own_dy, own_h]:
        copy.wait()
    for copy in exchange + to_blocks + dy_copies + biases + experts_x + experts_c + experts_f:
        copy.wait_send()
    for k in range(4):
        for stage in range(5):
            for copy in over(k, stage):
                copy.wait_send()


def front(
    n_dp,
    n_seq,
    cap,
    held,
    tokens,
    dy,
    w_qkv,
    w_out,
    first,
    second,
    w_router,
    vectors,
    order,
    picks,
    mask,
    bias1,
    bias2,
):
    bf, f32 = jnp.bfloat16, jnp.float32
    sds, dma, vmem = jax.ShapeDtypeStruct, pltpu.SemaphoreType.DMA, pltpu.VMEM
    tok = tokens.shape[0]
    slots = n_dp * held
    own = D // (n_dp * n_seq)
    block = (tok, D)
    return pl.pallas_call(
        functools.partial(front_kernel, n_dp, n_seq, cap),
        out_shape=(
            sds(block, bf),
            sds(block, f32),
            sds(block, bf),
            sds(block, bf),
            sds((tok, 3 * D), bf),
            sds((HEADS, tok, tok), bf),
            sds((D, 4 * D), bf),
            sds((8, D), f32),
            sds((D, 128), bf),
            sds(block, bf),
            sds((slots, tok), bf),
            sds((tok, slots), bf),
            sds((slots, D), bf),
            sds((n_seq,) + first.shape, bf),
            sds((n_seq,) + second.shape, bf),
            sds((n_seq, 16, D), f32),
        ),
        in_specs=[ANY] * 6 + [VMEM] * 7,
        out_specs=(ANY,) * 7 + (VMEM,) * 2 + (ANY,) * 6 + (VMEM,),
        scratch_shapes=[
            vmem((2, 2, 2, 4, own, 128 + D), bf),
            vmem((2, 2, 2, 4, own, D), bf),
            vmem((2, 2, 2, 4, own, D), bf),
            vmem((2, 2, 2, 4, own, D), bf),
            vmem((D, 4 * D), bf),
            vmem(block, bf),
            vmem(block, bf),
            vmem((tok, 128), bf),
            vmem((tok, 128), bf),
            vmem((tok, 3 * D), bf),
            vmem(block, bf),
            vmem((2, tok, tok), bf),
            vmem(block, f32),
            vmem(block, bf),
            vmem(block, bf),
            vmem((slots, tok), bf),
            vmem((tok, slots), bf),
            vmem((slots, D), bf),
            vmem((2, n_seq) + first.shape, bf),
            vmem((16, D), f32),
            dma((6,)),
            dma((8,)),
            dma((2,)),
            dma((4,)),
            dma((2, 4)),
            dma((4, 7)),
            dma((4, 7)),
            dma((n_seq,)),
            dma((n_seq,)),
            dma((n_seq,)),
            dma((n_seq,)),
            dma((n_dp,)),
            dma((n_dp,)),
            dma((2, 3)),
            dma((2, 3)),
            dma((n_seq,)),
            dma((n_seq,)),
            dma((n_seq,)),
            dma((n_seq,)),
        ],
        compiler_params=pltpu.CompilerParams(
            collective_id=3, has_side_effects=True, vmem_limit_bytes=61 * 2**20
        ),
        cost_estimate=pl.CostEstimate(
            flops=6 * 10**9, bytes_accessed=5 * 10**7, transcendentals=4 * 10**6
        ),
        name="front",
    )(
        tokens,
        dy,
        w_qkv,
        w_out,
        first,
        second,
        w_router,
        vectors,
        order,
        picks,
        mask,
        bias1,
        bias2,
    )


def shards_rows(
    tokens,
    cotangent,
    pad_mask,
    expert_ids,
    priority,
    ln1_gain,
    ln1_shift,
    w_qkv,
    w_out,
    out_bias,
    ln2_gain,
    ln2_shift,
    w_router,
    w_in,
    in_bias,
    w_exp_out,
    exp_out_bias,
):
    rows_dev, pos_dev = pad_mask.shape
    tok = rows_dev * pos_dev
    experts = w_router.shape[1]
    cap = (21 * tok + 10 * experts - 1) // (10 * experts)
    n_dp, n_seq = lax.axis_size("dp"), lax.axis_size("seq")
    seq, own = lax.axis_index("seq"), D // (n_dp * n_seq)
    bf, f32 = jnp.bfloat16, jnp.float32
    held = -(-cap // 16) * 16
    flat, dy_block = tokens.reshape(tok, D), cotangent.reshape(tok, D)
    (
        h_block,
        resid,
        x_row,
        attended,
        qkv,
        probs,
        packed,
        vectors,
        router,
        branch,
        into,
        outof,
        dy_slots,
        first,
        second,
        bias,
    ) = front(
        n_dp,
        n_seq,
        cap,
        held,
        flat,
        dy_block,
        w_qkv,
        w_out,
        w_in[0],
        w_exp_out[0],
        w_router,
        jnp.stack([ln1_gain, ln1_shift, out_bias, ln2_gain, ln2_shift] + [ln2_shift] * 3),
        priority,
        jnp.moveaxis(expert_ids, 2, 0),
        pad_mask,
        in_bias,
        exp_out_bias,
    )
    grad_h2, made, first_grad, second_grad, router_grad, bias_grad, dy_row, branch_block = moe(
        h_block, into, outof, dy_slots, first, second, bias, router, dy_block, branch, experts
    )
    out, tokens_grad, qkv_grad, out_grad, small, first_grad, bias_grad = back(
        n_dp,
        n_seq,
        grad_h2,
        resid,
        x_row,
        dy_row,
        attended,
        qkv,
        probs,
        packed,
        vectors,
        made,
        outof,
        flat,
        branch_block,
        first_grad,
        bias_grad,
        router_grad,
    )
    out, tokens_grad, qkv_grad, out_grad, first_grad, second_grad = finish(
        out, tokens_grad, qkv_grad, out_grad, first_grad, second_grad
    )
    small = lax.dynamic_slice_in_dim(
        small, (lax.axis_index("dp") * n_seq + seq) * own, own, 1
    )
    return (
        out.reshape(rows_dev, pos_dev, D),
        tokens_grad.reshape(rows_dev, pos_dev, D),
        small[0],
        small[1],
        qkv_grad,
        out_grad,
        small[2],
        small[3],
        small[4],
        small[8 : 8 + experts].T,
        first_grad[None],
        bias_grad[None, 0],
        second_grad[None],
        lax.dynamic_slice_in_dim(bias_grad[None, 8], seq * exp_out_bias.shape[1], exp_out_bias.shape[1], 1),
    )


def shards(*args):
    block_rows, local_experts, n_dp = args[2].shape[0], args[13].shape[0], lax.axis_size("dp")
    if block_rows == lax.axis_size("seq") and local_experts == 1 and n_dp == 8:
        return shards_rows(*args)
    return shards_general(*args)


def solution(mesh):
    return jax.shard_map(
        shards,
        mesh=mesh,
        in_specs=(
            P("dp", "seq", None),
            P("dp", "seq", None),
            P("dp", "seq"),
            P("dp", "seq", None),
            P("dp", "seq"),
            P(("dp", "seq")),
            P(("dp", "seq")),
            P(("dp", "seq"), None),
            P(("dp", "seq"), None),
            P(("dp", "seq")),
            P(("dp", "seq")),
            P(("dp", "seq")),
            P(("dp", "seq"), None),
            P("dp", None, "seq"),
            P("dp", "seq"),
            P("dp", "seq", None),
            P("dp", "seq"),
        ),
        out_specs=(
            P("dp", "seq", None),
            P("dp", "seq", None),
            P(("dp", "seq")),
            P(("dp", "seq")),
            P(("dp", "seq"), None),
            P(("dp", "seq"), None),
            P(("dp", "seq")),
            P(("dp", "seq")),
            P(("dp", "seq")),
            P(("dp", "seq"), None),
            P("dp", None, "seq"),
            P("dp", "seq"),
            P("dp", "seq", None),
            P("dp", "seq"),
        ),
        check_vma=False,
    )
```

```python
import functools

import jax
import jax.numpy as jnp
from jax import lax
from jax.experimental import pallas as pl
from jax.experimental.pallas import tpu as pltpu
from jax.sharding import PartitionSpec as P

D = 768
HEADS = 12
HEAD = 64


norm_eps = 1e-06


def norm_forward(values, norm_gain, norm_shift):
    average = jnp.mean(values, axis=-1, keepdims=True)
    centred = values - average
    inv_scale = lax.rsqrt(jnp.mean(centred * centred, axis=-1, keepdims=True) + norm_eps)
    normed = centred * inv_scale
    return (
        normed * norm_gain.astype(jnp.float32) + norm_shift.astype(jnp.float32),
        normed,
        inv_scale,
    )


def norm_backward(grad_output, normed, inv_scale, norm_gain):
    scaled = grad_output * norm_gain.astype(jnp.float32)
    grad_input = inv_scale * (
        scaled
        - jnp.mean(scaled, axis=-1, keepdims=True)
        - normed * jnp.mean(scaled * normed, axis=-1, keepdims=True)
    )
    return (
        grad_input,
        jnp.sum(grad_output * normed, axis=(0, 1)),
        jnp.sum(grad_output, axis=(0, 1)),
    )


def gelu_slope(values):
    return (
        0.5 * (1.0 + lax.erf(values * 0.7071067811865476))
        + values * jnp.exp(-0.5 * values * values) * 0.3989422804014327
    )


def slot_ranks(order, picks, valid, experts, capacity):
    count = order.shape[0]
    index = jnp.arange(count, dtype=jnp.int32)
    rank = jnp.sum(jnp.where(order[:, None] == index[None, :], index[:, None], 0), axis=0)
    earlier = (rank[None, :] < rank[:, None]).astype(jnp.bfloat16)
    chosen = picks[:, :, None] == jnp.arange(experts, dtype=jnp.int32)
    counted = chosen.astype(jnp.float32) * valid.astype(jnp.float32)[:, None, None]
    before = jnp.dot(
        earlier,
        counted.reshape(count, 2 * experts).astype(jnp.bfloat16),
        preferred_element_type=jnp.float32,
    ).reshape(count, 2, experts)
    firsts = jnp.sum(counted[:, 0], axis=0)
    before = before + jnp.stack([jnp.zeros_like(firsts), firsts])[None]
    slot = jnp.sum(jnp.where(chosen, before, 0.0), axis=2).astype(jnp.int32)
    kept = (valid[:, None] > 0) & (slot < capacity)
    return kept, slot


def pair_slots(order, expert_picks, valid_flags, expert_count, capacity):
    kept, slot = slot_ranks(order, expert_picks, valid_flags, expert_count, capacity)
    tokens = jnp.arange(order.shape[0], dtype=jnp.int32)
    return (
        jnp.concatenate([tokens, tokens]),
        expert_picks.T.reshape(-1),
        slot.T.reshape(-1),
        kept.T.reshape(-1).astype(jnp.int32),
    )


def shards_general(
    tokens,
    cotangent,
    pad_mask,
    expert_ids,
    priority,
    ln1_gain,
    ln1_shift,
    w_qkv,
    w_out,
    out_bias,
    ln2_gain,
    ln2_shift,
    w_router,
    w_in,
    in_bias,
    w_exp_out,
    exp_out_bias,
):
    rows_dev, pos_dev = pad_mask.shape
    tok_count = rows_dev * pos_dev
    expert_count = w_router.shape[1]
    local_experts = w_in.shape[0]
    capacity = (21 * tok_count + 10 * expert_count - 1) // (10 * expert_count)
    scale_factor = HEAD ** (-0.5)
    gain_one, shift_one, qkv_weight, out_weight, out_shift, gain_two, shift_two, router_weight = (
        lax.all_gather(ln1_gain, ("dp", "seq"), axis=0, tiled=True),
        lax.all_gather(ln1_shift, ("dp", "seq"), axis=0, tiled=True),
        lax.all_gather(w_qkv, ("dp", "seq"), axis=0, tiled=True),
        lax.all_gather(w_out, ("dp", "seq"), axis=0, tiled=True),
        lax.all_gather(out_bias, ("dp", "seq"), axis=0, tiled=True),
        lax.all_gather(ln2_gain, ("dp", "seq"), axis=0, tiled=True),
        lax.all_gather(ln2_shift, ("dp", "seq"), axis=0, tiled=True),
        lax.all_gather(w_router, ("dp", "seq"), axis=0, tiled=True),
    )
    x_float = tokens.astype(jnp.float32)
    h_one, normed_one, inv_one = norm_forward(x_float, gain_one, shift_one)
    h_one_low = h_one.astype(jnp.bfloat16)
    qkv_low = jnp.einsum(
        "rpd,de->rpe", h_one_low, qkv_weight, preferred_element_type=jnp.float32
    ).astype(jnp.bfloat16)
    queries = qkv_low[:, :, :D].reshape(rows_dev, pos_dev, HEADS, HEAD)
    kv_all, mask_all = (
        lax.all_gather(qkv_low[:, :, D:], "seq", axis=1, tiled=True),
        lax.all_gather(pad_mask.astype(jnp.bfloat16), "seq", axis=1, tiled=True),
    )
    full_len = kv_all.shape[1]
    keys_all = kv_all[:, :, :D].reshape(rows_dev, full_len, HEADS, HEAD)
    values_all = kv_all[:, :, D:].reshape(rows_dev, full_len, HEADS, HEAD)
    key_open = (mask_all > 0)[:, None, None, :]

    def score_block():
        raw_scores = (
            jnp.einsum("rphd,rkhd->rhpk", queries, keys_all, preferred_element_type=jnp.float32)
            * scale_factor
        )
        return jnp.where(key_open, raw_scores, -1e30)

    scores = score_block()
    row_max = jnp.max(scores, axis=-1, keepdims=True)
    exp_scores = jnp.exp(scores - row_max)
    row_total = jnp.sum(exp_scores, axis=-1, keepdims=True)
    log_total = row_max + jnp.log(row_total)
    probs_low = (exp_scores / row_total).astype(jnp.bfloat16)
    attended = (
        jnp.einsum("rhpk,rkhd->rphd", probs_low, values_all, preferred_element_type=jnp.float32)
        .reshape(rows_dev, pos_dev, D)
        .astype(jnp.bfloat16)
    )
    branch = jnp.einsum(
        "rpd,de->rpe", attended, out_weight, preferred_element_type=jnp.float32
    ) + out_shift.astype(jnp.float32)
    resid = x_float + branch
    h_two, normed_two, inv_two = norm_forward(resid, gain_two, shift_two)
    flat_low = h_two.astype(jnp.bfloat16).reshape(tok_count, D)
    logits = jnp.dot(flat_low, router_weight, preferred_element_type=jnp.float32)
    router_probs = jax.nn.softmax(logits, axis=-1)
    token_pairs, expert_pairs, slot_index, kept_flags = pair_slots(
        priority.reshape(-1),
        expert_ids.reshape(tok_count, 2),
        pad_mask.reshape(-1),
        expert_count,
        capacity,
    )
    dummy_row = expert_count * capacity
    destination = jnp.where(kept_flags > 0, expert_pairs * capacity + slot_index, dummy_row)
    kept_float = kept_flags.astype(jnp.float32)
    gate_pairs = router_probs[token_pairs, expert_pairs] * kept_float
    send_rows = (
        jnp.zeros((dummy_row + 1, D), jnp.bfloat16)
        .at[destination]
        .set(flat_low[token_pairs])[:-1]
        .reshape(expert_count, capacity, D)
    )
    received = lax.all_to_all(send_rows, "dp", split_axis=0, concat_axis=1, tiled=True)
    seq_index = lax.axis_index("seq")
    bias_cols = exp_out_bias.shape[1]
    rows_all = lax.all_gather(received, "seq", axis=1, tiled=True)
    pre_act = (
        jnp.einsum("erd,edf->erf", rows_all, w_in, preferred_element_type=jnp.float32)
        + in_bias.astype(jnp.float32)[:, None, :]
    )
    act_low = jax.nn.gelu(pre_act, approximate=False).astype(jnp.bfloat16)
    partial_out = jnp.einsum("erf,efd->erd", act_low, w_exp_out, preferred_element_type=jnp.float32)
    bias_full = lax.dynamic_update_slice_in_dim(
        jnp.zeros((local_experts, D), jnp.float32),
        exp_out_bias.astype(jnp.float32),
        seq_index * bias_cols,
        1,
    )
    partial_out = partial_out + bias_full[:, None, :]
    expert_out = lax.psum_scatter(
        partial_out.astype(jnp.bfloat16), "seq", scatter_dimension=1, tiled=True
    )
    returned_buf = lax.all_to_all(expert_out, "dp", split_axis=1, concat_axis=0, tiled=True)
    returned = jnp.concatenate(
        [returned_buf.reshape(-1, D), jnp.zeros((1, D), jnp.bfloat16)], axis=0
    )[destination].astype(jnp.float32)
    mixture = (
        jnp.zeros((tok_count, D), jnp.float32).at[token_pairs].add(gate_pairs[:, None] * returned)
    )
    block_output = (resid + mixture.reshape(rows_dev, pos_dev, D)).astype(jnp.bfloat16)
    grad_y = cotangent.astype(jnp.float32)
    grad_pairs = grad_y.reshape(tok_count, D)[token_pairs]
    grad_gates = jnp.sum(grad_pairs * returned, axis=-1) * kept_float
    grad_ret = (gate_pairs[:, None] * grad_pairs).astype(jnp.bfloat16)
    grad_send = (
        jnp.zeros((dummy_row + 1, D), jnp.bfloat16)
        .at[destination]
        .set(grad_ret)[:-1]
        .reshape(expert_count, capacity, D)
    )
    grad_recv = lax.all_to_all(grad_send, "dp", split_axis=0, concat_axis=1, tiled=True)
    grad_all = lax.all_gather(grad_recv, "seq", axis=1, tiled=True)
    pre_again = (
        jnp.einsum("erd,edf->erf", rows_all, w_in, preferred_element_type=jnp.float32)
        + in_bias.astype(jnp.float32)[:, None, :]
    )
    act_again = jax.nn.gelu(pre_again, approximate=False).astype(jnp.bfloat16)
    grad_act = jnp.einsum("erd,efd->erf", grad_all, w_exp_out, preferred_element_type=jnp.float32)
    grad_pre = (grad_act * gelu_slope(pre_again)).astype(jnp.bfloat16)
    w_exp_out_grad = jnp.einsum(
        "erf,erd->efd", act_again, grad_all, preferred_element_type=jnp.float32
    )
    bias_sums = jnp.sum(grad_all, axis=1, dtype=jnp.float32)
    exp_out_bias_grad = lax.dynamic_slice_in_dim(bias_sums, seq_index * bias_cols, bias_cols, 1)
    w_in_grad = jnp.einsum("erd,erf->edf", rows_all, grad_pre, preferred_element_type=jnp.float32)
    in_bias_grad = jnp.sum(grad_pre, axis=1, dtype=jnp.float32)
    grad_rows_part = jnp.einsum("erf,edf->erd", grad_pre, w_in, preferred_element_type=jnp.float32)
    grad_back = lax.psum_scatter(
        grad_rows_part.astype(jnp.bfloat16), "seq", scatter_dimension=1, tiled=True
    )
    grad_buf = lax.all_to_all(grad_back, "dp", split_axis=1, concat_axis=0, tiled=True)
    grad_rows_back = jnp.concatenate(
        [grad_buf.reshape(-1, D), jnp.zeros((1, D), jnp.bfloat16)], axis=0
    )[destination].astype(jnp.float32)
    grad_h2_experts = jnp.zeros((tok_count, D), jnp.float32).at[token_pairs].add(grad_rows_back)
    grad_probs = (
        jnp.zeros((tok_count, expert_count), jnp.float32)
        .at[token_pairs, expert_pairs]
        .add(grad_gates)
    )
    grad_logits = (
        router_probs * (grad_probs - jnp.sum(router_probs * grad_probs, axis=-1, keepdims=True))
    ).astype(jnp.bfloat16)
    router_grad = jnp.einsum("td,te->de", flat_low, grad_logits, preferred_element_type=jnp.float32)
    grad_h2 = grad_h2_experts + jnp.einsum(
        "te,de->td", grad_logits, router_weight, preferred_element_type=jnp.float32
    )
    grad_resid_norm, gain_two_grad, shift_two_grad = norm_backward(
        grad_h2.reshape(rows_dev, pos_dev, D), normed_two, inv_two, gain_two
    )
    grad_resid = grad_y + grad_resid_norm
    grad_branch = grad_resid.astype(jnp.bfloat16)
    out_weight_grad = jnp.einsum(
        "rpd,rpe->de", attended, grad_branch, preferred_element_type=jnp.float32
    )
    out_shift_grad = jnp.sum(grad_branch, axis=(0, 1), dtype=jnp.float32)
    grad_attended = jnp.einsum(
        "rpe,de->rpd", grad_branch, out_weight, preferred_element_type=jnp.float32
    ).astype(jnp.bfloat16)
    grad_att_heads = grad_attended.reshape(rows_dev, pos_dev, HEADS, HEAD)
    scores_again = score_block()
    probs_again = jnp.exp(scores_again - log_total)
    probs_again_low = probs_again.astype(jnp.bfloat16)
    grad_probs_att = jnp.einsum(
        "rphd,rkhd->rhpk", grad_att_heads, values_all, preferred_element_type=jnp.float32
    )
    row_delta = jnp.sum(probs_again * grad_probs_att, axis=-1, keepdims=True)
    grad_scores = (probs_again * (grad_probs_att - row_delta)).astype(jnp.bfloat16)
    grad_queries = (
        jnp.einsum("rhpk,rkhd->rphd", grad_scores, keys_all, preferred_element_type=jnp.float32)
        * scale_factor
    ).reshape(rows_dev, pos_dev, D)
    grad_keys = (
        jnp.einsum("rhpk,rphd->rkhd", grad_scores, queries, preferred_element_type=jnp.float32)
        * scale_factor
    ).reshape(rows_dev, full_len, D)
    grad_values = jnp.einsum(
        "rhpk,rphd->rkhd", probs_again_low, grad_att_heads, preferred_element_type=jnp.float32
    ).reshape(rows_dev, full_len, D)
    grad_kv = lax.psum_scatter(
        jnp.concatenate([grad_keys, grad_values], axis=-1).astype(jnp.bfloat16),
        "seq",
        scatter_dimension=1,
        tiled=True,
    )
    grad_qkv = jnp.concatenate([grad_queries.astype(jnp.bfloat16), grad_kv], axis=-1)
    qkv_weight_grad = jnp.einsum(
        "rpd,rpe->de", h_one_low, grad_qkv, preferred_element_type=jnp.float32
    )
    grad_h1 = jnp.einsum("rpe,de->rpd", grad_qkv, qkv_weight, preferred_element_type=jnp.float32)
    grad_x_norm, gain_one_grad, shift_one_grad = norm_backward(
        grad_h1, normed_one, inv_one, gain_one
    )
    tokens_grad = (grad_resid + grad_x_norm).astype(jnp.bfloat16)
    dense_parts = (
        lax.psum_scatter(gain_one_grad, ("dp", "seq"), scatter_dimension=0, tiled=True),
        lax.psum_scatter(shift_one_grad, ("dp", "seq"), scatter_dimension=0, tiled=True),
        lax.psum_scatter(qkv_weight_grad, ("dp", "seq"), scatter_dimension=0, tiled=True),
        lax.psum_scatter(out_weight_grad, ("dp", "seq"), scatter_dimension=0, tiled=True),
        lax.psum_scatter(out_shift_grad, ("dp", "seq"), scatter_dimension=0, tiled=True),
        lax.psum_scatter(gain_two_grad, ("dp", "seq"), scatter_dimension=0, tiled=True),
        lax.psum_scatter(shift_two_grad, ("dp", "seq"), scatter_dimension=0, tiled=True),
        lax.psum_scatter(router_grad, ("dp", "seq"), scatter_dimension=0, tiled=True),
    )
    return (
        block_output,
        tokens_grad,
        dense_parts[0],
        dense_parts[1],
        dense_parts[2],
        dense_parts[3],
        dense_parts[4],
        dense_parts[5],
        dense_parts[6],
        dense_parts[7],
        w_in_grad,
        in_bias_grad,
        w_exp_out_grad,
        exp_out_bias_grad,
    )


MESH = pl.DeviceIdType.MESH
VMEM = pl.BlockSpec(memory_space=pltpu.VMEM)
ANY = pl.BlockSpec(memory_space=pl.ANY)
ERF = (0.1274147955, -0.142248368, 0.7107068705, -0.7265760135, 0.5307027145)


def nn(a, b):
    return lax.dot_general(a, b, (((1,), (0,)), ((), ())), preferred_element_type=jnp.float32)


def nt(a, b):
    return lax.dot_general(a, b, (((1,), (1,)), ((), ())), preferred_element_type=jnp.float32)


def tn(a, b):
    return lax.dot_general(a, b, (((0,), (0,)), ((), ())), preferred_element_type=jnp.float32)


def gelu_parts(v):
    bell = jnp.exp(v * v * -0.5)
    t = 1.0 / (jnp.abs(v) * (0.3275911 * 0.7071067811865476) + 1.0)
    a, b, c, d, e = ERF
    tail = ((((e * t + d) * t + c) * t + b) * t + a) * t * bell
    cdf = jnp.where(v < 0.0, tail, 1.0 - tail)
    return v * cdf, cdf + v * (bell * 0.3989422804014327)


def other(me, step):
    bit = lambda k: lax.rem(me // k + step // k, 2) * k
    return bit(4) + bit(2) + bit(1)


def moe_kernel(
    experts,
    h_ref,
    into_ref,
    from_ref,
    dy_ref,
    first_any,
    second_any,
    bias_ref,
    router_ref,
    dy_any,
    branch_any,
    grad_ref,
    outs_ref,
    first_grad_any,
    second_grad_ref,
    router_grad_ref,
    bias_grad_ref,
    dy_row_any,
    branch_block_any,
    sent,
    rows,
    go,
    act,
    gp,
    back_sent,
    back,
    logit_grad,
    first,
    second,
    w_sem,
    send_sem,
    recv_sem,
    send_sem2,
    recv_sem2,
    send_sem3,
    recv_sem3,
    own_sem,
    grad_sem,
    recv_e,
    recv_x,
    es_sem,
    er_sem,
):
    n = experts
    cap = dy_ref.shape[0] // n
    bf, f32 = jnp.bfloat16, jnp.float32
    blocks = first.shape[0]
    me, seq = lax.axis_index("dp"), lax.axis_index("seq")
    n_seq = blocks
    pos = h_ref.shape[0] // n_seq
    load1 = pltpu.make_async_copy(first_any, first, w_sem.at[0])
    load2 = pltpu.make_async_copy(second_any, second, w_sem.at[1])
    load1.start()
    load2.start()
    at = lambda i: pl.ds(pl.multiple_of(i * cap, cap), cap)
    greet(n, n_seq)

    def dispatch(step, source, target, sems):
        to = other(me, step)
        return pltpu.make_async_remote_copy(
            source.at[at(to)],
            target.at[at(me)],
            sems[0].at[step],
            sems[1].at[step],
            device_id=(to, seq),
            device_id_type=MESH,
        )

    out_sems, back_sems = (send_sem, recv_sem), (send_sem2, recv_sem2)

    for step in (1, 4, 5, 2, 3, 6, 7):
        to = other(me, step)
        sent[at(to), :] = nn(into_ref[at(to), :], h_ref[...]).astype(bf)
        dispatch(step, sent, rows, out_sems).start()

    rows[at(me), :] = nn(into_ref[at(me), :], h_ref[...]).astype(bf)
    swaps, own_swaps = [], []
    for k, (source, target) in enumerate(((dy_any, dy_row_any), (branch_any, branch_block_any))):
        here = rows_of(seq, pos)
        own_swaps.append(pltpu.make_async_copy(source.at[here], target.at[here], own_sem.at[k]))
        for step in range(1, n_seq):
            to = lax.rem(seq + step, n_seq)
            swaps.append(
                remote(
                    source.at[rows_of(to, pos)],
                    target.at[here],
                    send_sem3.at[k, step],
                    recv_sem3.at[k, step],
                    (me, to),
                )
            )
    for copy in swaps + own_swaps:
        copy.start()
    load1.wait()
    load2.wait()
    pair = 2 * cap
    lane = lax.broadcasted_iota(jnp.int32, (pair, 128), 1)
    second_bias = jnp.sum(bias_ref[:, 1, :], axis=0, keepdims=True)

    @pl.loop(0, n // 2)
    def _(plane):
        group = rows_of(other(me, 2 * plane) // 2, pair)

        @pl.when(plane > 0)
        def _():
            dispatch(2 * plane, sent, rows, out_sems).wait_recv()

        dispatch(2 * plane + 1, sent, rows, out_sems).wait_recv()
        x = rows[group, :]
        dy = dy_ref[group, :].astype(f32)
        logits = jnp.where(lane < n, nn(x, router_ref[...]), -1e30)
        probs = jnp.exp(logits - jnp.max(logits, axis=-1, keepdims=True))
        probs = probs / jnp.sum(probs, axis=-1, keepdims=True)
        mine = (lane == me).astype(f32)
        gate = jnp.sum(probs * mine, axis=-1, keepdims=True)
        grad_out = (gate * dy).astype(bf)
        go[group, :] = grad_out

        def block(q, sums):
            out, grad_row = sums
            value, slope = gelu_parts(nn(x, first[q]) + bias_ref[q, 0:1])
            value = value.astype(bf)
            act[q, group, :] = value
            grad_pre = (nt(grad_out, second[q]) * slope).astype(bf)
            gp[q, group, :] = grad_pre
            return out + nn(value, second[q]), grad_row + nt(grad_pre, first[q])

        zero = jnp.zeros((pair, x.shape[1]), f32)
        out, grad_row = lax.fori_loop(0, blocks, block, (zero, zero), unroll=True)
        made = (out + second_bias).astype(bf).astype(f32)
        grad_gate = jnp.sum(dy * made, axis=-1, keepdims=True)
        grad_logits = (grad_gate * gate * (mine - probs)).astype(bf)
        logit_grad[group, :] = grad_logits
        grad_row = (grad_row + nt(grad_logits, router_ref[...])).astype(bf)
        outs_ref[group, :] = (gate * made).astype(bf)
        back_sent[group, :] = grad_row

        @pl.when(plane > 0)
        def _():
            dispatch(2 * plane, back_sent, back, back_sems).start()

        dispatch(2 * plane + 1, back_sent, back, back_sems).start()

    back[at(me), :] = back_sent[at(me), :]
    _, _, x_at, c_at = split_axes()
    core_peer, x_peer = (me, x_at * 2 + 1 - c_at), (me, (1 - x_at) * 2 + c_at)
    far, near = (1 - x_at) * 2 + c_at, seq

    def to_core(k):
        side = lax.rem(x_at + 1 + k, 2)
        return remote(
            second.at[side * 2 + 1 - c_at], recv_e.at[k], es_sem.at[k], er_sem.at[k], core_peer
        )

    to_x = remote(second.at[far], recv_x, es_sem.at[2], er_sem.at[2], x_peer)

    @pl.loop(0, blocks)
    def _(k):
        q = lax.rem(x_at + 1 + k // 2, 2) * 2 + lax.rem(c_at + 1 + k, 2)
        second[q] = tn(act[q], go[...]).astype(bf)

        @pl.when(lax.rem(k, 2) == 0)
        def _():
            to_core(k // 2).start()

    to_core(0).wait_recv()
    second[far] = (second[far].astype(f32) + recv_e[0].astype(f32)).astype(bf)
    to_x.start()
    ones = jnp.ones((8, rows.shape[0]), bf)

    @pl.loop(0, blocks)
    def _(q):
        first[q] = tn(rows[...], gp[q]).astype(bf)
        pltpu.make_async_copy(first.at[q], first_grad_any.at[q], grad_sem.at[q]).start()
        bias_grad_ref[q, :8] = nn(ones, gp[q])
        bias_grad_ref[q, 8:] = nn(ones, go[...])

    router_grad_ref[...] = tn(logit_grad[...], rows[...])[: router_grad_ref.shape[0]]

    @pl.loop(1, n)
    def _(step):
        dispatch(step, back_sent, back, back_sems).wait()
        dispatch(step, sent, rows, out_sems).wait_send()

    grad_ref[...] = nn(from_ref[...], back[...]).astype(bf)
    for copy in swaps + own_swaps:
        copy.wait()

    @pl.loop(0, blocks)
    def _(q):
        pltpu.make_async_copy(first.at[q], first_grad_any.at[q], grad_sem.at[q]).wait()

    to_core(1).wait_recv()
    to_x.wait_recv()

    @pl.loop(0, 6)
    def _(k):
        at = rows_of(k, recv_x.shape[0] // 6)
        second_grad_ref[at, :] = (
            second[near, at, :].astype(f32) + recv_e[1, at, :].astype(f32) + recv_x[at, :].astype(f32)
        )

    to_core(0).wait_send()
    to_core(1).wait_send()
    to_x.wait_send()


def moe(h_block, into, outof, dy_slots, first, second, bias, router, dy, branch, experts):
    bf, f32 = jnp.bfloat16, jnp.float32
    tok, width = h_block.shape
    slots = into.shape[0]
    blocks, hidden = first.shape[0], first.shape[2]
    sds = jax.ShapeDtypeStruct
    dma = pltpu.SemaphoreType.DMA
    big = (slots, width)
    return pl.pallas_call(
        functools.partial(moe_kernel, experts),
        out_shape=(
            sds((tok, width), bf),
            sds(big, bf),
            sds(first.shape, bf),
            sds(second.shape[1:], f32),
            sds((8, width), f32),
            sds((blocks, 16, hidden), f32),
            sds((tok, width), bf),
            sds((tok, width), bf),
        ),
        in_specs=[VMEM] * 4 + [ANY] * 2 + [VMEM] * 2 + [ANY] * 2,
        out_specs=(VMEM,) * 2 + (ANY,) + (VMEM,) * 3 + (ANY,) * 2,
        scratch_shapes=[
            pltpu.VMEM(big, bf),
            pltpu.VMEM(big, bf),
            pltpu.VMEM(big, bf),
            pltpu.VMEM((blocks, slots, hidden), bf),
            pltpu.VMEM((blocks, slots, hidden), bf),
            pltpu.VMEM(big, bf),
            pltpu.VMEM(big, bf),
            pltpu.VMEM((slots, 128), bf),
            pltpu.VMEM(first.shape, bf),
            pltpu.VMEM(second.shape, bf),
            dma((2,)),
            dma((experts,)),
            dma((experts,)),
            dma((experts,)),
            dma((experts,)),
            dma((2, blocks)),
            dma((2, blocks)),
            dma((2,)),
            dma((blocks,)),
            pltpu.VMEM((2,) + second.shape[1:], bf),
            pltpu.VMEM(second.shape[1:], bf),
            dma((3,)),
            dma((3,)),
        ],
        compiler_params=pltpu.CompilerParams(
            collective_id=1, has_side_effects=True, vmem_limit_bytes=61 * 2**20
        ),
        cost_estimate=pl.CostEstimate(
            flops=12 * slots * width * hidden * blocks, bytes_accessed=4 * 10**7, transcendentals=slots * hidden * blocks
        ),
        name="moe",
    )(h_block, into, outof, dy_slots, first, second, bias, router, dy, branch)


def norm_stats(values):
    average = jnp.mean(values, axis=-1, keepdims=True)
    centred = values - average
    inv = lax.rsqrt(jnp.mean(centred * centred, axis=-1, keepdims=True) + norm_eps)
    return centred * inv, inv


def norm_grad(grad_output, normed, inv, gain):
    scaled = grad_output * gain
    return inv * (
        scaled
        - jnp.mean(scaled, axis=-1, keepdims=True)
        - normed * jnp.mean(scaled * normed, axis=-1, keepdims=True)
    )


def rows_of(i, size):
    return pl.ds(pl.multiple_of(i * size, size), size)


def split_axes():
    dp, seq = lax.axis_index("dp"), lax.axis_index("seq")
    return dp // 2, lax.rem(dp, 2), seq // 2, lax.rem(seq, 2)


def greet(n_dp, n_seq):
    dp, seq = lax.axis_index("dp"), lax.axis_index("seq")
    barrier = pltpu.get_barrier_semaphore()
    for step in range(1, n_dp):
        pl.semaphore_signal(
            barrier, inc=1, device_id=(other(dp, step), seq), device_id_type=MESH
        )
    for step in range(1, n_seq):
        pl.semaphore_signal(
            barrier, inc=1, device_id=(dp, lax.rem(seq + step, n_seq)), device_id_type=MESH
        )
    pl.semaphore_wait(barrier, n_dp - 1 + n_seq - 1)


def remote(source, target, send, recv, device):
    return pltpu.make_async_remote_copy(
        source, target, send, recv, device_id=device, device_id_type=MESH
    )


def back_kernel(
    n_dp,
    n_seq,
    grad_any,
    resid_any,
    x_any,
    dy_any,
    att_any,
    qkv_any,
    probs_any,
    packed_any,
    vectors_ref,
    outs_any,
    outof_any,
    tokens_any,
    branch_any,
    first_any,
    bias_ref,
    router_grad_ref,
    block_out_ref,
    tokens_grad_ref,
    qkv_grad_ref,
    out_grad_ref,
    small_ref,
    first_out_ref,
    bias_out_ref,
    grad_rows,
    resid,
    x_row,
    dy_row,
    att,
    qkv,
    probs,
    w_qkv,
    w_out,
    outs,
    outof,
    tokens,
    branch,
    own_e,
    recv_e,
    recv_x,
    recv_b,
    grad_resid,
    grad_att,
    grad_qkv,
    h_one,
    grad_x,
    part,
    recv_c,
    recv_1,
    recv_2,
    recv_3,
    sums,
    recv_s,
    load_sem,
    probs_sem,
    own_sem,
    gs_sem,
    gr_sem,
    os_sem,
    or_sem,
    es_sem,
    er_sem,
    xs_sem,
    xr_sem,
    bs_sem,
    br_sem,
    ps_sem,
    pr_sem,
    ss_sem,
    sr_sem,
    ts_sem,
    tr_sem,
):
    bf, f32 = jnp.bfloat16, jnp.float32
    dp, seq = lax.axis_index("dp"), lax.axis_index("seq")
    z, y, x, c = split_axes()
    pos = grad_rows.shape[0] // n_seq
    cap = outs.shape[0] // n_dp
    core_peer, x_peer = (dp, x * 2 + 1 - c), (dp, (1 - x) * 2 + c)
    y_peer = (z * 2 + 1 - y, seq)
    z_peer = lambda step: (lax.rem(z + step, 4) * 2 + y, seq)
    loads = [
        pltpu.make_async_copy(a, b, load_sem.at[i])
        for i, (a, b) in enumerate(
            (
                (resid_any, resid),
                (dy_any, dy_row),
                (att_any, att),
                (packed_any.at[:, 3 * D : 4 * D], w_out),
                (qkv_any, qkv),
                (x_any, x_row),
                (packed_any.at[:, : 3 * D], w_qkv),
                (outof_any, outof),
                (tokens_any, tokens),
                (branch_any, branch),
            )
        )
    ]
    fetch = lambda head: pltpu.make_async_copy(
        probs_any.at[head], probs.at[head % 2], probs_sem.at[head % 2]
    )
    for load in loads[:4]:
        load.start()
    greet(n_dp, n_seq)
    to_rows = []
    for step in range(1, n_seq):
        to = lax.rem(seq + step, n_seq)
        to_rows.append(
            remote(
                grad_any.at[rows_of(to, pos)],
                grad_rows.at[rows_of(seq, pos)],
                gs_sem.at[step],
                gr_sem.at[step],
                (dp, to),
            )
        )
    for copy in to_rows:
        copy.start()
    own_rows = pltpu.make_async_copy(
        grad_any.at[rows_of(seq, pos)], grad_rows.at[rows_of(seq, pos)], own_sem.at[0]
    )
    own_rows.start()
    experts_c, experts_own = [], []
    for k, side in enumerate((1 - x, x)):
        experts_c.append(
            remote(
                first_any.at[side * 2 + 1 - c], recv_e.at[k], es_sem.at[k], er_sem.at[k], core_peer
            )
        )
        experts_own.append(
            pltpu.make_async_copy(first_any.at[side * 2 + c], own_e.at[k], own_sem.at[1 + k])
        )
    for copy in experts_c + experts_own:
        copy.start()
    returns = []
    for step in range(n_dp - 1, 0, -1):
        to = other(dp, step)
        returns.append(
            remote(
                outs_any.at[rows_of(to, cap)],
                outs.at[rows_of(dp, cap)],
                os_sem.at[step],
                or_sem.at[step],
                (to, seq),
            )
        )
    for copy in returns:
        copy.start()
    own_outs = pltpu.make_async_copy(
        outs_any.at[rows_of(dp, cap)], outs.at[rows_of(dp, cap)], own_sem.at[3]
    )
    own_outs.start()
    biases = []
    for step in range(1, n_seq):
        to = lax.rem(seq + step, n_seq)
        biases.append(
            remote(bias_ref.at[to], recv_b.at[step], bs_sem.at[step], br_sem.at[step], (dp, to))
        )
    for copy in biases:
        copy.start()
    for load in loads[4:]:
        load.start()
    fetch(0).start()
    fetch(1).start()
    vec = lambda i: vectors_ref[i : i + 1, :]
    row_sum = lambda v: jnp.sum(v, axis=0, keepdims=True)

    def norm_back(grad_output, values, gain):
        normed, inv = norm_stats(values)
        sums_of = (row_sum(grad_output * normed), row_sum(grad_output))
        return norm_grad(grad_output, normed, inv, gain), *sums_of

    def piece_fill(i, value):
        half = value.shape[1] // 2
        for owner in range(n_dp * n_seq):
            oz, oy, ox, oc = owner // 8, owner // 4 % 2, owner // 2 % 2, owner % 2
            block = value[24 * owner : 24 * owner + 24].astype(bf)
            part[i, oc, 0, ox, oy, oz] = block[:, :half]
            part[i, oc, 1, oy, ox, oz] = block[:, half:]

    first_axis = ((x, x_peer), (y, y_peer))

    def piece_copies(i, stage):
        sems = lambda k: (ps_sem.at[i, k], pr_sem.at[i, k])
        if stage == 0:
            return [remote(part.at[i, 1 - c], recv_c.at[i], *sems(0), core_peer)]
        made = []
        for h in range(2):
            (f, f_peer), (g, g_peer) = first_axis[h], first_axis[1 - h]
            if stage == 1:
                made.append(
                    remote(part.at[i, c, h, 1 - f], recv_1.at[i, h], *sems(1 + h), f_peer)
                )
            elif stage == 2:
                made.append(
                    remote(part.at[i, c, h, f, 1 - g], recv_2.at[i, h], *sems(3 + h), g_peer)
                )
            else:
                for step in range(1, 4):
                    made.append(
                        remote(
                            part.at[i, c, h, f, g, lax.rem(z + step, 4)],
                            recv_3.at[i, h, step],
                            *sems(4 + h * 3 + step),
                            z_peer(step),
                        )
                    )
        return made

    def add(a, b):
        return (a.astype(f32) + b.astype(f32)).astype(bf)

    def piece_advance(i, stage):
        for copy in piece_copies(i, stage - 1):
            copy.wait_recv()
        if stage == 1:
            part[i, c] = add(part[i, c], recv_c[i])
        for h in range(2):
            f, g = first_axis[h][0], first_axis[1 - h][0]
            if stage == 2:
                part[i, c, h, f] = add(part[i, c, h, f], recv_1[i, h])
            elif stage == 3:
                part[i, c, h, f, g] = add(part[i, c, h, f, g], recv_2[i, h])
            elif stage == 4:
                total = part[i, c, h, f, g, z].astype(f32)
                for step in range(1, 4):
                    total = total + recv_3[i, h, step].astype(f32)
                half = total.shape[1]
                for k in range(3):
                    at = h * half + k * 128
                    lanes = total[:, k * 128 : k * 128 + 128]
                    if i == 0:
                        out_grad_ref[:, at : at + 128] = lanes
                    else:
                        to = D * (at // 256) + 256 * (i - 1) + at % 256
                        qkv_grad_ref[:, to : to + 128] = lanes
        if stage < 4:
            for copy in piece_copies(i, stage):
                copy.start()

    def small_copies(stage):
        peers = ([core_peer], [x_peer], [y_peer], [z_peer(1), z_peer(2), z_peer(3)])[stage]
        return [
            remote(
                sums.at[stage],
                recv_s.at[stage + k],
                ss_sem.at[stage + k],
                sr_sem.at[stage + k],
                peer,
            )
            for k, peer in enumerate(peers)
        ]

    def small_advance(stage):
        for copy in small_copies(stage - 1):
            copy.wait_recv()
        if stage < 4:
            sums[stage] = sums[stage - 1] + recv_s[stage - 1]
            for copy in small_copies(stage):
                copy.start()
        else:
            small_ref[...] = sums[3] + recv_s[3] + recv_s[4] + recv_s[5]

    experts_x = remote(own_e.at[0], recv_x, xs_sem, xr_sem, x_peer)

    def experts_send_x():
        experts_c[0].wait_recv()
        experts_own[0].wait()
        own_e[0] = add(own_e[0], recv_e[0])
        experts_x.start()

    def experts_end():
        experts_c[1].wait_recv()
        experts_own[1].wait()
        experts_x.wait_recv()

        @pl.loop(0, 6)
        def _(k):
            at = rows_of(k, recv_x.shape[0] // 6)
            first_out_ref[at, :] = (
                own_e[1, at, :].astype(f32)
                + recv_e[1, at, :].astype(f32)
                + recv_x[at, :].astype(f32)
            )

        bias = bias_ref[seq]
        for step in range(1, n_seq):
            biases[step - 1].wait_recv()
            bias = bias + recv_b[step]
        bias_out_ref[...] = bias

    for load in loads[:3]:
        load.wait()
    own_rows.wait()
    for copy in to_rows:
        copy.wait_recv()
    experts_send_x()
    grad_in, gain_two, shift_two = norm_back(grad_rows[...].astype(f32), resid[...], vec(3))
    grad_resid[...] = dy_row[...].astype(f32) + grad_in
    grad_branch = grad_resid[...].astype(bf)
    out_shift = row_sum(grad_branch.astype(f32))
    loads[3].wait()
    grad_att[...] = nt(grad_branch, w_out[...]).astype(bf)
    piece_fill(0, tn(att[...], grad_branch))
    for copy in piece_copies(0, 0):
        copy.start()
    loads[4].wait()
    loads[5].wait()
    x_normed, _ = norm_stats(x_row[...].astype(f32))
    h_one[...] = (x_normed * vec(0) + vec(1)).astype(bf)
    ahead = (((0, 1),), (), ((1, 1),), ((0, 2),), ((2, 1),), ((0, 3), (1, 2)))
    lane = lax.broadcasted_iota(jnp.int32, (1, 128), 1) // HEAD
    scale = HEAD ** (-0.5)
    for pair in range(HEADS // 2):
        cols = slice(128 * pair, 128 * pair + 128)
        q, k, v = (qkv[:, D * i + 128 * pair : D * i + 128 * pair + 128] for i in range(3))
        go = grad_att[:, cols]
        both = go.astype(f32) * att[:, cols].astype(f32)
        grads = [jnp.zeros(q.shape, f32)] * 3
        for h in range(2):
            head = 2 * pair + h
            keep = (lane == h).astype(bf)
            fetch(head).wait()
            p = probs[head % 2]
            go_h = go * keep
            delta = jnp.sum(both * keep.astype(f32), axis=-1, keepdims=True)
            ds = (p.astype(f32) * (nt(go_h, v) - delta)).astype(bf)
            grads = [
                grads[0] + nn(ds, k * keep),
                grads[1] + tn(ds, q * keep),
                grads[2] + tn(p, go_h),
            ]
            if head + 2 < HEADS:
                fetch(head + 2).start()
        for i, factor in enumerate((scale, scale, 1.0)):
            at = (2 * 128) * (3 * (pair // 2) + i) + 128 * (pair % 2)
            grad_qkv[:, at : at + 128] = (grads[i] * factor).astype(bf)
        for i, stage in ahead[pair]:
            piece_advance(i, stage)
        if pair % 2 == 1:
            i = pair // 2 + 1
            piece_fill(i, tn(h_one[...], grad_qkv[:, D * (i - 1) : D * i]))
            for copy in piece_copies(i, 0):
                copy.start()
    loads[6].wait()
    grad_h1 = jnp.zeros(resid.shape, f32)
    for i in range(9):
        at = 256 * i
        col = D * (i % 3) + 256 * (i // 3)
        grad_h1 = grad_h1 + nt(grad_qkv[:, at : at + 256], w_qkv[:, col : col + 256])
    piece_advance(3, 1)
    piece_advance(2, 2)
    piece_advance(1, 3)
    grad_in, gain_one, shift_one = norm_back(grad_h1, x_row[...].astype(f32), vec(0))
    sums[0] = jnp.concatenate(
        [gain_one, shift_one, out_shift, gain_two, shift_two, jnp.zeros((3, D), f32), router_grad_ref[...]], axis=0
    )
    for copy in small_copies(0):
        copy.start()
    grad_x[...] = (grad_resid[...] + grad_in).astype(bf)
    to_blocks = []
    for step in range(1, n_seq):
        to = lax.rem(seq + step, n_seq)
        to_blocks.append(
            remote(
                grad_x.at[rows_of(to, pos)],
                tokens_grad_ref.at[rows_of(seq, pos)],
                ts_sem.at[step],
                tr_sem.at[step],
                (dp, to),
            )
        )
    piece_advance(3, 2)
    for copy in to_blocks:
        copy.start()
    tokens_grad_ref[rows_of(seq, pos), :] = grad_x[rows_of(seq, pos), :]
    small_advance(1)
    own_outs.wait()
    for copy in returns:
        copy.wait_recv()
    for load in loads[7:]:
        load.wait()
    block_out_ref[...] = (
        tokens[...].astype(f32) + branch[...].astype(f32) + nn(outof[...], outs[...])
    ).astype(bf)
    piece_advance(3, 3)
    piece_advance(0, 4)
    piece_advance(2, 3)
    small_advance(2)
    piece_advance(1, 4)
    experts_end()
    small_advance(3)
    piece_advance(2, 4)
    piece_advance(3, 4)
    small_advance(4)
    for copy in to_blocks:
        copy.wait_recv()
    for copy in to_rows + experts_c + returns + biases + [experts_x] + to_blocks:
        copy.wait_send()
    for stage in range(4):
        for i in range(4):
            for copy in piece_copies(i, stage):
                copy.wait_send()
        for copy in small_copies(stage):
            copy.wait_send()


def back(
    n_dp,
    n_seq,
    grad_h2,
    resid,
    x_row,
    dy_row,
    att,
    qkv,
    probs,
    packed,
    vectors,
    outs,
    outof,
    tokens,
    branch,
    first_grad,
    biases,
    router_grad,
):
    bf, f32 = jnp.bfloat16, jnp.float32
    sds, dma, vmem = jax.ShapeDtypeStruct, pltpu.SemaphoreType.DMA, pltpu.VMEM
    tok, slots = outof.shape
    pos = tok // n_seq
    half = D // 2
    return pl.pallas_call(
        functools.partial(back_kernel, n_dp, n_seq),
        out_shape=(
            sds((tok, D), bf),
            sds((tok, D), bf),
            sds((D // (n_dp * n_seq), 3 * D), f32),
            sds((D // (n_dp * n_seq), D), f32),
            sds((16, D), f32),
            sds(first_grad.shape[1:], f32),
            sds(biases.shape[1:], f32),
        ),
        in_specs=[ANY] * 8 + [VMEM] + [ANY] * 5 + [VMEM] * 2,
        out_specs=(VMEM,) * 7,
        scratch_shapes=[
            vmem((tok, D), bf),
            vmem((tok, D), f32),
            vmem((tok, D), bf),
            vmem((tok, D), bf),
            vmem((tok, D), bf),
            vmem((tok, 3 * D), bf),
            vmem((2,) + probs.shape[1:], bf),
            vmem((D, 3 * D), bf),
            vmem((D, D), bf),
            vmem((slots, D), bf),
            vmem((tok, slots), bf),
            vmem((tok, D), bf),
            vmem((tok, D), bf),
            vmem((2, D, D), bf),
            vmem((2, D, D), bf),
            vmem((D, D), bf),
            vmem((n_seq,) + biases.shape[1:], f32),
            vmem((tok, D), f32),
            vmem((tok, D), bf),
            vmem((tok, 3 * D), bf),
            vmem((tok, D), bf),
            vmem((tok, D), bf),
            vmem((4, 2, 2, 2, 2, 4, 24, half), bf),
            vmem((4, 2, 2, 2, 4, 24, half), bf),
            vmem((4, 2, 2, 4, 24, half), bf),
            vmem((4, 2, 4, 24, half), bf),
            vmem((4, 2, 4, 24, half), bf),
            vmem((4, 16, D), f32),
            vmem((6, 16, D), f32),
            dma((10,)),
            dma((2,)),
            dma((4,)),
            dma((n_seq,)),
            dma((n_seq,)),
            dma((n_dp,)),
            dma((n_dp,)),
            dma((2,)),
            dma((2,)),
            dma,
            dma,
            dma((n_seq,)),
            dma((n_seq,)),
            dma((4, 11)),
            dma((4, 11)),
            dma((6,)),
            dma((6,)),
            dma((n_seq,)),
            dma((n_seq,)),
        ],
        compiler_params=pltpu.CompilerParams(
            collective_id=2, has_side_effects=True, vmem_limit_bytes=61 * 2**20
        ),
        cost_estimate=pl.CostEstimate(
            flops=10**10, bytes_accessed=5 * 10**7, transcendentals=10**6
        ),
        name="back",
    )(
        grad_h2,
        resid,
        x_row,
        dy_row,
        att,
        qkv,
        probs,
        packed,
        vectors,
        outs,
        outof,
        tokens,
        branch,
        first_grad,
        biases,
        router_grad,
    )


def finish_kernel(count, *refs):
    sources, targets, held = refs[:count], refs[count : 2 * count], refs[2 * count : 3 * count]
    in_sem, out_sem = refs[3 * count :]
    reads = [
        pltpu.make_async_copy(a, b, in_sem.at[i]) for i, (a, b) in enumerate(zip(sources, held))
    ]
    writes = [
        pltpu.make_async_copy(a, b, out_sem.at[i]) for i, (a, b) in enumerate(zip(held, targets))
    ]
    for copy in reads:
        copy.start()
    for read, write in zip(reads, writes):
        read.wait()
        write.start()
    for copy in writes:
        copy.wait()


def finish(*arrays):
    count = len(arrays)
    return pl.pallas_call(
        functools.partial(finish_kernel, count),
        out_shape=tuple(jax.ShapeDtypeStruct(a.shape, a.dtype) for a in arrays),
        in_specs=[ANY] * count,
        out_specs=(ANY,) * count,
        scratch_shapes=[pltpu.VMEM(a.shape, a.dtype) for a in arrays]
        + [pltpu.SemaphoreType.DMA((count,))] * 2,
        compiler_params=pltpu.CompilerParams(vmem_limit_bytes=61 * 2**20),
        name="finish",
    )(*arrays)


def front_kernel(
    n_dp,
    n_seq,
    cap,
    tokens_any,
    dy_any,
    w_qkv_any,
    w_out_any,
    first_any,
    second_any,
    router_in_ref,
    vectors_in_ref,
    order_ref,
    picks_ref,
    open_ref,
    bias1_ref,
    bias2_ref,
    h_block_any,
    resid_any,
    x_any,
    att_any,
    qkv_any,
    probs_any,
    packed_any,
    vectors_ref,
    router_ref,
    branch_any,
    into_any,
    outof_any,
    dy_slots_any,
    first_all,
    second_all,
    bias_all,
    wide_q,
    wide_k,
    wide_v,
    wide_o,
    packed,
    x_row,
    dy,
    mask_out,
    mask_in,
    qkv,
    att,
    probs,
    resid,
    branch,
    h_two,
    into,
    outof,
    dy_sent,
    weights,
    bias_ref,
    load_sem,
    store_sem,
    probs_sem,
    own_sem,
    keep_sem,
    gs_sem,
    gr_sem,
    xs_sem,
    xr_sem,
    ms_sem,
    mr_sem,
    ds_sem,
    dr_sem,
    es_sem,
    er_sem,
    bs_sem,
    br_sem,
    hs_sem,
    hr_sem,
):
    bf, f32, i32 = jnp.bfloat16, jnp.float32, jnp.int32
    dp, seq = lax.axis_index("dp"), lax.axis_index("seq")
    z, y, x, c = split_axes()
    tok = x_row.shape[0]
    pos, held, slots = tok // n_seq, into.shape[0] // n_dp, into.shape[0]
    core_peer, x_peer = (dp, x * 2 + 1 - c), (dp, (1 - x) * 2 + c)
    y_peer = (z * 2 + 1 - y, seq)
    z_peer = lambda step: (lax.rem(z + step, 4) * 2 + y, seq)
    wide = (wide_q, wide_k, wide_v, wide_o)
    mine = [ref.at[c, y, x, z] for ref in wide]
    shard = [
        pltpu.make_async_copy(a, b, load_sem.at[i])
        for i, (a, b) in enumerate(
            (
                (w_qkv_any.at[:, :D], mine[0].at[:, 128:]),
                (w_qkv_any.at[:, D : 2 * D], mine[1]),
                (w_qkv_any.at[:, 2 * D :], mine[2]),
                (w_out_any, mine[3]),
                (dy_any, dy),
                (tokens_any.at[rows_of(seq, pos)], x_row.at[rows_of(seq, pos)]),
            )
        )
    ]
    own_w = [
        pltpu.make_async_copy(ref, weights.at[j, seq], own_sem.at[j])
        for j, ref in enumerate((first_any, second_any))
    ]
    for copy in shard + own_w:
        copy.start()
    unit = lambda rows, shift: (
        lax.broadcasted_iota(i32, (rows, 128), 0) + shift
        == lax.broadcasted_iota(i32, (rows, 128), 1)
    ).astype(f32).astype(bf)
    narrow = nn(router_in_ref[...], unit(n_dp, 0)) + tn(vectors_in_ref[...], unit(8, n_dp))
    wide_q[c, y, x, z, :, :128] = narrow.astype(bf)

    def column(block):
        turned = jnp.concatenate([block.astype(f32)] * 2, axis=0).T
        return jnp.concatenate([turned[:, r : r + 1] for r in range(n_seq)], axis=0)

    order, valid = column(order_ref[...]), column(open_ref[...])
    ids = [column(picks_ref[k]).astype(i32) for k in range(2)]
    mask_out[...] = jnp.broadcast_to(valid, mask_out.shape).astype(bf)
    spots = lax.broadcasted_iota(i32, (bias2_ref.shape[1], D), 1)
    here = lax.broadcasted_iota(i32, spots.shape, 0) + seq * bias2_ref.shape[1]
    placed = nn(bias2_ref[...], (spots == here).astype(f32).astype(bf))
    bias_ref[...] = jnp.concatenate(
        [bias1_ref[...].astype(f32), placed, jnp.zeros((14, D), f32)], axis=0
    )
    for copy in shard[:4]:
        copy.wait()
    greet(n_dp, n_seq)
    seq_peers = [(step, lax.rem(seq + step, n_seq)) for step in range(1, n_seq)]

    def over(k, stage):
        sems = lambda i: (gs_sem.at[k, i], gr_sem.at[k, i])
        same = lambda ref, i, peer: remote(ref, ref, *sems(i), peer)
        if stage == 0:
            return [same(mine[k], step, z_peer(step)) for step in range(1, 4)]
        if stage == 1:
            return [same(wide[k].at[c, y, x], 0, x_peer)]
        if stage == 2:
            return [same(wide[k].at[c, y], 4, y_peer)]
        return [same(wide[k].at[c, (y, 1 - y)[stage - 3]], 2 + stage, core_peer)]

    def begin(k, *stages):
        for stage in stages:
            for copy in over(k, stage):
                copy.start()

    def arrived(k, stage):
        for copy in over(k, stage):
            copy.wait_recv()

    begin(0, 0)
    begin(1, 0)
    exchange = []
    for step, to in seq_peers:
        for source, target, sems in (
            (tokens_any, x_row, (xs_sem, xr_sem)),
            (mask_out, mask_in, (ms_sem, mr_sem)),
        ):
            exchange.append(
                remote(
                    source.at[rows_of(to, pos)],
                    target.at[rows_of(seq, pos)],
                    sems[0].at[step],
                    sems[1].at[step],
                    (dp, to),
                )
            )
    for copy in exchange:
        copy.start()
    mask_in[rows_of(seq, pos), :] = mask_out[rows_of(seq, pos), :]
    biases = [
        remote(bias_ref, bias_all.at[seq], bs_sem.at[step], br_sem.at[step], (dp, to))
        for step, to in seq_peers
    ]
    for copy in biases:
        copy.start()
    bias_all[seq] = bias_ref[...]
    for k in range(2):
        arrived(k, 0)
        begin(k, 1)
        begin(k + 2, 0)
    down = lax.broadcasted_iota(i32, (tok, tok), 0)
    across = lax.broadcasted_iota(i32, (tok, tok), 1)
    order_row = jnp.broadcast_to(order, (tok, 128)).T[:1].astype(i32)
    hit = order.astype(i32) == across
    rank_row = jnp.sum(jnp.where(hit, down.astype(f32), 0.0), axis=0, keepdims=True)
    hit = order_row == down
    rank_col = jnp.sum(jnp.where(hit, across.astype(f32), 0.0), axis=1, keepdims=True)
    earlier = (rank_row < rank_col).astype(bf)
    lane = lax.broadcasted_iota(i32, (tok, 128), 1)
    chosen = (lane == ids[0], lane == ids[1] + n_dp)
    counted = jnp.where(chosen[0] | chosen[1], 1.0, 0.0) * valid
    before = nn(earlier, counted.astype(bf))
    firsts = jnp.sum(jnp.where(lane == ids[0] + n_dp, 1.0, 0.0) * valid, axis=0, keepdims=True)
    spot = lax.broadcasted_iota(i32, (tok, slots), 1).astype(f32)
    spot_down = lax.broadcasted_iota(i32, (slots, tok), 0).astype(f32)
    hits, hits_down = [], []
    for k in range(2):
        slot = jnp.sum(jnp.where(chosen[k], before + firsts * k, 0.0), axis=1, keepdims=True)
        place = ids[k].astype(f32) * held + slot
        place = jnp.where((slot < cap) & (valid > 0.0), place, 1.0 * slots)
        place_row = jnp.broadcast_to(place, (tok, 128)).T[:1]
        hits.append(place == spot)
        hits_down.append(place_row == spot_down)
    outof[...] = jnp.where(hits[0] | hits[1], 1.0, 0.0).astype(bf)
    into[...] = jnp.where(hits_down[0] | hits_down[1], 1.0, 0.0).astype(bf)
    stores = [
        pltpu.make_async_copy(a, b, store_sem.at[i])
        for i, (a, b) in enumerate(
            (
                (into, into_any),
                (outof, outof_any),
                (x_row, x_any),
                (packed, packed_any),
                (qkv, qkv_any),
                (att, att_any),
                (branch, branch_any),
                (resid, resid_any),
            )
        )
    ]
    stores[0].start()
    stores[1].start()
    arrived(2, 0)
    begin(2, 1)
    arrived(0, 1)
    begin(0, 2, 3)
    arrived(3, 0)
    begin(3, 1)
    shard[4].wait()
    dy_sent[...] = nn(into[...], dy[...]).astype(bf)
    dy_copies = []
    for step in range(n_dp - 1, 0, -1):
        to = other(dp, step)
        dy_copies.append(
            remote(
                dy_sent.at[rows_of(to, held)],
                dy_slots_any.at[rows_of(dp, held)],
                ds_sem.at[step],
                dr_sem.at[step],
                (to, seq),
            )
        )
    for copy in dy_copies:
        copy.start()
    own_dy = pltpu.make_async_copy(
        dy_sent.at[rows_of(dp, held)], dy_slots_any.at[rows_of(dp, held)], own_sem.at[2]
    )
    own_dy.start()
    arrived(1, 1)
    begin(1, 2, 3)
    experts_x, experts_c, experts_f, kept_w = [], [], [], []
    for j, target in enumerate((first_all, second_all)):
        far = (1 - x) * 2 + c
        held_w = weights.at[j]
        sems = lambda k: (es_sem.at[j, k], er_sem.at[j, k])
        own_w[j].wait()
        experts_x.append(remote(held_w.at[seq], held_w.at[seq], *sems(0), x_peer))
        experts_c.append(remote(held_w.at[seq], held_w.at[seq], *sems(1), core_peer))
        experts_f.append(remote(held_w.at[far], held_w.at[far], *sems(2), core_peer))
        kept_w.append([])
        for k, block in enumerate((seq, x * 2 + 1 - c, far, (1 - x) * 2 + 1 - c)):
            kept_w[j].append(
                pltpu.make_async_copy(held_w.at[block], target.at[block], keep_sem.at[j, k])
            )
        kept_w[j][0].start()
    for copy in experts_x:
        copy.start()
    shard[5].wait()
    for copy in exchange:
        copy.wait_recv()
    normed, _ = norm_stats(x_row[...].astype(f32))
    stores[2].start()
    arrived(2, 1)
    begin(2, 2, 3)
    arrived(0, 2)
    begin(0, 4)
    arrived(3, 1)
    begin(3, 2, 3)

    def assemble(k, lanes):
        arrived(k, 3)
        arrived(k, 4)
        return gathered(k, lanes)

    def gathered(k, lanes):
        blocks = []
        for at in range(n_dp * n_seq):
            oz, oy, ox, oc = at // 8, at // 4 % 2, at // 2 % 2, at % 2
            blocks.append(wide[k][oc, oy, ox, oz, :, lanes].astype(f32))
        return jnp.concatenate(blocks, axis=0)

    narrow = assemble(0, slice(0, 128))
    router_ref[...] = narrow.astype(bf)
    vectors = narrow.T[8:16]
    vectors_ref[...] = vectors
    vec = lambda i: vectors[i : i + 1]
    h_one = (normed * vec(0) + vec(1)).astype(bf)
    for k in range(3):
        here = slice(D * k, D * k + D)
        if k < 2:
            arrived(k + 1, 2)
            begin(k + 1, 4)
        block = gathered(0, slice(128, 128 + D)) if k == 0 else assemble(k, slice(0, D))
        packed[:, here] = block.astype(bf)
        qkv[:, here] = nn(h_one, packed[:, here]).astype(bf)
    stores[4].start()
    arrived(3, 2)
    begin(3, 4)
    for copy in experts_c:
        copy.start()
    lane = lax.broadcasted_iota(i32, (1, 128), 1)
    closed = jnp.where(mask_in[...].astype(f32) > 0.0, 0.0, -1e30).astype(bf)
    keep_out = lambda head: pltpu.make_async_copy(
        probs.at[head % 2], probs_any.at[head], probs_sem.at[head % 2]
    )
    for pair in range(HEADS // 2):
        q, k, v = (qkv[:, D * i + 128 * pair : D * i + 128 * pair + 128] for i in range(3))
        q = q * jnp.asarray(HEAD ** (-0.5), bf)
        out = jnp.zeros(q.shape, f32)
        for h in range(2):
            head = 2 * pair + h
            keep = (lane // HEAD == h).astype(bf)
            spare = (lane == HEAD * (1 - h)).astype(bf)
            scores = nt(q * keep + spare, k * keep + closed * spare)
            soft = jnp.exp(scores - jnp.max(scores, axis=-1, keepdims=True))
            soft = soft * (1.0 / jnp.sum(soft, axis=-1, keepdims=True))
            if head >= 2:
                keep_out(head - 2).wait()
            low = soft.astype(bf)
            probs[head % 2] = low
            keep_out(head).start()
            out = out + nn(low, v * keep)
        att[:, 128 * pair : 128 * pair + 128] = out.astype(bf)
        if pair > 3:
            j = pair - 4
            experts_x[j].wait_recv()
            experts_f[j].start()
            kept_w[j][2].start()
    stores[5].start()
    packed[:, 3 * D :] = assemble(3, slice(0, D)).astype(bf)
    stores[3].start()
    made = nn(att[...], packed[:, 3 * D :]) + vec(2)
    branch[...] = made.astype(bf)
    resid[...] = x_row[...].astype(f32) + made
    normed, _ = norm_stats(resid[...])
    h_two[...] = (normed * vec(3) + vec(4)).astype(bf)
    to_blocks = [
        remote(
            h_two.at[rows_of(to, pos)],
            h_block_any.at[rows_of(seq, pos)],
            hs_sem.at[step],
            hr_sem.at[step],
            (dp, to),
        )
        for step, to in seq_peers
    ]
    for copy in to_blocks:
        copy.start()
    own_h = pltpu.make_async_copy(
        h_two.at[rows_of(seq, pos)], h_block_any.at[rows_of(seq, pos)], own_sem.at[3]
    )
    own_h.start()
    stores[6].start()
    stores[7].start()
    for j in range(2):
        experts_c[j].wait_recv()
        kept_w[j][1].start()
    for j in range(2):
        experts_f[j].wait_recv()
        kept_w[j][3].start()
    for copy in to_blocks + dy_copies + biases:
        copy.wait_recv()
    keep_out(HEADS - 2).wait()
    keep_out(HEADS - 1).wait()
    for copy in stores + kept_w[0] + kept_w[1] + [own_dy, own_h]:
        copy.wait()
    for copy in exchange + to_blocks + dy_copies + biases + experts_x + experts_c + experts_f:
        copy.wait_send()
    for k in range(4):
        for stage in range(5):
            for copy in over(k, stage):
                copy.wait_send()


def front(
    n_dp,
    n_seq,
    cap,
    held,
    tokens,
    dy,
    w_qkv,
    w_out,
    first,
    second,
    w_router,
    vectors,
    order,
    picks,
    mask,
    bias1,
    bias2,
):
    bf, f32 = jnp.bfloat16, jnp.float32
    sds, dma, vmem = jax.ShapeDtypeStruct, pltpu.SemaphoreType.DMA, pltpu.VMEM
    tok = tokens.shape[0]
    slots = n_dp * held
    own = D // (n_dp * n_seq)
    block = (tok, D)
    return pl.pallas_call(
        functools.partial(front_kernel, n_dp, n_seq, cap),
        out_shape=(
            sds(block, bf),
            sds(block, f32),
            sds(block, bf),
            sds(block, bf),
            sds((tok, 3 * D), bf),
            sds((HEADS, tok, tok), bf),
            sds((D, 4 * D), bf),
            sds((8, D), f32),
            sds((D, 128), bf),
            sds(block, bf),
            sds((slots, tok), bf),
            sds((tok, slots), bf),
            sds((slots, D), bf),
            sds((n_seq,) + first.shape, bf),
            sds((n_seq,) + second.shape, bf),
            sds((n_seq, 16, D), f32),
        ),
        in_specs=[ANY] * 6 + [VMEM] * 7,
        out_specs=(ANY,) * 7 + (VMEM,) * 2 + (ANY,) * 6 + (VMEM,),
        scratch_shapes=[
            vmem((2, 2, 2, 4, own, 128 + D), bf),
            vmem((2, 2, 2, 4, own, D), bf),
            vmem((2, 2, 2, 4, own, D), bf),
            vmem((2, 2, 2, 4, own, D), bf),
            vmem((D, 4 * D), bf),
            vmem(block, bf),
            vmem(block, bf),
            vmem((tok, 128), bf),
            vmem((tok, 128), bf),
            vmem((tok, 3 * D), bf),
            vmem(block, bf),
            vmem((2, tok, tok), bf),
            vmem(block, f32),
            vmem(block, bf),
            vmem(block, bf),
            vmem((slots, tok), bf),
            vmem((tok, slots), bf),
            vmem((slots, D), bf),
            vmem((2, n_seq) + first.shape, bf),
            vmem((16, D), f32),
            dma((6,)),
            dma((8,)),
            dma((2,)),
            dma((4,)),
            dma((2, 4)),
            dma((4, 7)),
            dma((4, 7)),
            dma((n_seq,)),
            dma((n_seq,)),
            dma((n_seq,)),
            dma((n_seq,)),
            dma((n_dp,)),
            dma((n_dp,)),
            dma((2, 3)),
            dma((2, 3)),
            dma((n_seq,)),
            dma((n_seq,)),
            dma((n_seq,)),
            dma((n_seq,)),
        ],
        compiler_params=pltpu.CompilerParams(
            collective_id=3, has_side_effects=True, vmem_limit_bytes=61 * 2**20
        ),
        cost_estimate=pl.CostEstimate(
            flops=6 * 10**9, bytes_accessed=5 * 10**7, transcendentals=4 * 10**6
        ),
        name="front",
    )(
        tokens,
        dy,
        w_qkv,
        w_out,
        first,
        second,
        w_router,
        vectors,
        order,
        picks,
        mask,
        bias1,
        bias2,
    )


def shards_rows(
    tokens,
    cotangent,
    pad_mask,
    expert_ids,
    priority,
    ln1_gain,
    ln1_shift,
    w_qkv,
    w_out,
    out_bias,
    ln2_gain,
    ln2_shift,
    w_router,
    w_in,
    in_bias,
    w_exp_out,
    exp_out_bias,
):
    rows_dev, pos_dev = pad_mask.shape
    tok = rows_dev * pos_dev
    experts = w_router.shape[1]
    cap = (21 * tok + 10 * experts - 1) // (10 * experts)
    n_dp, n_seq = lax.axis_size("dp"), lax.axis_size("seq")
    seq, own = lax.axis_index("seq"), D // (n_dp * n_seq)
    bf, f32 = jnp.bfloat16, jnp.float32
    held = -(-cap // 16) * 16
    flat, dy_block = tokens.reshape(tok, D), cotangent.reshape(tok, D)
    (
        h_block,
        resid,
        x_row,
        attended,
        qkv,
        probs,
        packed,
        vectors,
        router,
        branch,
        into,
        outof,
        dy_slots,
        first,
        second,
        bias,
    ) = front(
        n_dp,
        n_seq,
        cap,
        held,
        flat,
        dy_block,
        w_qkv,
        w_out,
        w_in[0],
        w_exp_out[0],
        w_router,
        jnp.stack([ln1_gain, ln1_shift, out_bias, ln2_gain, ln2_shift] + [ln2_shift] * 3),
        priority,
        jnp.moveaxis(expert_ids, 2, 0),
        pad_mask,
        in_bias,
        exp_out_bias,
    )
    grad_h2, made, first_grad, second_grad, router_grad, bias_grad, dy_row, branch_block = moe(
        h_block, into, outof, dy_slots, first, second, bias, router, dy_block, branch, experts
    )
    out, tokens_grad, qkv_grad, out_grad, small, first_grad, bias_grad = back(
        n_dp,
        n_seq,
        grad_h2,
        resid,
        x_row,
        dy_row,
        attended,
        qkv,
        probs,
        packed,
        vectors,
        made,
        outof,
        flat,
        branch_block,
        first_grad,
        bias_grad,
        router_grad,
    )
    out, tokens_grad, qkv_grad, out_grad, first_grad, second_grad = finish(
        out, tokens_grad, qkv_grad, out_grad, first_grad, second_grad
    )
    small = lax.dynamic_slice_in_dim(
        small, (lax.axis_index("dp") * n_seq + seq) * own, own, 1
    )
    return (
        out.reshape(rows_dev, pos_dev, D),
        tokens_grad.reshape(rows_dev, pos_dev, D),
        small[0],
        small[1],
        qkv_grad,
        out_grad,
        small[2],
        small[3],
        small[4],
        small[8 : 8 + experts].T,
        first_grad[None],
        bias_grad[None, 0],
        second_grad[None],
        lax.dynamic_slice_in_dim(bias_grad[None, 8], seq * exp_out_bias.shape[1], exp_out_bias.shape[1], 1),
    )


def shards(*args):
    block_rows, local_experts, n_dp = args[2].shape[0], args[13].shape[0], lax.axis_size("dp")
    if block_rows == lax.axis_size("seq") and local_experts == 1 and n_dp == 8:
        return shards_rows(*args)
    return shards_general(*args)


def solution(mesh):
    return jax.shard_map(
        shards,
        mesh=mesh,
        in_specs=(
            P("dp", "seq", None),
            P("dp", "seq", None),
            P("dp", "seq"),
            P("dp", "seq", None),
            P("dp", "seq"),
            P(("dp", "seq")),
            P(("dp", "seq")),
            P(("dp", "seq"), None),
            P(("dp", "seq"), None),
            P(("dp", "seq")),
            P(("dp", "seq")),
            P(("dp", "seq")),
            P(("dp", "seq"), None),
            P("dp", None, "seq"),
            P("dp", "seq"),
            P("dp", "seq", None),
            P("dp", "seq"),
        ),
        out_specs=(
            P("dp", "seq", None),
            P("dp", "seq", None),
            P(("dp", "seq")),
            P(("dp", "seq")),
            P(("dp", "seq"), None),
            P(("dp", "seq"), None),
            P(("dp", "seq")),
            P(("dp", "seq")),
            P(("dp", "seq")),
            P(("dp", "seq"), None),
            P("dp", None, "seq"),
            P("dp", "seq"),
            P("dp", "seq", None),
            P("dp", "seq"),
        ),
        check_vma=False,
    )
```
